128 devices in a mesh: dp: 4 (over x), expert: 32 (over z, y, core).
Axes of the slice: x: 4, y: 4, z: 4, core: 2. Of those that a mesh axis runs over, the one named last changes fastest.
Arguments:
- tokens: bfloat16 [32768, 1536], P(('dp', 'expert')), may hold values from -6 to 6
- routes: int32 [32768, 4], P(('dp', 'expert')), may hold values from 0 to 31, all different within a row; in each aligned block of 256 rows (0 to 255, 256 to 511, ...) at most 40 rows name the same one
- w_query: bfloat16 [1536, 1536], P('dp'), may hold values from -0.15625 to 0.15625
- key_matrix: bfloat16 [1536, 256], P('dp'), may hold values from -0.15625 to 0.15625
- value_matrix: bfloat16 [1536, 256], P('dp'), may hold values from -0.15625 to 0.15625
- w_output: bfloat16 [1536, 1536], P('dp'), may hold values from -0.625 to 0.625
- norm_one: bfloat16 [1536], P('dp'), may hold values from 0.5 to 1.5
- norm_two: bfloat16 [1536], P('dp'), may hold values from 0.5 to 1.5
- w_router: bfloat16 [1536, 32], P('dp'), may hold values from -0.078125 to 0.078125
- w_gate: bfloat16 [32, 1536, 768], P('expert', 'dp'), may hold values from -0.15625 to 0.15625
- w_up: bfloat16 [32, 1536, 768], P('expert', 'dp'), may hold values from -0.15625 to 0.15625
- w_down: bfloat16 [32, 1536, 768], P('expert', 'dp'), may hold values from -0.4375 to 0.4375
- cotangent: bfloat16 [32768, 1536], P(('dp', 'expert')), may hold values from -6 to 6
Outputs:
- mixed: bfloat16 [32768, 1536], P(('dp', 'expert'))
- grad_tokens: float32 [32768, 1536], P(('dp', 'expert'))
- grad_query: float32 [1536, 1536], P('dp')
- grad_key: float32 [1536, 256], P('dp')
- grad_value: float32 [1536, 256], P('dp')
- grad_output: float32 [1536, 1536], P('dp')
- grad_norm_one: float32 [1536], P('dp')
- grad_norm_two: float32 [1536], P('dp')
- grad_router: float32 [1536, 32], P('dp')
- grad_gate: float32 [32, 1536, 768], P('expert', 'dp')
- grad_up: float32 [32, 1536, 768], P('expert', 'dp')
- grad_down: float32 [32, 1536, 768], P('expert', 'dp')
The draws below stay inside these ranges and needn't reach their ends.
Inputs may be any that keep to these rules, and one draw needn't show every extreme that they name: `routes`: each row names 4 different experts. In each aligned block of 256 rows (one sequence) no expert is named by more than 40 rows, and in every draw some block names some expert exactly 40 times.
All inputs are finite; a program needn't handle non-finite values.
Results may differ from the reference program's by a relative error of at most 0.025.
Values may be sent and summed in bfloat16 or wider, within the bound.
A program may use at most 192 MiB of HBM per device.

```python
import math
import jax
import jax.numpy as jnp
import numpy as np
from jax import lax

MODEL_WIDTH = 1536
QUERY_HEADS = 12
KEY_VALUE_HEADS = 2
HEAD_SIZE = 128
FF = 768
TOPK = 4
TOK_DEV = 256
EXPERTS = 32
TOKENS = 32768
CAP = 40


def block_scale(own_key, shape, pieces, smallest, high):
    def one(dim, blocks):
        heights = jax.random.uniform(jax.random.fold_in(jax.random.fold_in(own_key, 6), dim), (blocks,), jnp.float32, smallest / len(pieces), high / len(pieces))
        return jnp.repeat(jnp.exp(heights), shape[dim] // blocks).reshape((-1,) + (1,) * (len(shape) - dim - 1))

    level = one(*pieces[0])
    for cut in pieces[1:]:
        level = level * one(*cut)
    return level


def assign_block(own_key, own, number, rows, count, top, limit, lean):
    sequence = jax.random.permutation(own_key, count)
    packed, common = portions_of(count, rows * top, limit, lean, True), portions_of(count, rows * top, limit, lean, False)
    places = jnp.arange(count)

    def named(sizes, rotation):
        used = int((sizes > 0).sum())
        fixed = max(1, used // 4)
        moved = fixed + (places - fixed + rotation * (used - fixed)) % max(1, count - fixed)
        return jnp.zeros((count,), jnp.int32).at[sequence[jnp.where(places < fixed, places, moved)]].set(jnp.asarray(sizes, jnp.int32))

    sizes = jnp.where(number % 4 == 0, named(packed, number // 4), named(common, number - number // 4 - 1))
    mixed = jax.random.permutation(jax.random.fold_in(own, 3), count)
    donor, taker = mixed[0:count // 2 * 2:2], mixed[1:count // 2 * 2:2]
    margin = jnp.minimum(sizes[donor] - 1, limit - sizes[taker]) // 2
    margin = jnp.where((donor == sequence[0]) | (taker == sequence[0]) | (sizes[taker] == 0), 0, jnp.maximum(margin, 0))
    moved = jax.random.randint(jax.random.fold_in(own, 4), (count // 2,), 0, 1 << 20) % (margin + 1)
    sizes = sizes.at[donor].add(-moved).at[taker].add(moved)
    items = jnp.searchsorted(jnp.cumsum(sizes), jnp.arange(rows * top), side="right").astype(jnp.int32)
    grid = items.reshape(top, rows).T
    grid = grid[jax.random.permutation(jax.random.fold_in(own, 1), rows)]
    rotation = jax.random.randint(jax.random.fold_in(own, 2), (rows, 1), 0, top)
    return jnp.take_along_axis(grid, (jnp.arange(top)[None, :] + rotation) % top, axis=1)


def portions_of(amount, total, bound, lean, full):
    loads = [(1 << 20) // math.isqrt(grade ** lean) + 1 for grade in range(1, amount + 1)]
    largest = bound if full else min(bound, max(-(-total // amount), total * loads[0] // sum(loads)))
    least = 1 if total - largest >= amount - 1 else 0
    given, spare = [largest] + [least] * (amount - 1), total - largest - least * (amount - 1)
    while spare > 0:
        candidates = [i for i in range(1, amount) if given[i] < largest] or [i for i in range(1, amount) if given[i] < bound]
        whole, left = sum([loads[i] for i in candidates]), spare
        for i in candidates:
            addition = min(bound - given[i], max(1, left * loads[i] // whole), spare)
            given[i] = given[i] + addition
            spare = spare - addition
    return np.array(given)


def gaussian(key, shape, width, reach, split=(), held_as=jnp.bfloat16):
    loudness = block_scale(key, shape, split, -0.22, 0.18) if split else 1.0
    result = jax.random.normal(key, shape, jnp.float32) * width * loudness
    return jnp.minimum(jnp.maximum(result, -reach), reach).astype(held_as)


def setup_inputs(seed: int = 0) -> dict:
    arg_keys = jax.random.split(jax.random.key(seed), 14)
    tokens = gaussian(arg_keys[0], (TOKENS, MODEL_WIDTH), 1.0, 6.0, ((0, 128),))
    routes_keys = jax.random.split(jax.random.fold_in(arg_keys[1], 1), TOKENS // TOK_DEV)
    routes_turns = jax.random.permutation(jax.random.fold_in(arg_keys[1], 3), TOKENS // TOK_DEV)
    routes = jax.vmap(lambda own, number: assign_block(jax.random.fold_in(arg_keys[1], 2), own, number, TOK_DEV, EXPERTS, TOPK, CAP, 2))(routes_keys, routes_turns).reshape((TOKENS, TOPK))
    w_query = gaussian(arg_keys[2], (MODEL_WIDTH, QUERY_HEADS * HEAD_SIZE), MODEL_WIDTH ** -0.5, 0.15625, ((0, 4),))
    key_matrix = gaussian(arg_keys[3], (MODEL_WIDTH, KEY_VALUE_HEADS * HEAD_SIZE), MODEL_WIDTH ** -0.5, 0.15625, ((0, 4),))
    value_matrix = gaussian(arg_keys[4], (MODEL_WIDTH, KEY_VALUE_HEADS * HEAD_SIZE), MODEL_WIDTH ** -0.5, 0.15625, ((0, 4),))
    w_output = gaussian(arg_keys[5], (QUERY_HEADS * HEAD_SIZE, MODEL_WIDTH), (QUERY_HEADS * HEAD_SIZE // 16) ** -0.5, 0.625, ((0, 4),))
    norm_one = jnp.clip(1.0 + 0.1 * jax.random.normal(arg_keys[6], (MODEL_WIDTH,), jnp.float32), 0.5, 1.5).astype(jnp.bfloat16)
    norm_two = jnp.clip(1.0 + 0.1 * jax.random.normal(arg_keys[7], (MODEL_WIDTH,), jnp.float32), 0.5, 1.5).astype(jnp.bfloat16)
    w_router = gaussian(arg_keys[8], (MODEL_WIDTH, EXPERTS), (4 * MODEL_WIDTH) ** -0.5, 0.078125, ((0, 4),))
    w_gate = gaussian(arg_keys[9], (EXPERTS, MODEL_WIDTH, FF), MODEL_WIDTH ** -0.5, 0.15625, ((0, 32), (1, 4)))
    w_up = gaussian(arg_keys[10], (EXPERTS, MODEL_WIDTH, FF), MODEL_WIDTH ** -0.5, 0.15625, ((0, 32), (1, 4)))
    w_down = gaussian(arg_keys[11], (EXPERTS, MODEL_WIDTH, FF), (FF // 4) ** -0.5, 0.4375, ((0, 32), (1, 4)))
    cotangent = gaussian(arg_keys[12], (TOKENS, MODEL_WIDTH), 1.0, 6.0, ((0, 128),))
    return dict(tokens=tokens, routes=routes, w_query=w_query, key_matrix=key_matrix, value_matrix=value_matrix, w_output=w_output, norm_one=norm_one, norm_two=norm_two, w_router=w_router, w_gate=w_gate, w_up=w_up, w_down=w_down, cotangent=cotangent)


EPSILON = 1e-06
ROPE_BASE = 10000.0

@jax.custom_vjp
def reduced_precision(v):
    return lax.optimization_barrier(v.astype(jnp.bfloat16)).astype(jnp.float32)

@jax.custom_vjp
def low_back(v):
    return v

def low_keep(v):
    return (reduced_precision(v), None)

def low_pass(kept, grad):
    return (grad,)

def back_keep(v):
    return (v, None)

def back_low(kept, grad):
    return (reduced_precision(grad),)
reduced_precision.defvjp(low_keep, low_pass)
low_back.defvjp(back_keep, back_low)

def matmul_high(left_side, right_side):
    return jnp.dot(left_side, right_side, precision=lax.Precision.HIGHEST, preferred_element_type=jnp.float32)

def scaled_norm(values, gain_vector):
    return values * lax.rsqrt(lax.optimization_barrier(jnp.mean(values * values, axis=-1, keepdims=True)) + EPSILON) * gain_vector

def apply_rotary(values, head_count):
    sequence_length = values.shape[0]
    shaped = values.reshape(sequence_length, head_count, HEAD_SIZE)
    half_dim = HEAD_SIZE // 2
    position = jnp.arange(sequence_length).astype(jnp.float32)
    frequency = ROPE_BASE ** (-jnp.arange(half_dim).astype(jnp.float32) * 2.0 / HEAD_SIZE)
    angles = position[:, None] * frequency[None, :]
    cosine = jnp.cos(angles)[:, None, :]
    sine_part = jnp.sin(angles)[:, None, :]
    first_half = shaped[..., :half_dim]
    second_half = shaped[..., half_dim:]
    turned = jnp.concatenate([first_half * cosine - second_half * sine_part, second_half * cosine + first_half * sine_part], axis=-1)
    return turned.reshape(sequence_length, head_count * HEAD_SIZE)

def gelu_tanh(values):
    return 0.5 * values * (1.0 + jnp.tanh(0.7978845608028654 * (values + 0.044715 * values * values * values)))

def slot_tables(route_rows, experts, capacity):
    assigned = route_rows.reshape(-1).astype(jnp.int32)
    onehot = (assigned[:, None] == jnp.arange(experts, dtype=jnp.int32)[None, :]).astype(jnp.int32)
    before = jnp.cumsum(onehot, axis=0) - onehot
    within = lax.optimization_barrier(jnp.sum(before * onehot, axis=1))
    target = (assigned * capacity + within).astype(jnp.int32)
    count_all = assigned.shape[0]
    owners = jnp.zeros((experts * capacity,), jnp.int32).at[target].set(jnp.arange(count_all, dtype=jnp.int32))
    filled = jnp.zeros((experts * capacity,), jnp.float32).at[target].set(1.0)
    return (target, owners, filled)

def layer_block(block_tokens, block_routes, weights):
    w_query, key_matrix, value_matrix, w_output, gain_one, gain_two, w_router, w_gate, w_up, w_down = weights
    sequence_length = block_tokens.shape[0]
    experts = w_router.shape[1]
    capacity = 5 * sequence_length * TOPK // (4 * experts)
    head_groups = QUERY_HEADS // KEY_VALUE_HEADS
    normed = reduced_precision(scaled_norm(block_tokens, gain_one))
    unrotated_query = low_back(matmul_high(normed, w_query))
    unrotated_key = low_back(matmul_high(normed, key_matrix))
    projected_value = low_back(matmul_high(normed, value_matrix))
    query_rows = reduced_precision(apply_rotary(unrotated_query, QUERY_HEADS)).reshape(sequence_length, KEY_VALUE_HEADS, head_groups, HEAD_SIZE)
    per_head_keys = reduced_precision(apply_rotary(unrotated_key, KEY_VALUE_HEADS)).reshape(sequence_length, KEY_VALUE_HEADS, HEAD_SIZE)
    per_head_values = reduced_precision(projected_value).reshape(sequence_length, KEY_VALUE_HEADS, HEAD_SIZE)
    scores = low_back(jnp.einsum('ihgd,jhd->hgij', query_rows, per_head_keys, precision=lax.Precision.HIGHEST) * HEAD_SIZE ** (-0.5))
    causal = jnp.arange(sequence_length)[:, None] >= jnp.arange(sequence_length)[None, :]
    scores = jnp.where(causal, scores, -jnp.inf)
    largest = lax.optimization_barrier(jnp.max(scores, axis=-1, keepdims=True))
    exponent = jnp.exp(scores - largest)
    softmax_weights = reduced_precision(exponent / lax.optimization_barrier(jnp.sum(exponent, axis=-1, keepdims=True)))
    mixed_heads = jnp.einsum('hgij,jhd->ihgd', softmax_weights, per_head_values, precision=lax.Precision.HIGHEST).reshape(sequence_length, QUERY_HEADS * HEAD_SIZE)
    mixed_heads = reduced_precision(low_back(mixed_heads))
    attended = low_back(matmul_high(mixed_heads, w_output))
    residual = block_tokens + attended
    second = reduced_precision(scaled_norm(residual, gain_two))
    logits = low_back(matmul_high(block_tokens, w_router))
    onehot = (block_routes[:, :, None] == jnp.arange(experts, dtype=jnp.int32)[None, None, :]).astype(jnp.float32)
    chosen = lax.optimization_barrier(jnp.sum(onehot * logits[:, None, :], axis=-1))
    chosen_top = lax.optimization_barrier(jnp.max(chosen, axis=-1, keepdims=True))
    chosen_exp = jnp.exp(chosen - chosen_top)
    gate_share = chosen_exp / lax.optimization_barrier(jnp.sum(chosen_exp, axis=-1, keepdims=True))
    target, owners, filled = slot_tables(block_routes, experts, capacity)
    slot_rows = low_back(second[owners // TOPK] * filled[:, None]).reshape(experts, capacity, MODEL_WIDTH)
    gate_pre = low_back(jnp.einsum('ecd,edf->ecf', slot_rows, w_gate, precision=lax.Precision.HIGHEST))
    up_pre = low_back(jnp.einsum('ecd,edf->ecf', slot_rows, w_up, precision=lax.Precision.HIGHEST))
    hidden = reduced_precision(gelu_tanh(gate_pre) * up_pre)
    expert_out = reduced_precision(low_back(jnp.einsum('ecf,edf->ecd', hidden, w_down, precision=lax.Precision.HIGHEST)))
    returned = expert_out.reshape(experts * capacity, MODEL_WIDTH)[target].reshape(sequence_length, TOPK, MODEL_WIDTH)
    combined = lax.optimization_barrier(jnp.sum(gate_share[:, :, None] * returned, axis=1))
    return residual + combined

def reference(tokens, routes, w_query, key_matrix, value_matrix, w_output, norm_one, norm_two, w_router, w_gate, w_up, w_down, cotangent):
    sequence_length = TOK_DEV
    blocks = tokens.shape[0] // sequence_length
    inputs = tokens.astype(jnp.float32)
    params = tuple((weight_item.astype(jnp.float32) for weight_item in (w_query, key_matrix, value_matrix, w_output, norm_one, norm_two, w_router, w_gate, w_up, w_down)))
    route_blocks = routes.reshape(blocks, sequence_length, TOPK)

    def forward(layer_input, weights):

        def one_block(block_pair):
            return layer_block(block_pair[0], block_pair[1], weights)
        outputs = lax.map(jax.checkpoint(one_block), (layer_input.reshape(blocks, sequence_length, MODEL_WIDTH), route_blocks))
        return outputs.reshape(blocks * sequence_length, MODEL_WIDTH)
    output, backward = jax.vjp(forward, inputs, params)
    grad_input, grad_weights = backward(cotangent.astype(jnp.float32))
    return (output.astype(jnp.bfloat16), grad_input, grad_weights[0], grad_weights[1], grad_weights[2], grad_weights[3], grad_weights[4], grad_weights[5], grad_weights[6], grad_weights[7], grad_weights[8], grad_weights[9])
```

```python
import functools
import itertools

import jax
import jax.numpy as jnp
import numpy as np
from jax import lax
from jax.experimental import pallas as pl
from jax.experimental.pallas import tpu as pltpu
from jax.sharding import PartitionSpec as P

MODEL_WIDTH = 1536
QUERY_HEADS = 12
KEY_VALUE_HEADS = 2
HEAD_SIZE = 128
TOPK = 4
SEQ = 256
EXPERTS = 32
CAP = 40
FF = 768
KV = KEY_VALUE_HEADS * HEAD_SIZE
SHARD = MODEL_WIDTH // 4
HALF = SHARD // 2
QUARTER = HALF // 2
EPSILON = 1e-06
ROPE_BASE = 10000.0
SCALE = HEAD_SIZE ** (-0.5)
MESH = pl.DeviceIdType.MESH
F32 = jnp.float32
BF16 = jnp.bfloat16
VMEM = pltpu.VMEM
ANY = pl.ANY
LIMIT = 60 * 1024 * 1024


def _offsets():
    def far(a):
        return min(a, 4 - a)

    every = [o for o in itertools.product(range(4), range(4), range(2)) if o != (0, 0, 0)]
    return sorted(every, key=lambda o: (far(o[0]) + far(o[1]), o))[::-1]


OFFSETS = _offsets()


def rope_tables():
    position = np.arange(SEQ, dtype=np.float32)
    frequency = (
        np.float32(ROPE_BASE) ** (-np.arange(64, dtype=np.float32) * np.float32(2.0 / HEAD_SIZE))
    ).astype(np.float32)
    angles = (position[:, None] * frequency[None, :]).astype(np.float32)
    cosine = np.cos(angles.astype(np.float64)).astype(np.float32)
    sine = np.sin(angles.astype(np.float64)).astype(np.float32)
    return (
        np.concatenate([cosine, cosine], axis=1),
        np.concatenate([-sine, sine], axis=1),
    )


def mm(left, right, left_dim=1, right_dim=0):
    return lax.dot_general(
        left, right, (((left_dim,), (right_dim,)), ((), ())), preferred_element_type=F32
    )


class Place:
    def __init__(self):
        self.x = lax.axis_index("dp")
        self.e = lax.axis_index("expert")
        self.core = lax.rem(self.e, 2)
        self.y = lax.rem(self.e // 2, 4)
        self.z = self.e // 8
        self.xl = lax.rem(self.x + 3, 4)
        self.xr = lax.rem(self.x + 1, 4)
        self.x2 = lax.rem(self.x + 2, 4)
        self.left = (self.xl, self.e)
        self.right = (self.xr, self.e)
        self.across = (self.x2, self.e)
        self.sibling = (self.x, self.e + 1 - 2 * self.core)

    def peer(self, offset):
        dz, dy, dc = offset
        return (
            lax.rem(self.z + dz, 4) * 8 + lax.rem(self.y + dy, 4) * 2 + lax.rem(self.core + dc, 2)
        )

    def peers(self):
        return [self.peer(o) for o in OFFSETS]


def greet(devices):
    barrier = pltpu.get_barrier_semaphore()
    for d in devices:
        pl.semaphore_signal(barrier, inc=1, device_id=d, device_id_type=MESH)
    return barrier


def remote(src, dst, send, recv, device):
    return pltpu.make_async_remote_copy(
        src_ref=src, dst_ref=dst, send_sem=send, recv_sem=recv, device_id=device, device_id_type=MESH
    )


def rows(start, count, align=16):
    return pl.ds(pl.multiple_of(start, align), count)


class Gather:
    def __init__(self, place, shard, full, send, recv):
        p = place
        half = p.core * HALF
        other = HALF - half

        def region(x, first, count):
            return full.at[rows(x * SHARD + first, count, 32)]

        def move(k, src, dst, device):
            return remote(src, dst, send.at[k], recv.at[k], device)

        mine = shard.at[rows(half, HALF, 32)]
        self.direct = [
            move(0, mine, region(p.x, half, HALF), p.right),
            move(1, mine, region(p.x, half, HALF), p.left),
        ]
        from_left = region(p.xl, half, QUARTER)
        from_right = region(p.xr, half + QUARTER, QUARTER)
        self.forward = [
            move(2, from_left, from_left, p.right),
            move(3, from_right, from_right, p.left),
        ]
        whole_left = region(p.xl, half, HALF)
        whole_right = region(p.xr, half, HALF)
        far_one = region(p.x2, half, QUARTER)
        far_two = region(p.x2, half + QUARTER, QUARTER)
        self.near = [
            move(4, whole_left, whole_left, p.sibling),
            move(5, whole_right, whole_right, p.sibling),
        ]
        self.far = [
            move(6, far_one, far_one, p.sibling),
            move(7, far_two, far_two, p.sibling),
        ]

    def start(self):
        for c in self.direct:
            c.start()

    def relay(self):
        for k in range(2):
            self.direct[k].wait_recv()
            self.forward[k].start()
            self.near[k].start()

    def relay_far(self):
        for k in range(2):
            self.forward[k].wait_recv()
            self.far[k].start()

    def arrived_near(self):
        for c in self.near:
            c.wait_recv()

    def arrived_far(self):
        for c in self.far:
            c.wait_recv()

    def finish(self):
        for c in self.direct + self.forward + self.near + self.far:
            c.wait_send()


def slot_rows(posm_ref, first, count):
    slot = lax.broadcasted_iota(jnp.int32, (CAP, SEQ), 0).astype(F32)
    return [
        jnp.where(posm_ref[pl.ds(first + j, 1), :] == slot, 1.0, 0.0) for j in range(count)
    ]


def turn(values, cosine, sine):
    return values * cosine + pltpu.roll(values, 64, 1) * sine


def turn_back(values, cosine, sine):
    return values * cosine - pltpu.roll(values, 64, 1) * sine


def softmax_parts(q_head, k_head, causal):
    scores = mm(q_head, k_head, 1, 1) * SCALE
    scores = jnp.where(causal, scores, -jnp.inf)
    largest = jnp.max(scores, axis=-1, keepdims=True)
    exponent = jnp.exp(scores - largest)
    return exponent / jnp.sum(exponent, axis=-1, keepdims=True)


def causal_mask():
    row = lax.broadcasted_iota(jnp.int32, (SEQ, SEQ), 0)
    column = lax.broadcasted_iota(jnp.int32, (SEQ, SEQ), 1)
    return column <= row


def front_kernel(
    tokens, cotangent, routes, small, wq, wkv, wo, cosine, sine,
    dy_in, wq_full, wkv_full, wo_full, small_all, posm, share, n1, q, kv, o, r, n2,
    dy_out, wqf, wkvf, wof, qacc, kvacc, racc,
    gs, gr, ss, sr, as_, ar, ls,
):
    p = Place()
    peers = p.peers()
    barrier = greet([p.left, p.right, p.across] + [(p.x, t) for t in peers])

    lane = lax.broadcasted_iota(jnp.int32, (EXPERTS, SEQ), 0)
    named = routes[0:1, :] == lane
    for j in range(1, TOPK):
        named = jnp.logical_or(named, routes[j : j + 1, :] == lane)
    earlier = (
        lax.broadcasted_iota(jnp.int32, (SEQ, SEQ), 0)
        < lax.broadcasted_iota(jnp.int32, (SEQ, SEQ), 1)
    ).astype(F32).astype(BF16)
    place_of = mm(named.astype(F32).astype(BF16), earlier)
    posm[...] = jnp.where(named, place_of, -1.0)

    small_all[p.x] = small[...]
    pl.semaphore_wait(barrier, len(peers) + 3)

    small_moves = [
        remote(small, small_all.at[p.x], ss.at[k], sr.at[k], d)
        for k, d in enumerate([p.right, p.left, p.across])
    ]
    for c in small_moves:
        c.start()
    gq = Gather(p, wq, wqf, gs.at[0], gr.at[0])
    gkv = Gather(p, wkv, wkvf, gs.at[1], gr.at[1])
    go = Gather(p, wo, wof, gs.at[2], gr.at[2])
    gq.start()
    gkv.start()

    mine = [
        pltpu.make_async_copy(w, f.at[rows(p.x * SHARD, SHARD, 128)], ls.at[k])
        for k, (w, f) in enumerate([(wq, wqf), (wkv, wkvf), (wo, wof)])
    ]
    for c in mine:
        c.start()

    x = tokens[...].astype(F32)
    unit = x * lax.rsqrt(jnp.mean(x * x, axis=-1, keepdims=True) + EPSILON)
    for c in small_moves:
        c.wait_recv()
    for s in range(4):
        cut = slice(s * SHARD, (s + 1) * SHARD)
        n1[:, cut] = (unit[:, cut] * small_all[s, 32:33, :].astype(F32)).astype(BF16)
    logits = mm(small_all[0, 0:32, :], tokens[:, 0:SHARD], 1, 1)
    for s in range(1, 4):
        logits += mm(small_all[s, 0:32, :], tokens[:, s * SHARD : (s + 1) * SHARD], 1, 1)
    top = jnp.max(jnp.where(named, logits, -jnp.inf), axis=0, keepdims=True)
    weight = jnp.where(named, jnp.exp(jnp.minimum(logits - top, 0.0)), 0.0)
    share[...] = weight / jnp.sum(weight, axis=0, keepdims=True)

    @pl.loop(0, EXPERTS // 4)
    def _(i):
        blocks = slot_rows(posm, i * 4, 4)
        gain = jnp.concatenate(
            [
                jnp.sum(b * share[pl.ds(i * 4 + j, 1), :], axis=-1, keepdims=True)
                for j, b in enumerate(blocks)
            ],
            axis=0,
        )
        picked = mm(jnp.concatenate(blocks, axis=0).astype(BF16), cotangent[...])
        dy_out[pl.ds(i * 4, 4)] = (picked * gain).reshape(4, CAP, MODEL_WIDTH).astype(BF16)

    sends = [
        remote(dy_out.at[t], dy_in.at[p.e], as_.at[k], ar.at[k], (p.x, t))
        for k, t in enumerate(peers)
    ]
    for c in sends:
        c.start()
    own_dy = pltpu.make_async_copy(dy_out.at[p.e], dy_in.at[p.e], ls.at[3])
    own_dy.start()

    def part(x_index):
        return n1[:, rows(x_index * SHARD, SHARD, 128)]

    def block(full, x_index):
        return full[rows(x_index * SHARD, SHARD, 128), :]

    own = part(p.x)
    qacc[...] = mm(own, wq[...])
    kvacc[...] = mm(own, wkv[...])
    gq.relay()
    gkv.relay()
    go.start()
    gq.arrived_near()
    gkv.arrived_near()
    for s in (p.xl, p.xr):
        qacc[...] += mm(part(s), block(wqf, s))
        kvacc[...] += mm(part(s), block(wkvf, s))
    gq.relay_far()
    gkv.relay_far()
    gq.arrived_far()
    gkv.arrived_far()
    qacc[...] += mm(part(p.x2), block(wqf, p.x2))
    kvacc[...] += mm(part(p.x2), block(wkvf, p.x2))
    for c in mine:
        c.wait()
    keep = [
        pltpu.make_async_copy(f, out, ls.at[4 + k])
        for k, (f, out) in enumerate([(wqf, wq_full), (wkvf, wkv_full), (wof, wo_full)])
    ]
    keep[0].start()
    keep[1].start()

    cos = cosine[...]
    sin = sine[...]
    for h in range(KEY_VALUE_HEADS):
        cut = slice(h * HEAD_SIZE, (h + 1) * HEAD_SIZE)
        kv[:, cut] = turn(kvacc[:, cut], cos, sin).astype(BF16)
        cut = slice(KV + h * HEAD_SIZE, KV + (h + 1) * HEAD_SIZE)
        kv[:, cut] = kvacc[:, cut].astype(BF16)
    causal = causal_mask()
    for h in range(QUERY_HEADS):
        cut = slice(h * HEAD_SIZE, (h + 1) * HEAD_SIZE)
        c = h // (QUERY_HEADS // KEY_VALUE_HEADS)
        q_head = turn(qacc[:, cut], cos, sin).astype(BF16)
        q[:, cut] = q_head
        weights = softmax_parts(q_head, kv[:, c * HEAD_SIZE : (c + 1) * HEAD_SIZE], causal)
        o[:, cut] = mm(
            weights.astype(BF16), kv[:, KV + c * HEAD_SIZE : KV + (c + 1) * HEAD_SIZE]
        ).astype(BF16)

    def opart(x_index):
        return o[:, rows(x_index * SHARD, SHARD, 128)]

    racc[...] = tokens[...].astype(F32) + mm(opart(p.x), wo[...])
    go.relay()
    go.arrived_near()
    for s in (p.xl, p.xr):
        racc[...] += mm(opart(s), block(wof, s))
    go.relay_far()
    go.arrived_far()
    keep[2].start()
    residual = racc[...] + mm(opart(p.x2), block(wof, p.x2))
    r[...] = residual
    unit = residual * lax.rsqrt(jnp.mean(residual * residual, axis=-1, keepdims=True) + EPSILON)
    for s in range(4):
        cut = slice(s * SHARD, (s + 1) * SHARD)
        n2[:, cut] = (unit[:, cut] * small_all[s, 33:34, :].astype(F32)).astype(BF16)

    for c in sends:
        c.wait()
    own_dy.wait()
    for c in small_moves:
        c.wait_send()
    for g in (gq, gkv, go):
        g.finish()
    for c in keep:
        c.wait()


def front(tokens, cotangent, routes, small, wq, wkv, wo):
    cosine, sine = rope_tables()
    D = MODEL_WIDTH

    def arr(shape, dtype=BF16):
        return jax.ShapeDtypeStruct(shape, dtype)

    outs = [
        arr((EXPERTS, CAP, D)), arr((D, D)), arr((D, 2 * KV)), arr((D, D)), arr((4, 48, SHARD)),
        arr((EXPERTS, SEQ), F32), arr((EXPERTS, SEQ), F32), arr((SEQ, D)), arr((SEQ, D)),
        arr((SEQ, 2 * KV)), arr((SEQ, D)), arr((SEQ, D), F32), arr((SEQ, D)),
    ]
    vm = pl.BlockSpec(memory_space=VMEM)
    hb = pl.BlockSpec(memory_space=ANY)
    sem = pltpu.SemaphoreType.DMA
    return pl.pallas_call(
        front_kernel,
        out_shape=outs,
        in_specs=[vm] * 9,
        out_specs=[hb] * 4 + [vm] * 9,
        scratch_shapes=[
            VMEM((EXPERTS, CAP, D), BF16),
            VMEM((D, D), BF16),
            VMEM((D, 2 * KV), BF16),
            VMEM((D, D), BF16),
            VMEM((SEQ, D), F32),
            VMEM((SEQ, 2 * KV), F32),
            VMEM((SEQ, D), F32),
            sem((3, 8)),
            sem((3, 8)),
            sem((3,)),
            sem((3,)),
            sem((31,)),
            sem((31,)),
            sem((7,)),
        ],
        compiler_params=pltpu.CompilerParams(
            collective_id=0, has_side_effects=True, vmem_limit_bytes=LIMIT
        ),
        name="front",
    )(tokens, cotangent, routes, small, wq, wkv, wo, jnp.asarray(cosine), jnp.asarray(sine))


def norm_back(v, gain, grad):
    scale = lax.rsqrt(jnp.mean(v * v, axis=-1, keepdims=True) + EPSILON)
    unit = v * scale
    w = grad * gain
    return (
        (w - unit * jnp.mean(w * unit, axis=-1, keepdims=True)) * scale,
        jnp.sum(grad * unit, axis=0),
    )


def gelu_parts(a):
    inner = jnp.tanh(0.7978845608028654 * (a + 0.044715 * a * a * a))
    value = 0.5 * a * (1.0 + inner)
    slope = 0.5 * (1.0 + inner) + 0.5 * a * (1.0 - inner * inner) * 0.7978845608028654 * (
        1.0 + 3.0 * 0.044715 * a * a
    )
    return value, slope


def exchange(v):
    return lax.all_to_all(v, "expert", split_axis=0, concat_axis=0, tiled=True)


def pack_small(w_router, norm_one, norm_two):
    return jnp.concatenate(
        [w_router.T, norm_one[None], norm_two[None], jnp.zeros((14, SHARD), BF16)], axis=0
    )


def shards(
    tokens, routes, w_query, key_matrix, value_matrix, w_output, norm_one, norm_two,
    w_router, w_gate, w_up, w_down, cotangent,
):
    small = pack_small(w_router, norm_one, norm_two)
    wkv = jnp.concatenate([key_matrix, value_matrix], axis=1)
    (dy, fq, fkv, fo, small_all, posm, share, n1, q, kv, o, r, n2) = front(
        tokens, cotangent, routes.T, small, w_query, wkv, w_output
    )
    gate = lax.all_gather(w_gate[0], "dp", axis=0, tiled=True)
    up = lax.all_gather(w_up[0], "dp", axis=0, tiled=True)
    down = lax.all_gather(w_down[0], "dp", axis=0, tiled=True)
    D = (posm[:, None, :] == jnp.arange(CAP, dtype=F32)[None, :, None]).astype(BF16)
    D = D.reshape(EXPERTS * CAP, SEQ)
    N = EXPERTS * CAP
    R = exchange(mm(D, n2).astype(BF16).reshape(EXPERTS, CAP, MODEL_WIDTH)).reshape(N, MODEL_WIDTH)
    dy = dy.reshape(N, MODEL_WIDTH)
    a = mm(R, gate)
    b = mm(R, up)
    value, slope = gelu_parts(a)
    hid = (value * b).astype(BF16)
    y = mm(hid, down, 1, 1).astype(BF16)
    y = exchange(y.reshape(EXPERTS, CAP, MODEL_WIDTH)).reshape(N, MODEL_WIDTH)
    dh = mm(dy, down)
    da = (dh * b * slope).astype(BF16)
    db = (dh * value).astype(BF16)
    dR = (mm(da, gate, 1, 1) + mm(db, up, 1, 1)).astype(BF16)
    dR = exchange(dR.reshape(EXPERTS, CAP, MODEL_WIDTH)).reshape(N, MODEL_WIDTH)

    def scatter(v):
        return lax.psum_scatter(v.astype(BF16), "dp", scatter_dimension=0, tiled=True).astype(F32)

    g_gate = scatter(mm(R, da, 0, 0))[None]
    g_up = scatter(mm(R, db, 0, 0))[None]
    g_down = scatter(mm(dy, hid, 0, 0))[None]

    dz = cotangent.astype(F32)
    gain_one = small_all[:, 32].reshape(-1).astype(F32)
    gain_two = small_all[:, 33].reshape(-1).astype(F32)
    router = jnp.transpose(small_all[:, :32], (0, 2, 1)).reshape(MODEL_WIDTH, EXPERTS)
    gslot = jnp.sum(D.reshape(EXPERTS, CAP, SEQ).astype(F32) * share[:, None, :], axis=-1)
    weighted = (D.reshape(EXPERTS, CAP, SEQ).astype(F32) * share[:, None, :]).reshape(N, SEQ)
    hi = weighted.astype(BF16)
    lo = (weighted - hi.astype(F32)).astype(BF16)
    mixed = (r + (mm(hi, y, 0, 0) + mm(lo, y, 0, 0))).astype(BF16)
    dslot = jnp.sum(mm(D, cotangent) * y.astype(F32), axis=-1).reshape(EXPERTS, CAP)
    dg = jnp.sum(D.reshape(EXPERTS, CAP, SEQ).astype(F32) * dslot[:, :, None], axis=1)
    dl = share * (dg - jnp.sum(share * dg, axis=0, keepdims=True))
    dlogits = jnp.where(posm >= 0, dl, 0.0).astype(BF16)
    g_router = mm(tokens, dlogits, 0, 1)
    dn2 = mm(D, dR, 0, 0)
    back, g_two = norm_back(r, gain_two, dn2)
    dr = dz + back
    dA = dr.astype(BF16)
    g_out = mm(o, dA, 0, 0)
    do = mm(dA, fo, 1, 1).astype(BF16)
    cosine, sine = rope_tables()
    causal = causal_mask()
    dqs, dks, dvs = [], [], []
    for c in range(KEY_VALUE_HEADS):
        dk = 0.0
        dv = 0.0
        k_head = kv[:, c * 128 : (c + 1) * 128]
        v_head = kv[:, KV + c * 128 : KV + (c + 1) * 128]
        for h in range(c * 6, c * 6 + 6):
            cut = slice(h * 128, (h + 1) * 128)
            pf = softmax_parts(q[:, cut], k_head, causal)
            dp = mm(do[:, cut], v_head, 1, 1)
            ds = (pf * (dp - jnp.sum(pf * dp, axis=-1, keepdims=True))).astype(BF16)
            dq = mm(ds, k_head) * SCALE
            dqs.append((dq * cosine - jnp.roll(dq, 64, 1) * sine).astype(BF16))
            dk += mm(ds, q[:, cut], 0, 0)
            dv += mm(pf.astype(BF16), do[:, cut], 0, 0)
        dk = dk * SCALE
        dks.append((dk * cosine - jnp.roll(dk, 64, 1) * sine).astype(BF16))
        dvs.append(dv.astype(BF16))
    dqp = jnp.concatenate(dqs, axis=1)
    dkvp = jnp.concatenate(dks + dvs, axis=1)
    dn1 = mm(dqp, fq, 1, 1) + mm(dkvp, fkv, 1, 1)
    g_q = mm(n1, dqp, 0, 0)
    g_kv = mm(n1, dkvp, 0, 0)
    back, g_one = norm_back(tokens.astype(F32), gain_one, dn1)
    g_tok = dr + back + mm(dlogits, router, 0, 1)
    g_small = jnp.concatenate([g_router.T, g_one[None], g_two[None]], axis=0)
    whole = jnp.concatenate([g_q, g_kv, g_out, g_small.T], axis=1).astype(BF16)
    part = lax.psum_scatter(whole, "dp", scatter_dimension=0, tiled=True)
    part = lax.psum(part, "expert").astype(F32)
    D_ = MODEL_WIDTH
    return (
        mixed,
        g_tok,
        part[:, :D_],
        part[:, D_ : D_ + KV],
        part[:, D_ + KV : D_ + 2 * KV],
        part[:, D_ + 2 * KV : 2 * D_ + 2 * KV],
        part[:, 2 * D_ + 2 * KV + 32],
        part[:, 2 * D_ + 2 * KV + 33],
        part[:, 2 * D_ + 2 * KV : 2 * D_ + 2 * KV + 32],
        g_gate,
        g_up,
        g_down,
    )


def solution(mesh):
    rows_split = P(("dp", "expert"), None)
    flat = P("dp", None)
    vector = P("dp")
    owned = P("expert", "dp", None)
    return jax.shard_map(
        shards,
        mesh=mesh,
        in_specs=(
            rows_split, rows_split, flat, flat, flat, flat, vector, vector, flat, owned, owned, owned,
            rows_split,
        ),
        out_specs=(
            rows_split, rows_split, flat, flat, flat, flat, vector, vector, flat, owned, owned, owned,
        ),
        check_vma=False,
    )
```

```python
import functools
import itertools

import jax
import jax.numpy as jnp
import numpy as np
from jax import lax
from jax.experimental import pallas as pl
from jax.experimental.pallas import tpu as pltpu
from jax.sharding import PartitionSpec as P

MODEL_WIDTH = 1536
QUERY_HEADS = 12
KEY_VALUE_HEADS = 2
HEAD_SIZE = 128
TOPK = 4
SEQ = 256
EXPERTS = 32
CAP = 40
FF = 768
KV = KEY_VALUE_HEADS * HEAD_SIZE
SHARD = MODEL_WIDTH // 4
HALF = SHARD // 2
QUARTER = HALF // 2
EPSILON = 1e-06
ROPE_BASE = 10000.0
SCALE = HEAD_SIZE ** (-0.5)
MESH = pl.DeviceIdType.MESH
F32 = jnp.float32
BF16 = jnp.bfloat16
VMEM = pltpu.VMEM
ANY = pl.ANY
LIMIT = 60 * 1024 * 1024


def _offsets():
    def far(a):
        return min(a, 4 - a)

    every = [o for o in itertools.product(range(4), range(4), range(2)) if o != (0, 0, 0)]
    return sorted(every, key=lambda o: (far(o[0]) + far(o[1]), o))[::-1]


OFFSETS = _offsets()


def rope_tables():
    position = np.arange(SEQ, dtype=np.float32)
    frequency = (
        np.float32(ROPE_BASE) ** (-np.arange(64, dtype=np.float32) * np.float32(2.0 / HEAD_SIZE))
    ).astype(np.float32)
    angles = (position[:, None] * frequency[None, :]).astype(np.float32)
    cosine = np.cos(angles.astype(np.float64)).astype(np.float32)
    sine = np.sin(angles.astype(np.float64)).astype(np.float32)
    return (
        np.concatenate([cosine, cosine], axis=1),
        np.concatenate([-sine, sine], axis=1),
    )


def mm(left, right, left_dim=1, right_dim=0):
    return lax.dot_general(
        left, right, (((left_dim,), (right_dim,)), ((), ())), preferred_element_type=F32
    )


class Place:
    def __init__(self):
        self.x = lax.axis_index("dp")
        self.e = lax.axis_index("expert")
        self.core = lax.rem(self.e, 2)
        self.y = lax.rem(self.e // 2, 4)
        self.z = self.e // 8
        self.xl = lax.rem(self.x + 3, 4)
        self.xr = lax.rem(self.x + 1, 4)
        self.x2 = lax.rem(self.x + 2, 4)
        self.left = (self.xl, self.e)
        self.right = (self.xr, self.e)
        self.across = (self.x2, self.e)
        self.sibling = (self.x, self.e + 1 - 2 * self.core)

    def peer(self, offset):
        dz, dy, dc = offset
        return (
            lax.rem(self.z + dz, 4) * 8 + lax.rem(self.y + dy, 4) * 2 + lax.rem(self.core + dc, 2)
        )

    def peers(self):
        return [self.peer(o) for o in OFFSETS]


def greet(devices):
    barrier = pltpu.get_barrier_semaphore()
    for d in devices:
        pl.semaphore_signal(barrier, inc=1, device_id=d, device_id_type=MESH)
    return barrier


def remote(src, dst, send, recv, device):
    return pltpu.make_async_remote_copy(
        src_ref=src, dst_ref=dst, send_sem=send, recv_sem=recv, device_id=device, device_id_type=MESH
    )


def rows(start, count, align=16):
    return pl.ds(pl.multiple_of(start, align), count)


class Gather:
    def __init__(self, place, shard, full, send, recv):
        p = place
        half = p.core * HALF
        other = HALF - half

        def region(x, first, count):
            return full.at[rows(x * SHARD + first, count, 32)]

        def move(k, src, dst, device):
            return remote(src, dst, send.at[k], recv.at[k], device)

        mine = shard.at[rows(half, HALF, 32)]
        self.direct = [
            move(0, mine, region(p.x, half, HALF), p.right),
            move(1, mine, region(p.x, half, HALF), p.left),
        ]
        from_left = region(p.xl, half, QUARTER)
        from_right = region(p.xr, half + QUARTER, QUARTER)
        self.forward = [
            move(2, from_left, from_left, p.right),
            move(3, from_right, from_right, p.left),
        ]
        whole_left = region(p.xl, half, HALF)
        whole_right = region(p.xr, half, HALF)
        far_one = region(p.x2, half, QUARTER)
        far_two = region(p.x2, half + QUARTER, QUARTER)
        self.near = [
            move(4, whole_left, whole_left, p.sibling),
            move(5, whole_right, whole_right, p.sibling),
        ]
        self.far = [
            move(6, far_one, far_one, p.sibling),
            move(7, far_two, far_two, p.sibling),
        ]

    def start(self):
        for c in self.direct:
            c.start()

    def relay(self):
        for k in range(2):
            self.direct[k].wait_recv()
            self.forward[k].start()
            self.near[k].start()

    def relay_far(self):
        for k in range(2):
            self.forward[k].wait_recv()
            self.far[k].start()

    def arrived_near(self):
        for c in self.near:
            c.wait_recv()

    def arrived_far(self):
        for c in self.far:
            c.wait_recv()

    def finish(self):
        for c in self.direct + self.forward + self.near + self.far:
            c.wait_send()


def slot_rows(posm_ref, first, count):
    slot = lax.broadcasted_iota(jnp.int32, (CAP, SEQ), 0).astype(F32)
    return [
        jnp.where(posm_ref[pl.ds(first + j, 1), :] == slot, 1.0, 0.0) for j in range(count)
    ]


def turn(values, cosine, sine):
    return values * cosine + pltpu.roll(values, 64, 1) * sine


def turn_back(values, cosine, sine):
    return values * cosine - pltpu.roll(values, 64, 1) * sine


def softmax_parts(q_head, k_head, causal):
    scores = mm(q_head, k_head, 1, 1) * SCALE
    scores = jnp.where(causal, scores, -jnp.inf)
    largest = jnp.max(scores, axis=-1, keepdims=True)
    exponent = jnp.exp(scores - largest)
    return exponent / jnp.sum(exponent, axis=-1, keepdims=True)


def causal_mask():
    row = lax.broadcasted_iota(jnp.int32, (SEQ, SEQ), 0)
    column = lax.broadcasted_iota(jnp.int32, (SEQ, SEQ), 1)
    return column <= row


def front_kernel(
    tokens, cotangent, routes, small, wq, wkv, wo, cosine, sine,
    dy_in, wq_full, wkv_full, wo_full, small_all, posm, share, n1, q, kv, o, r, n2,
    dy_out, wqf, wkvf, wof, qacc, kvacc, racc,
    gs, gr, ss, sr, as_, ar, ls,
):
    p = Place()
    peers = p.peers()
    barrier = greet([p.left, p.right, p.across] + [(p.x, t) for t in peers])

    lane = lax.broadcasted_iota(jnp.int32, (EXPERTS, SEQ), 0)
    named = routes[0:1, :] == lane
    for j in range(1, TOPK):
        named = jnp.logical_or(named, routes[j : j + 1, :] == lane)
    earlier = (
        lax.broadcasted_iota(jnp.int32, (SEQ, SEQ), 0)
        < lax.broadcasted_iota(jnp.int32, (SEQ, SEQ), 1)
    ).astype(F32).astype(BF16)
    place_of = mm(named.astype(F32).astype(BF16), earlier)
    posm[...] = jnp.where(named, place_of, -1.0)

    small_all[p.x] = small[...]
    pl.semaphore_wait(barrier, len(peers) + 3)

    small_moves = [
        remote(small, small_all.at[p.x], ss.at[k], sr.at[k], d)
        for k, d in enumerate([p.right, p.left, p.across])
    ]
    for c in small_moves:
        c.start()
    gq = Gather(p, wq, wqf, gs.at[0], gr.at[0])
    gkv = Gather(p, wkv, wkvf, gs.at[1], gr.at[1])
    go = Gather(p, wo, wof, gs.at[2], gr.at[2])
    gq.start()
    gkv.start()

    mine = [
        pltpu.make_async_copy(w, f.at[rows(p.x * SHARD, SHARD, 128)], ls.at[k])
        for k, (w, f) in enumerate([(wq, wqf), (wkv, wkvf), (wo, wof)])
    ]
    for c in mine:
        c.start()

    x = tokens[...].astype(F32)
    unit = x * lax.rsqrt(jnp.mean(x * x, axis=-1, keepdims=True) + EPSILON)
    for c in small_moves:
        c.wait_recv()
    for s in range(4):
        cut = slice(s * SHARD, (s + 1) * SHARD)
        n1[:, cut] = (unit[:, cut] * small_all[s, 32:33, :].astype(F32)).astype(BF16)
    logits = mm(small_all[0, 0:32, :], tokens[:, 0:SHARD], 1, 1)
    for s in range(1, 4):
        logits += mm(small_all[s, 0:32, :], tokens[:, s * SHARD : (s + 1) * SHARD], 1, 1)
    top = jnp.max(jnp.where(named, logits, -jnp.inf), axis=0, keepdims=True)
    weight = jnp.where(named, jnp.exp(jnp.minimum(logits - top, 0.0)), 0.0)
    share[...] = weight / jnp.sum(weight, axis=0, keepdims=True)

    @pl.loop(0, EXPERTS // 4)
    def _(i):
        blocks = slot_rows(posm, i * 4, 4)
        gain = jnp.concatenate(
            [
                jnp.sum(b * share[pl.ds(i * 4 + j, 1), :], axis=-1, keepdims=True)
                for j, b in enumerate(blocks)
            ],
            axis=0,
        )
        picked = mm(jnp.concatenate(blocks, axis=0).astype(BF16), cotangent[...])
        dy_out[pl.ds(i * 4, 4)] = (picked * gain).reshape(4, CAP, MODEL_WIDTH).astype(BF16)

    sends = [
        remote(dy_out.at[t], dy_in.at[k], as_.at[k], ar.at[k], (p.x, t))
        for k, t in enumerate(peers)
    ]
    for c in sends:
        c.start()
    own_dy = pltpu.make_async_copy(dy_out.at[p.e], dy_in.at[31], ls.at[3])
    own_dy.start()

    def part(x_index):
        return n1[:, rows(x_index * SHARD, SHARD, 128)]

    def block(full, x_index):
        return full[rows(x_index * SHARD, SHARD, 128), :]

    own = part(p.x)
    qacc[...] = mm(own, wq[...])
    kvacc[...] = mm(own, wkv[...])
    gq.relay()
    gkv.relay()
    go.start()
    gq.arrived_near()
    gkv.arrived_near()
    for s in (p.xl, p.xr):
        qacc[...] += mm(part(s), block(wqf, s))
        kvacc[...] += mm(part(s), block(wkvf, s))
    gq.relay_far()
    gkv.relay_far()
    gq.arrived_far()
    gkv.arrived_far()
    qacc[...] += mm(part(p.x2), block(wqf, p.x2))
    kvacc[...] += mm(part(p.x2), block(wkvf, p.x2))
    for c in mine:
        c.wait()
    keep = [
        pltpu.make_async_copy(f, out, ls.at[4 + k])
        for k, (f, out) in enumerate([(wqf, wq_full), (wkvf, wkv_full), (wof, wo_full)])
    ]
    keep[0].start()
    keep[1].start()

    cos = cosine[...]
    sin = sine[...]
    for h in range(KEY_VALUE_HEADS):
        cut = slice(h * HEAD_SIZE, (h + 1) * HEAD_SIZE)
        kv[:, cut] = turn(kvacc[:, cut], cos, sin).astype(BF16)
        cut = slice(KV + h * HEAD_SIZE, KV + (h + 1) * HEAD_SIZE)
        kv[:, cut] = kvacc[:, cut].astype(BF16)
    causal = causal_mask()
    for h in range(QUERY_HEADS):
        cut = slice(h * HEAD_SIZE, (h + 1) * HEAD_SIZE)
        c = h // (QUERY_HEADS // KEY_VALUE_HEADS)
        q_head = turn(qacc[:, cut], cos, sin).astype(BF16)
        q[:, cut] = q_head
        weights = softmax_parts(q_head, kv[:, c * HEAD_SIZE : (c + 1) * HEAD_SIZE], causal)
        o[:, cut] = mm(
            weights.astype(BF16), kv[:, KV + c * HEAD_SIZE : KV + (c + 1) * HEAD_SIZE]
        ).astype(BF16)

    def opart(x_index):
        return o[:, rows(x_index * SHARD, SHARD, 128)]

    racc[...] = tokens[...].astype(F32) + mm(opart(p.x), wo[...])
    go.relay()
    go.arrived_near()
    for s in (p.xl, p.xr):
        racc[...] += mm(opart(s), block(wof, s))
    go.relay_far()
    go.arrived_far()
    keep[2].start()
    residual = racc[...] + mm(opart(p.x2), block(wof, p.x2))
    r[...] = residual
    unit = residual * lax.rsqrt(jnp.mean(residual * residual, axis=-1, keepdims=True) + EPSILON)
    for s in range(4):
        cut = slice(s * SHARD, (s + 1) * SHARD)
        n2[:, cut] = (unit[:, cut] * small_all[s, 33:34, :].astype(F32)).astype(BF16)

    for c in sends:
        c.wait()
    own_dy.wait()
    for c in small_moves:
        c.wait_send()
    for g in (gq, gkv, go):
        g.finish()
    for c in keep:
        c.wait()


def front(tokens, cotangent, routes, small, wq, wkv, wo):
    cosine, sine = rope_tables()
    D = MODEL_WIDTH

    def arr(shape, dtype=BF16):
        return jax.ShapeDtypeStruct(shape, dtype)

    outs = [
        arr((EXPERTS, CAP, D)), arr((D, D)), arr((D, 2 * KV)), arr((D, D)), arr((4, 48, SHARD)),
        arr((EXPERTS, SEQ), F32), arr((EXPERTS, SEQ), F32), arr((SEQ, D)), arr((SEQ, D)),
        arr((SEQ, 2 * KV)), arr((SEQ, D)), arr((SEQ, D), F32), arr((SEQ, D)),
    ]
    vm = pl.BlockSpec(memory_space=VMEM)
    hb = pl.BlockSpec(memory_space=ANY)
    sem = pltpu.SemaphoreType.DMA
    return pl.pallas_call(
        front_kernel,
        out_shape=outs,
        in_specs=[vm] * 9,
        out_specs=[hb] * 4 + [vm] * 9,
        scratch_shapes=[
            VMEM((EXPERTS, CAP, D), BF16),
            VMEM((D, D), BF16),
            VMEM((D, 2 * KV), BF16),
            VMEM((D, D), BF16),
            VMEM((SEQ, D), F32),
            VMEM((SEQ, 2 * KV), F32),
            VMEM((SEQ, D), F32),
            sem((3, 8)),
            sem((3, 8)),
            sem((3,)),
            sem((3,)),
            sem((31,)),
            sem((31,)),
            sem((7,)),
        ],
        compiler_params=pltpu.CompilerParams(
            collective_id=0, has_side_effects=True, vmem_limit_bytes=LIMIT
        ),
        name="front",
    )(tokens, cotangent, routes, small, wq, wkv, wo, jnp.asarray(cosine), jnp.asarray(sine))


def norm_back(v, gain, grad):
    scale = lax.rsqrt(jnp.mean(v * v, axis=-1, keepdims=True) + EPSILON)
    unit = v * scale
    w = grad * gain
    return (
        (w - unit * jnp.mean(w * unit, axis=-1, keepdims=True)) * scale,
        jnp.sum(grad * unit, axis=0),
    )


def gelu_parts(a):
    inner = jnp.tanh(0.7978845608028654 * (a + 0.044715 * a * a * a))
    value = 0.5 * a * (1.0 + inner)
    slope = 0.5 * (1.0 + inner) + 0.5 * a * (1.0 - inner * inner) * 0.7978845608028654 * (
        1.0 + 3.0 * 0.044715 * a * a
    )
    return value, slope


class GatherOwn:
    def __init__(self, place, shard, region, send, recv):
        p = place

        def move(k, src, dst, device):
            return remote(src, dst, send.at[k], recv.at[k], device)

        self.direct = [
            move(0, shard, region(p.x, 0, SHARD), p.right),
            move(1, shard, region(p.x, 0, SHARD), p.left),
        ]
        from_left = region(p.xl, 0, HALF)
        from_right = region(p.xr, HALF, HALF)
        self.forward = [
            move(2, from_left, from_left, p.right),
            move(3, from_right, from_right, p.left),
        ]

    def start(self):
        for c in self.direct:
            c.start()

    def relay(self):
        for k in range(2):
            self.direct[k].wait_recv()
            self.forward[k].start()

    def arrived(self):
        for c in self.forward:
            c.wait_recv()

    def finish(self):
        for c in self.direct + self.forward:
            c.wait_send()


class Scatter:
    def __init__(self, place, partial, landing, send, recv, first=0, height=SHARD):
        p = self.p = place
        half = height // 2
        self.partial, self.landing, self.first, self.height = partial, landing, first, height

        def region(x, part):
            return partial.at[rows(x * SHARD + first + part * half, half, 32)]

        def move(k, src, device):
            return remote(src, landing.at[k], send.at[k], recv.at[k], device)

        self.far = [move(0, region(p.x2, 0), p.right), move(1, region(p.x2, 1), p.left)]
        self.near = [move(2, region(p.xr, 1), p.right), move(3, region(p.xl, 0), p.left)]
        self.summed = [move(4, region(p.xr, 0), p.right), move(5, region(p.xl, 1), p.left)]

    def relay(self):
        p, half = self.p, self.height // 2
        for k, x, part in ((0, p.xr, 0), (1, p.xl, 1)):
            self.far[k].wait_recv()
            where = rows(x * SHARD + self.first + part * half, half, 32)
            self.partial[where, :] = (
                self.partial[where, :].astype(F32) + self.landing[k].astype(F32)
            ).astype(BF16)
            self.summed[k].start()

    def result(self, part, columns=slice(None)):
        p, half = self.p, self.height // 2
        own = self.partial[rows(p.x * SHARD + self.first + part * half, half, 32), columns]
        one, two = ((4, 3), (2, 5))[part]
        return (
            own.astype(F32)
            + self.landing[one, :, columns].astype(F32)
            + self.landing[two, :, columns].astype(F32)
        )

    def arrived(self):
        for c in self.near + self.summed:
            c.wait_recv()

    def finish(self):
        for c in self.far + self.near + self.summed:
            c.wait_send()


GROUP = 8
BLOCK = GROUP * CAP


def flatten(slots):
    return slots.astype(F32).reshape(BLOCK, MODEL_WIDTH).astype(BF16)


def unflatten(values):
    return values.reshape(GROUP, CAP, MODEL_WIDTH).astype(BF16)


def expert_kernel(
    n2, posm, wgate, wup, wdown, dy,
    dr_in, y_out, g_gate, g_up, g_down,
    sendbuf, landing, ybuf, rflat, dyflat, wgu, wd, hid, gab, dab, part_down, part_gu, land_down, land_gu,
    gs, gr, ns, nr, bs, br, ss, sr, ls,
):
    p = Place()
    peers = p.peers()
    sources = [p.peer(tuple((-v) % m for v, m in zip(o, (4, 4, 2)))) for o in OFFSETS]
    barrier = greet([p.left, p.right] + [(p.x, t) for t in peers])
    load_dy = pltpu.make_async_copy(dy, ybuf, ls.at[0])
    load_dy.start()

    def columns(full, first):
        return lambda x, start, count: full.at[
            rows(x * SHARD + start, count, 32), pl.ds(first, FF)
        ]

    mine = [
        pltpu.make_async_copy(w, f(p.x, 0, SHARD), ls.at[1 + k])
        for k, (w, f) in enumerate(
            [(wgate, columns(wgu, 0)), (wup, columns(wgu, FF)), (wdown, columns(wd, 0))]
        )
    ]
    for c in mine:
        c.start()

    @pl.loop(0, EXPERTS // 4)
    def _(i):
        hot = jnp.concatenate(slot_rows(posm, i * 4, 4), axis=0).astype(BF16)
        sendbuf[pl.ds(i * 4, 4)] = mm(hot, n2[...]).reshape(4, CAP, MODEL_WIDTH).astype(BF16)

    pl.semaphore_wait(barrier, len(peers) + 2)
    ggate = GatherOwn(p, wgate, columns(wgu, 0), gs.at[0], gr.at[0])
    gup = GatherOwn(p, wup, columns(wgu, FF), gs.at[1], gr.at[1])
    gdown = GatherOwn(p, wdown, columns(wd, 0), gs.at[2], gr.at[2])
    ggate.start()
    gup.start()
    sends = [
        remote(sendbuf.at[t], landing.at[k], ns.at[k], nr.at[k], (p.x, t))
        for k, t in enumerate(peers)
    ]
    for c in sends:
        c.start()
    own_rows = pltpu.make_async_copy(sendbuf.at[p.e], landing.at[31], ls.at[4])
    own_rows.start()

    load_dy.wait()

    @pl.loop(0, 4)
    def _(i):
        dyflat[rows(i * BLOCK, BLOCK), :] = flatten(ybuf[pl.ds(i * GROUP, GROUP)])

    ggate.relay()
    gup.relay()
    gdown.start()
    for c in mine:
        c.wait()
    ggate.arrived()
    gup.arrived()

    for i in range(4):
        for c in sends[i * GROUP : (i + 1) * GROUP]:
            c.wait_recv()
        if i == 3:
            own_rows.wait()
        cut = slice(i * BLOCK, (i + 1) * BLOCK)
        rflat[cut, :] = flatten(landing[i * GROUP : (i + 1) * GROUP])
        ab = mm(rflat[cut, :], wgu[...])
        value, slope = gelu_parts(ab[:, :FF])
        b = ab[:, FF:]
        hid[cut, :] = (value * b).astype(BF16)
        gab[cut, :FF] = (slope * b).astype(BF16)
        gab[cut, FF:] = value.astype(BF16)

    sdown = Scatter(p, part_down, land_down, ss.at[0], sr.at[0])
    sgu = Scatter(p, part_gu, land_gu, ss.at[1], sr.at[1])

    def down_block(x):
        where = rows(x * SHARD, SHARD, 128)
        part_down[where, :] = mm(dyflat[:, where], hid[...], 0, 0).astype(BF16)

    down_block(p.x2)
    for c in sdown.far:
        c.start()
    gdown.relay()
    down_block(p.xr)
    sdown.near[0].start()
    down_block(p.xl)
    sdown.near[1].start()
    down_block(p.x)
    gdown.arrived()

    for c in sends:
        c.wait_send()
    backs = []
    for i in range(4):
        cut = slice(i * BLOCK, (i + 1) * BLOCK)
        dh = mm(dyflat[cut, :], wd[...])
        dab[cut, :FF] = (dh * gab[cut, :FF].astype(F32)).astype(BF16)
        dab[cut, FF:] = (dh * gab[cut, FF:].astype(F32)).astype(BF16)
        sendbuf[i * GROUP : (i + 1) * GROUP] = unflatten(mm(dab[cut, :], wgu[...], 1, 1))
        for k in range(i * GROUP, min((i + 1) * GROUP, 31)):
            c = remote(sendbuf.at[k], dr_in.at[p.e], bs.at[k], br.at[k], (p.x, sources[k]))
            c.start()
            backs.append(c)
        if i == 1:
            sdown.relay()
    own_back = pltpu.make_async_copy(sendbuf.at[31], dr_in.at[p.e], ls.at[5])
    own_back.start()

    def gu_block(x):
        where = rows(x * SHARD, SHARD, 128)
        part_gu[where, :] = mm(rflat[:, where], dab[...], 0, 0).astype(BF16)

    gu_block(p.x2)
    for c in sgu.far:
        c.start()
    gu_block(p.xr)
    sgu.near[0].start()
    gu_block(p.xl)
    sgu.near[1].start()
    gu_block(p.x)

    for i in range(4):
        cut = slice(i * BLOCK, (i + 1) * BLOCK)
        ybuf[i * GROUP : (i + 1) * GROUP] = unflatten(mm(hid[cut, :], wd[...], 1, 1))
    keep_y = pltpu.make_async_copy(ybuf, y_out, ls.at[6])
    keep_y.start()

    sdown.arrived()
    for part in range(2):
        g_down[part * HALF : (part + 1) * HALF, :] = sdown.result(part)
    sgu.relay()
    sgu.arrived()
    for part in range(2):
        cut = slice(part * HALF, (part + 1) * HALF)
        g_gate[cut, :] = sgu.result(part, slice(0, FF))
        g_up[cut, :] = sgu.result(part, slice(FF, 2 * FF))

    for c in backs:
        c.wait()
    own_back.wait()
    keep_y.wait()
    for g in (ggate, gup, gdown, sdown, sgu):
        g.finish()


def experts(n2, posm, wgate, wup, wdown, dy):
    D = MODEL_WIDTH

    def arr(shape, dtype=BF16):
        return jax.ShapeDtypeStruct(shape, dtype)

    vm = pl.BlockSpec(memory_space=VMEM)
    hb = pl.BlockSpec(memory_space=ANY)
    sem = pltpu.SemaphoreType.DMA
    N = EXPERTS * CAP
    return pl.pallas_call(
        expert_kernel,
        out_shape=[
            arr((EXPERTS, CAP, D)), arr((EXPERTS, CAP, D)),
            arr((SHARD, FF), F32), arr((SHARD, FF), F32), arr((SHARD, FF), F32),
        ],
        in_specs=[vm] * 5 + [hb],
        out_specs=[hb, hb, vm, vm, vm],
        scratch_shapes=[
            VMEM((EXPERTS, CAP, D), BF16),
            VMEM((EXPERTS, CAP, D), BF16),
            VMEM((EXPERTS, CAP, D), BF16),
            VMEM((N, D), BF16),
            VMEM((N, D), BF16),
            VMEM((D, 2 * FF), BF16),
            VMEM((D, FF), BF16),
            VMEM((N, FF), BF16),
            VMEM((N, 2 * FF), BF16),
            VMEM((N, 2 * FF), BF16),
            VMEM((D, FF), BF16),
            VMEM((D, 2 * FF), BF16),
            VMEM((6, HALF, FF), BF16),
            VMEM((6, HALF, 2 * FF), BF16),
            sem((3, 4)),
            sem((3, 4)),
            sem((31,)),
            sem((31,)),
            sem((31,)),
            sem((31,)),
            sem((2, 6)),
            sem((2, 6)),
            sem((7,)),
        ],
        compiler_params=pltpu.CompilerParams(
            collective_id=1, has_side_effects=True, vmem_limit_bytes=LIMIT
        ),
        name="experts",
    )(n2, posm, wgate, wup, wdown, dy)


def y_slots(y):
    e = lax.axis_index("expert")
    z, yy, c = e // 8, lax.rem(e // 2, 4), lax.rem(e, 2)
    order = jnp.array(OFFSETS + [(0, 0, 0)], jnp.int32)
    source = (
        lax.rem(z - order[:, 0] + 4, 4) * 8
        + lax.rem(yy - order[:, 1] + 4, 4) * 2
        + lax.rem(c - order[:, 2] + 2, 2)
    )
    return jnp.zeros_like(y).at[source].set(y)


def exchange(v):
    return lax.all_to_all(v, "expert", split_axis=0, concat_axis=0, tiled=True)


def pack_small(w_router, norm_one, norm_two):
    return jnp.concatenate(
        [w_router.T, norm_one[None], norm_two[None], jnp.zeros((14, SHARD), BF16)], axis=0
    )


def shards(
    tokens, routes, w_query, key_matrix, value_matrix, w_output, norm_one, norm_two,
    w_router, w_gate, w_up, w_down, cotangent,
):
    small = pack_small(w_router, norm_one, norm_two)
    wkv = jnp.concatenate([key_matrix, value_matrix], axis=1)
    (dy, fq, fkv, fo, small_all, posm, share, n1, q, kv, o, r, n2) = front(
        tokens, cotangent, routes.T, small, w_query, wkv, w_output
    )
    dR, y, g_gate, g_up, g_down = experts(n2, posm, w_gate[0], w_up[0], w_down[0], dy)
    D = (posm[:, None, :] == jnp.arange(CAP, dtype=F32)[None, :, None]).astype(BF16)
    D = D.reshape(EXPERTS * CAP, SEQ)
    N = EXPERTS * CAP
    y = exchange(y_slots(y)).reshape(N, MODEL_WIDTH)
    dR = dR.reshape(N, MODEL_WIDTH)
    g_gate, g_up, g_down = g_gate[None], g_up[None], g_down[None]

    dz = cotangent.astype(F32)
    gain_one = small_all[:, 32].reshape(-1).astype(F32)
    gain_two = small_all[:, 33].reshape(-1).astype(F32)
    router = jnp.transpose(small_all[:, :32], (0, 2, 1)).reshape(MODEL_WIDTH, EXPERTS)
    gslot = jnp.sum(D.reshape(EXPERTS, CAP, SEQ).astype(F32) * share[:, None, :], axis=-1)
    weighted = (D.reshape(EXPERTS, CAP, SEQ).astype(F32) * share[:, None, :]).reshape(N, SEQ)
    hi = weighted.astype(BF16)
    lo = (weighted - hi.astype(F32)).astype(BF16)
    mixed = (r + (mm(hi, y, 0, 0) + mm(lo, y, 0, 0))).astype(BF16)
    dslot = jnp.sum(mm(D, cotangent) * y.astype(F32), axis=-1).reshape(EXPERTS, CAP)
    dg = jnp.sum(D.reshape(EXPERTS, CAP, SEQ).astype(F32) * dslot[:, :, None], axis=1)
    dl = share * (dg - jnp.sum(share * dg, axis=0, keepdims=True))
    dlogits = jnp.where(posm >= 0, dl, 0.0).astype(BF16)
    g_router = mm(tokens, dlogits, 0, 1)
    dn2 = mm(D, dR, 0, 0)
    back, g_two = norm_back(r, gain_two, dn2)
    dr = dz + back
    dA = dr.astype(BF16)
    g_out = mm(o, dA, 0, 0)
    do = mm(dA, fo, 1, 1).astype(BF16)
    cosine, sine = rope_tables()
    causal = causal_mask()
    dqs, dks, dvs = [], [], []
    for c in range(KEY_VALUE_HEADS):
        dk = 0.0
        dv = 0.0
        k_head = kv[:, c * 128 : (c + 1) * 128]
        v_head = kv[:, KV + c * 128 : KV + (c + 1) * 128]
        for h in range(c * 6, c * 6 + 6):
            cut = slice(h * 128, (h + 1) * 128)
            pf = softmax_parts(q[:, cut], k_head, causal)
            dp = mm(do[:, cut], v_head, 1, 1)
            ds = (pf * (dp - jnp.sum(pf * dp, axis=-1, keepdims=True))).astype(BF16)
            dq = mm(ds, k_head) * SCALE
            dqs.append((dq * cosine - jnp.roll(dq, 64, 1) * sine).astype(BF16))
            dk += mm(ds, q[:, cut], 0, 0)
            dv += mm(pf.astype(BF16), do[:, cut], 0, 0)
        dk = dk * SCALE
        dks.append((dk * cosine - jnp.roll(dk, 64, 1) * sine).astype(BF16))
        dvs.append(dv.astype(BF16))
    dqp = jnp.concatenate(dqs, axis=1)
    dkvp = jnp.concatenate(dks + dvs, axis=1)
    dn1 = mm(dqp, fq, 1, 1) + mm(dkvp, fkv, 1, 1)
    g_q = mm(n1, dqp, 0, 0)
    g_kv = mm(n1, dkvp, 0, 0)
    back, g_one = norm_back(tokens.astype(F32), gain_one, dn1)
    g_tok = dr + back + mm(dlogits, router, 0, 1)
    g_small = jnp.concatenate([g_router.T, g_one[None], g_two[None]], axis=0)
    whole = jnp.concatenate([g_q, g_kv, g_out, g_small.T], axis=1).astype(BF16)
    part = lax.psum_scatter(whole, "dp", scatter_dimension=0, tiled=True)
    part = lax.psum(part, "expert").astype(F32)
    D_ = MODEL_WIDTH
    return (
        mixed,
        g_tok,
        part[:, :D_],
        part[:, D_ : D_ + KV],
        part[:, D_ + KV : D_ + 2 * KV],
        part[:, D_ + 2 * KV : 2 * D_ + 2 * KV],
        part[:, 2 * D_ + 2 * KV + 32],
        part[:, 2 * D_ + 2 * KV + 33],
        part[:, 2 * D_ + 2 * KV : 2 * D_ + 2 * KV + 32],
        g_gate,
        g_up,
        g_down,
    )


def solution(mesh):
    rows_split = P(("dp", "expert"), None)
    flat = P("dp", None)
    vector = P("dp")
    owned = P("expert", "dp", None)
    return jax.shard_map(
        shards,
        mesh=mesh,
        in_specs=(
            rows_split, rows_split, flat, flat, flat, flat, vector, vector, flat, owned, owned, owned,
            rows_split,
        ),
        out_specs=(
            rows_split, rows_split, flat, flat, flat, flat, vector, vector, flat, owned, owned, owned,
        ),
        check_vma=False,
    )
```

```python
import functools
import itertools

import jax
import jax.numpy as jnp
import numpy as np
from jax import lax
from jax.experimental import pallas as pl
from jax.experimental.pallas import tpu as pltpu
from jax.sharding import PartitionSpec as P

MODEL_WIDTH = 1536
QUERY_HEADS = 12
KEY_VALUE_HEADS = 2
HEAD_SIZE = 128
TOPK = 4
SEQ = 256
EXPERTS = 32
CAP = 40
FF = 768
KV = KEY_VALUE_HEADS * HEAD_SIZE
SHARD = MODEL_WIDTH // 4
HALF = SHARD // 2
QUARTER = HALF // 2
EPSILON = 1e-06
ROPE_BASE = 10000.0
SCALE = HEAD_SIZE ** (-0.5)
MESH = pl.DeviceIdType.MESH
F32 = jnp.float32
BF16 = jnp.bfloat16
VMEM = pltpu.VMEM
ANY = pl.ANY
LIMIT = 60 * 1024 * 1024


def _offsets():
    def far(a):
        return min(a, 4 - a)

    every = [o for o in itertools.product(range(4), range(4), range(2)) if o != (0, 0, 0)]
    return sorted(every, key=lambda o: (far(o[0]) + far(o[1]), o))[::-1]


OFFSETS = _offsets()


def rope_tables():
    position = np.arange(SEQ, dtype=np.float32)
    frequency = (
        np.float32(ROPE_BASE) ** (-np.arange(64, dtype=np.float32) * np.float32(2.0 / HEAD_SIZE))
    ).astype(np.float32)
    angles = (position[:, None] * frequency[None, :]).astype(np.float32)
    cosine = np.cos(angles.astype(np.float64)).astype(np.float32)
    sine = np.sin(angles.astype(np.float64)).astype(np.float32)
    return (
        np.concatenate([cosine, cosine], axis=1),
        np.concatenate([-sine, sine], axis=1),
    )


def mm(left, right, left_dim=1, right_dim=0):
    return lax.dot_general(
        left, right, (((left_dim,), (right_dim,)), ((), ())), preferred_element_type=F32
    )


class Place:
    def __init__(self):
        self.x = lax.axis_index("dp")
        self.e = lax.axis_index("expert")
        self.core = lax.rem(self.e, 2)
        self.y = lax.rem(self.e // 2, 4)
        self.z = self.e // 8
        self.xl = lax.rem(self.x + 3, 4)
        self.xr = lax.rem(self.x + 1, 4)
        self.x2 = lax.rem(self.x + 2, 4)
        self.left = (self.xl, self.e)
        self.right = (self.xr, self.e)
        self.across = (self.x2, self.e)
        self.sibling = (self.x, self.e + 1 - 2 * self.core)

    def peer(self, offset):
        dz, dy, dc = offset
        return (
            lax.rem(self.z + dz, 4) * 8 + lax.rem(self.y + dy, 4) * 2 + lax.rem(self.core + dc, 2)
        )

    def peers(self):
        return [self.peer(o) for o in OFFSETS]


def greet(devices):
    barrier = pltpu.get_barrier_semaphore()
    for d in devices:
        pl.semaphore_signal(barrier, inc=1, device_id=d, device_id_type=MESH)
    return barrier


def remote(src, dst, send, recv, device):
    return pltpu.make_async_remote_copy(
        src_ref=src, dst_ref=dst, send_sem=send, recv_sem=recv, device_id=device, device_id_type=MESH
    )


def rows(start, count, align=16):
    return pl.ds(pl.multiple_of(start, align), count)


class Gather:
    def __init__(self, place, shard, full, send, recv):
        p = place
        half = p.core * HALF
        other = HALF - half

        def region(x, first, count):
            return full.at[rows(x * SHARD + first, count, 32)]

        def move(k, src, dst, device):
            return remote(src, dst, send.at[k], recv.at[k], device)

        mine = shard.at[rows(half, HALF, 32)]
        self.direct = [
            move(0, mine, region(p.x, half, HALF), p.right),
            move(1, mine, region(p.x, half, HALF), p.left),
        ]
        from_left = region(p.xl, half, QUARTER)
        from_right = region(p.xr, half + QUARTER, QUARTER)
        self.forward = [
            move(2, from_left, from_left, p.right),
            move(3, from_right, from_right, p.left),
        ]
        whole_left = region(p.xl, half, HALF)
        whole_right = region(p.xr, half, HALF)
        far_one = region(p.x2, half, QUARTER)
        far_two = region(p.x2, half + QUARTER, QUARTER)
        self.near = [
            move(4, whole_left, whole_left, p.sibling),
            move(5, whole_right, whole_right, p.sibling),
        ]
        self.far = [
            move(6, far_one, far_one, p.sibling),
            move(7, far_two, far_two, p.sibling),
        ]

    def start(self):
        for c in self.direct:
            c.start()

    def relay(self):
        for k in range(2):
            self.direct[k].wait_recv()
            self.forward[k].start()
            self.near[k].start()

    def relay_far(self):
        for k in range(2):
            self.forward[k].wait_recv()
            self.far[k].start()

    def arrived_near(self):
        for c in self.near:
            c.wait_recv()

    def arrived_far(self):
        for c in self.far:
            c.wait_recv()

    def finish(self):
        for c in self.direct + self.forward + self.near + self.far:
            c.wait_send()


def slot_rows(posm_ref, first, count):
    slot = lax.broadcasted_iota(jnp.int32, (CAP, SEQ), 0).astype(F32)
    return [
        jnp.where(posm_ref[pl.ds(first + j, 1), :] == slot, 1.0, 0.0) for j in range(count)
    ]


def turn(values, cosine, sine):
    return values * cosine + pltpu.roll(values, 64, 1) * sine


def turn_back(values, cosine, sine):
    return values * cosine - pltpu.roll(values, 64, 1) * sine


def softmax_parts(q_head, k_head, causal):
    scores = mm(q_head, k_head, 1, 1) * SCALE
    scores = jnp.where(causal, scores, -jnp.inf)
    largest = jnp.max(scores, axis=-1, keepdims=True)
    exponent = jnp.exp(scores - largest)
    return exponent / jnp.sum(exponent, axis=-1, keepdims=True)


def causal_mask():
    row = lax.broadcasted_iota(jnp.int32, (SEQ, SEQ), 0)
    column = lax.broadcasted_iota(jnp.int32, (SEQ, SEQ), 1)
    return column <= row


def front_kernel(
    tokens, cotangent, routes, small, wq, wkv, wo, cosine, sine,
    dy_in, wq_full, wkv_full, wo_full, small_all, posm, share, n1, q, kv, o, r, n2,
    dy_out, wqf, wkvf, wof, qacc, kvacc, racc,
    gs, gr, ss, sr, as_, ar, ls,
):
    p = Place()
    peers = p.peers()
    barrier = greet([p.left, p.right, p.across] + [(p.x, t) for t in peers])

    lane = lax.broadcasted_iota(jnp.int32, (EXPERTS, SEQ), 0)
    named = routes[0:1, :] == lane
    for j in range(1, TOPK):
        named = jnp.logical_or(named, routes[j : j + 1, :] == lane)
    earlier = (
        lax.broadcasted_iota(jnp.int32, (SEQ, SEQ), 0)
        < lax.broadcasted_iota(jnp.int32, (SEQ, SEQ), 1)
    ).astype(F32).astype(BF16)
    place_of = mm(named.astype(F32).astype(BF16), earlier)
    posm[...] = jnp.where(named, place_of, -1.0)

    small_all[p.x] = small[...]
    pl.semaphore_wait(barrier, len(peers) + 3)

    small_moves = [
        remote(small, small_all.at[p.x], ss.at[k], sr.at[k], d)
        for k, d in enumerate([p.right, p.left, p.across])
    ]
    for c in small_moves:
        c.start()
    gq = Gather(p, wq, wqf, gs.at[0], gr.at[0])
    gkv = Gather(p, wkv, wkvf, gs.at[1], gr.at[1])
    go = Gather(p, wo, wof, gs.at[2], gr.at[2])
    gq.start()
    gkv.start()

    mine = [
        pltpu.make_async_copy(w, f.at[rows(p.x * SHARD, SHARD, 128)], ls.at[k])
        for k, (w, f) in enumerate([(wq, wqf), (wkv, wkvf), (wo, wof)])
    ]
    for c in mine:
        c.start()

    x = tokens[...].astype(F32)
    unit = x * lax.rsqrt(jnp.mean(x * x, axis=-1, keepdims=True) + EPSILON)
    for c in small_moves:
        c.wait_recv()
    for s in range(4):
        cut = slice(s * SHARD, (s + 1) * SHARD)
        n1[:, cut] = (unit[:, cut] * small_all[s, 32:33, :].astype(F32)).astype(BF16)
    logits = mm(small_all[0, 0:32, :], tokens[:, 0:SHARD], 1, 1)
    for s in range(1, 4):
        logits += mm(small_all[s, 0:32, :], tokens[:, s * SHARD : (s + 1) * SHARD], 1, 1)
    top = jnp.max(jnp.where(named, logits, -jnp.inf), axis=0, keepdims=True)
    weight = jnp.where(named, jnp.exp(jnp.minimum(logits - top, 0.0)), 0.0)
    share[...] = weight / jnp.sum(weight, axis=0, keepdims=True)

    @pl.loop(0, EXPERTS // 4)
    def _(i):
        blocks = slot_rows(posm, i * 4, 4)
        gain = jnp.concatenate(
            [
                jnp.sum(b * share[pl.ds(i * 4 + j, 1), :], axis=-1, keepdims=True)
                for j, b in enumerate(blocks)
            ],
            axis=0,
        )
        picked = mm(jnp.concatenate(blocks, axis=0).astype(BF16), cotangent[...])
        dy_out[pl.ds(i * 4, 4)] = (picked * gain).reshape(4, CAP, MODEL_WIDTH).astype(BF16)

    sends = [
        remote(dy_out.at[t], dy_in.at[k], as_.at[k], ar.at[k], (p.x, t))
        for k, t in enumerate(peers)
    ]
    for c in sends:
        c.start()
    own_dy = pltpu.make_async_copy(dy_out.at[p.e], dy_in.at[31], ls.at[3])
    own_dy.start()

    def part(x_index):
        return n1[:, rows(x_index * SHARD, SHARD, 128)]

    def block(full, x_index):
        return full[rows(x_index * SHARD, SHARD, 128), :]

    own = part(p.x)
    qacc[...] = mm(own, wq[...])
    kvacc[...] = mm(own, wkv[...])
    gq.relay()
    gkv.relay()
    go.start()
    gq.arrived_near()
    gkv.arrived_near()
    for s in (p.xl, p.xr):
        qacc[...] += mm(part(s), block(wqf, s))
        kvacc[...] += mm(part(s), block(wkvf, s))
    gq.relay_far()
    gkv.relay_far()
    gq.arrived_far()
    gkv.arrived_far()
    qacc[...] += mm(part(p.x2), block(wqf, p.x2))
    kvacc[...] += mm(part(p.x2), block(wkvf, p.x2))
    for c in mine:
        c.wait()
    keep = [
        pltpu.make_async_copy(f, out, ls.at[4 + k])
        for k, (f, out) in enumerate([(wqf, wq_full), (wkvf, wkv_full), (wof, wo_full)])
    ]
    keep[0].start()
    keep[1].start()

    cos = cosine[...]
    sin = sine[...]
    for h in range(KEY_VALUE_HEADS):
        cut = slice(h * HEAD_SIZE, (h + 1) * HEAD_SIZE)
        kv[:, cut] = turn(kvacc[:, cut], cos, sin).astype(BF16)
        cut = slice(KV + h * HEAD_SIZE, KV + (h + 1) * HEAD_SIZE)
        kv[:, cut] = kvacc[:, cut].astype(BF16)
    causal = causal_mask()
    for h in range(QUERY_HEADS):
        cut = slice(h * HEAD_SIZE, (h + 1) * HEAD_SIZE)
        c = h // (QUERY_HEADS // KEY_VALUE_HEADS)
        q_head = turn(qacc[:, cut], cos, sin).astype(BF16)
        q[:, cut] = q_head
        weights = softmax_parts(q_head, kv[:, c * HEAD_SIZE : (c + 1) * HEAD_SIZE], causal)
        o[:, cut] = mm(
            weights.astype(BF16), kv[:, KV + c * HEAD_SIZE : KV + (c + 1) * HEAD_SIZE]
        ).astype(BF16)

    def opart(x_index):
        return o[:, rows(x_index * SHARD, SHARD, 128)]

    racc[...] = tokens[...].astype(F32) + mm(opart(p.x), wo[...])
    go.relay()
    go.arrived_near()
    for s in (p.xl, p.xr):
        racc[...] += mm(opart(s), block(wof, s))
    go.relay_far()
    go.arrived_far()
    keep[2].start()
    residual = racc[...] + mm(opart(p.x2), block(wof, p.x2))
    r[...] = residual
    unit = residual * lax.rsqrt(jnp.mean(residual * residual, axis=-1, keepdims=True) + EPSILON)
    for s in range(4):
        cut = slice(s * SHARD, (s + 1) * SHARD)
        n2[:, cut] = (unit[:, cut] * small_all[s, 33:34, :].astype(F32)).astype(BF16)

    for c in sends:
        c.wait()
    own_dy.wait()
    for c in small_moves:
        c.wait_send()
    for g in (gq, gkv, go):
        g.finish()
    for c in keep:
        c.wait()


def front(tokens, cotangent, routes, small, wq, wkv, wo):
    cosine, sine = rope_tables()
    D = MODEL_WIDTH

    def arr(shape, dtype=BF16):
        return jax.ShapeDtypeStruct(shape, dtype)

    outs = [
        arr((EXPERTS, CAP, D)), arr((D, D)), arr((D, 2 * KV)), arr((D, D)), arr((4, 48, SHARD)),
        arr((EXPERTS, SEQ), F32), arr((EXPERTS, SEQ), F32), arr((SEQ, D)), arr((SEQ, D)),
        arr((SEQ, 2 * KV)), arr((SEQ, D)), arr((SEQ, D), F32), arr((SEQ, D)),
    ]
    vm = pl.BlockSpec(memory_space=VMEM)
    hb = pl.BlockSpec(memory_space=ANY)
    sem = pltpu.SemaphoreType.DMA
    return pl.pallas_call(
        front_kernel,
        out_shape=outs,
        in_specs=[vm] * 9,
        out_specs=[hb] * 4 + [vm] * 9,
        scratch_shapes=[
            VMEM((EXPERTS, CAP, D), BF16),
            VMEM((D, D), BF16),
            VMEM((D, 2 * KV), BF16),
            VMEM((D, D), BF16),
            VMEM((SEQ, D), F32),
            VMEM((SEQ, 2 * KV), F32),
            VMEM((SEQ, D), F32),
            sem((3, 8)),
            sem((3, 8)),
            sem((3,)),
            sem((3,)),
            sem((31,)),
            sem((31,)),
            sem((7,)),
        ],
        compiler_params=pltpu.CompilerParams(
            collective_id=0, has_side_effects=True, vmem_limit_bytes=LIMIT
        ),
        name="front",
    )(tokens, cotangent, routes, small, wq, wkv, wo, jnp.asarray(cosine), jnp.asarray(sine))


def norm_back(v, gain, grad):
    scale = lax.rsqrt(jnp.mean(v * v, axis=-1, keepdims=True) + EPSILON)
    unit = v * scale
    w = grad * gain
    return (
        (w - unit * jnp.mean(w * unit, axis=-1, keepdims=True)) * scale,
        jnp.sum(grad * unit, axis=0, keepdims=True),
    )


def gelu_parts(a):
    inner = jnp.tanh(0.7978845608028654 * (a + 0.044715 * a * a * a))
    value = 0.5 * a * (1.0 + inner)
    slope = 0.5 * (1.0 + inner) + 0.5 * a * (1.0 - inner * inner) * 0.7978845608028654 * (
        1.0 + 3.0 * 0.044715 * a * a
    )
    return value, slope


class GatherOwn:
    def __init__(self, place, shard, region, send, recv):
        p = place

        def move(k, src, dst, device):
            return remote(src, dst, send.at[k], recv.at[k], device)

        self.direct = [
            move(0, shard, region(p.x, 0, SHARD), p.right),
            move(1, shard, region(p.x, 0, SHARD), p.left),
        ]
        from_left = region(p.xl, 0, HALF)
        from_right = region(p.xr, HALF, HALF)
        self.forward = [
            move(2, from_left, from_left, p.right),
            move(3, from_right, from_right, p.left),
        ]

    def start(self):
        for c in self.direct:
            c.start()

    def relay(self):
        for k in range(2):
            self.direct[k].wait_recv()
            self.forward[k].start()

    def arrived(self):
        for c in self.forward:
            c.wait_recv()

    def finish(self):
        for c in self.direct + self.forward:
            c.wait_send()


class Scatter:
    def __init__(self, place, partial, landing, send, recv, first=0, height=SHARD):
        p = self.p = place
        half = height // 2
        self.partial, self.landing, self.first, self.height = partial, landing, first, height

        def region(x, part):
            return partial.at[rows(x * SHARD + first + part * half, half, 32)]

        def move(k, src, device):
            return remote(src, landing.at[k], send.at[k], recv.at[k], device)

        self.far = [move(0, region(p.x2, 0), p.right), move(1, region(p.x2, 1), p.left)]
        self.near = [move(2, region(p.xr, 1), p.right), move(3, region(p.xl, 0), p.left)]
        self.summed = [move(4, region(p.xr, 0), p.right), move(5, region(p.xl, 1), p.left)]

    def relay(self):
        p, half = self.p, self.height // 2
        for k, x, part in ((0, p.xr, 0), (1, p.xl, 1)):
            self.far[k].wait_recv()
            where = rows(x * SHARD + self.first + part * half, half, 32)
            self.partial[where, :] = (
                self.partial[where, :].astype(F32) + self.landing[k].astype(F32)
            ).astype(BF16)
            self.summed[k].start()

    def result(self, part, columns=slice(None)):
        p, half = self.p, self.height // 2
        own = self.partial[rows(p.x * SHARD + self.first + part * half, half, 32), columns]
        one, two = ((4, 3), (2, 5))[part]
        return (
            own.astype(F32)
            + self.landing[one, :, columns].astype(F32)
            + self.landing[two, :, columns].astype(F32)
        )

    def arrived(self):
        for c in self.near + self.summed:
            c.wait_recv()

    def finish(self):
        for c in self.far + self.near + self.summed:
            c.wait_send()


GROUP = 8
BLOCK = GROUP * CAP


def flatten(slots):
    return slots.astype(F32).reshape(BLOCK, MODEL_WIDTH).astype(BF16)


def unflatten(values):
    return values.reshape(GROUP, CAP, MODEL_WIDTH).astype(BF16)


def expert_kernel(
    n2, posm, wgate, wup, wdown, dy,
    dr_in, y_out, g_gate, g_up, g_down,
    sendbuf, landing, ybuf, rflat, dyflat, wgu, wd, hid, gab, dab, part_down, part_gu, land_down, land_gu,
    gs, gr, ns, nr, bs, br, ss, sr, ls,
):
    p = Place()
    peers = p.peers()
    sources = [p.peer(tuple((-v) % m for v, m in zip(o, (4, 4, 2)))) for o in OFFSETS]
    barrier = greet([p.left, p.right] + [(p.x, t) for t in peers])
    load_dy = pltpu.make_async_copy(dy, ybuf, ls.at[0])
    load_dy.start()

    def columns(full, first):
        return lambda x, start, count: full.at[
            rows(x * SHARD + start, count, 32), pl.ds(first, FF)
        ]

    mine = [
        pltpu.make_async_copy(w, f(p.x, 0, SHARD), ls.at[1 + k])
        for k, (w, f) in enumerate(
            [(wgate, columns(wgu, 0)), (wup, columns(wgu, FF)), (wdown, columns(wd, 0))]
        )
    ]
    for c in mine:
        c.start()

    @pl.loop(0, EXPERTS // 4)
    def _(i):
        hot = jnp.concatenate(slot_rows(posm, i * 4, 4), axis=0).astype(BF16)
        sendbuf[pl.ds(i * 4, 4)] = mm(hot, n2[...]).reshape(4, CAP, MODEL_WIDTH).astype(BF16)

    pl.semaphore_wait(barrier, len(peers) + 2)
    ggate = GatherOwn(p, wgate, columns(wgu, 0), gs.at[0], gr.at[0])
    gup = GatherOwn(p, wup, columns(wgu, FF), gs.at[1], gr.at[1])
    gdown = GatherOwn(p, wdown, columns(wd, 0), gs.at[2], gr.at[2])
    ggate.start()
    gup.start()
    sends = [
        remote(sendbuf.at[t], landing.at[k], ns.at[k], nr.at[k], (p.x, t))
        for k, t in enumerate(peers)
    ]
    for c in sends:
        c.start()
    own_rows = pltpu.make_async_copy(sendbuf.at[p.e], landing.at[31], ls.at[4])
    own_rows.start()

    load_dy.wait()

    @pl.loop(0, 4)
    def _(i):
        dyflat[rows(i * BLOCK, BLOCK), :] = flatten(ybuf[pl.ds(i * GROUP, GROUP)])

    ggate.relay()
    gup.relay()
    gdown.start()
    for c in mine:
        c.wait()
    ggate.arrived()
    gup.arrived()

    for i in range(4):
        for c in sends[i * GROUP : (i + 1) * GROUP]:
            c.wait_recv()
        if i == 3:
            own_rows.wait()
        cut = slice(i * BLOCK, (i + 1) * BLOCK)
        rflat[cut, :] = flatten(landing[i * GROUP : (i + 1) * GROUP])
        ab = mm(rflat[cut, :], wgu[...])
        value, slope = gelu_parts(ab[:, :FF])
        b = ab[:, FF:]
        hid[cut, :] = (value * b).astype(BF16)
        gab[cut, :FF] = (slope * b).astype(BF16)
        gab[cut, FF:] = value.astype(BF16)

    sdown = Scatter(p, part_down, land_down, ss.at[0], sr.at[0])
    sgu = Scatter(p, part_gu, land_gu, ss.at[1], sr.at[1])

    def down_block(x):
        where = rows(x * SHARD, SHARD, 128)
        part_down[where, :] = mm(dyflat[:, where], hid[...], 0, 0).astype(BF16)

    down_block(p.x2)
    for c in sdown.far:
        c.start()
    gdown.relay()
    down_block(p.xr)
    sdown.near[0].start()
    down_block(p.xl)
    sdown.near[1].start()
    down_block(p.x)
    gdown.arrived()

    for c in sends:
        c.wait_send()
    backs = []
    for i in range(4):
        cut = slice(i * BLOCK, (i + 1) * BLOCK)
        dh = mm(dyflat[cut, :], wd[...])
        dab[cut, :FF] = (dh * gab[cut, :FF].astype(F32)).astype(BF16)
        dab[cut, FF:] = (dh * gab[cut, FF:].astype(F32)).astype(BF16)
        sendbuf[i * GROUP : (i + 1) * GROUP] = unflatten(mm(dab[cut, :], wgu[...], 1, 1))
        for k in range(i * GROUP, min((i + 1) * GROUP, 31)):
            c = remote(sendbuf.at[k], dr_in.at[p.e], bs.at[k], br.at[k], (p.x, sources[k]))
            c.start()
            backs.append(c)
        if i == 1:
            sdown.relay()
    own_back = pltpu.make_async_copy(sendbuf.at[31], dr_in.at[p.e], ls.at[5])
    own_back.start()

    def gu_block(x):
        where = rows(x * SHARD, SHARD, 128)
        part_gu[where, :] = mm(rflat[:, where], dab[...], 0, 0).astype(BF16)

    gu_block(p.x2)
    for c in sgu.far:
        c.start()
    gu_block(p.xr)
    sgu.near[0].start()
    gu_block(p.xl)
    sgu.near[1].start()
    gu_block(p.x)

    for i in range(4):
        cut = slice(i * BLOCK, (i + 1) * BLOCK)
        ybuf[i * GROUP : (i + 1) * GROUP] = unflatten(mm(hid[cut, :], wd[...], 1, 1))
    keep_y = pltpu.make_async_copy(ybuf, y_out, ls.at[6])
    keep_y.start()

    sdown.arrived()
    for part in range(2):
        g_down[part * HALF : (part + 1) * HALF, :] = sdown.result(part)
    sgu.relay()
    sgu.arrived()
    for part in range(2):
        cut = slice(part * HALF, (part + 1) * HALF)
        g_gate[cut, :] = sgu.result(part, slice(0, FF))
        g_up[cut, :] = sgu.result(part, slice(FF, 2 * FF))

    for c in backs:
        c.wait()
    own_back.wait()
    keep_y.wait()
    for g in (ggate, gup, gdown, sdown, sgu):
        g.finish()


def experts(n2, posm, wgate, wup, wdown, dy):
    D = MODEL_WIDTH

    def arr(shape, dtype=BF16):
        return jax.ShapeDtypeStruct(shape, dtype)

    vm = pl.BlockSpec(memory_space=VMEM)
    hb = pl.BlockSpec(memory_space=ANY)
    sem = pltpu.SemaphoreType.DMA
    N = EXPERTS * CAP
    return pl.pallas_call(
        expert_kernel,
        out_shape=[
            arr((EXPERTS, CAP, D)), arr((EXPERTS, CAP, D)),
            arr((SHARD, FF), F32), arr((SHARD, FF), F32), arr((SHARD, FF), F32),
        ],
        in_specs=[vm] * 5 + [hb],
        out_specs=[hb, hb, vm, vm, vm],
        scratch_shapes=[
            VMEM((EXPERTS, CAP, D), BF16),
            VMEM((EXPERTS, CAP, D), BF16),
            VMEM((EXPERTS, CAP, D), BF16),
            VMEM((N, D), BF16),
            VMEM((N, D), BF16),
            VMEM((D, 2 * FF), BF16),
            VMEM((D, FF), BF16),
            VMEM((N, FF), BF16),
            VMEM((N, 2 * FF), BF16),
            VMEM((N, 2 * FF), BF16),
            VMEM((D, FF), BF16),
            VMEM((D, 2 * FF), BF16),
            VMEM((6, HALF, FF), BF16),
            VMEM((6, HALF, 2 * FF), BF16),
            sem((3, 4)),
            sem((3, 4)),
            sem((31,)),
            sem((31,)),
            sem((31,)),
            sem((31,)),
            sem((2, 6)),
            sem((2, 6)),
            sem((7,)),
        ],
        compiler_params=pltpu.CompilerParams(
            collective_id=1, has_side_effects=True, vmem_limit_bytes=LIMIT
        ),
        name="experts",
    )(n2, posm, wgate, wup, wdown, dy)


class PairSum:
    def __init__(self, place, partial, landing, send, recv):
        p = place
        self.order = [p.x2, p.xr, p.xl, p.x]
        self.partial, self.landing = partial, landing
        self.half = p.core * HALF
        self.moves = [
            remote(
                partial.at[rows(x * SHARD + HALF - self.half, HALF, 32)],
                landing.at[i],
                send.at[i],
                recv.at[i],
                p.sibling,
            )
            for i, x in enumerate(self.order)
        ]

    def add(self, i):
        self.moves[i].wait_recv()
        where = rows(self.order[i] * SHARD + self.half, HALF, 32)
        self.partial[where, :] = (
            self.partial[where, :].astype(F32) + self.landing[i].astype(F32)
        ).astype(BF16)

    def finish(self):
        for c in self.moves:
            c.wait_send()


class PlaneSum:
    def __init__(self, place, current, piece, out, land_a, land_b, width, z_first, send, recv):
        p = self.p = place
        self.current, self.piece, self.out = current, piece, out
        self.land_a, self.land_b = land_a, land_b
        w = self.w = width // 4
        t = HALF // 4
        a, b = (p.z, p.y) if z_first else (p.y, p.z)
        self.a, self.b = a, b

        def along_a(d):
            return (p.x, p.peer((d, 0, 0) if z_first else (0, d, 0)))

        def along_b(d):
            return (p.x, p.peer((0, d, 0) if z_first else (d, 0, 0)))

        def cut(i):
            return pl.ds(pl.multiple_of(i * w, 128), w)

        self.cut_a = cut(a)
        self.rows_b = rows(b * t, t)
        base = p.core * HALF
        self.mine = (rows(base + b * t, t), cut(a))
        spot = out.at[rows(base + b * t, t), cut(a)]
        strip = out.at[rows(base, HALF, 32), cut(a)]
        whole = out.at[rows(base, HALF, 32)]
        steps = (1, 2, 3)
        self.step_a = [
            remote(
                current.at[:, cut(lax.rem(a + d, 4))],
                land_a.at[d - 1],
                send.at[d - 1],
                recv.at[d - 1],
                along_a(d),
            )
            for d in steps
        ]
        self.step_b = [
            remote(
                piece.at[rows(lax.rem(b + d, 4) * t, t)],
                land_b.at[d - 1],
                send.at[2 + d],
                recv.at[2 + d],
                along_b(d),
            )
            for d in steps
        ]
        self.back_b = [remote(spot, spot, send.at[5 + d], recv.at[5 + d], along_b(d)) for d in steps]
        self.back_a = [
            remote(strip, strip, send.at[8 + d], recv.at[8 + d], along_a(d)) for d in steps
        ]
        self.pass_on = [remote(whole, whole, send.at[12], recv.at[12], p.sibling)]

    def start_a(self, scatter):
        part = HALF // 2
        scatter.arrived()
        for k in range(2):
            self.current[k * part : (k + 1) * part, :] = scatter.result(k).astype(BF16)
        for c in self.step_a:
            c.start()

    def start_b(self):
        for c in self.step_a:
            c.wait_recv()
        total = self.current[:, self.cut_a].astype(F32)
        for k in range(3):
            total += self.land_a[k].astype(F32)
        self.piece[...] = total.astype(BF16)
        for c in self.step_b:
            c.start()

    def start_back_b(self):
        for c in self.step_b:
            c.wait_recv()
        total = self.piece[self.rows_b, :].astype(F32)
        for k in range(3):
            total += self.land_b[k].astype(F32)
        self.out[self.mine] = total.astype(BF16)
        for c in self.back_b:
            c.start()

    def start_back_a(self):
        for c in self.back_b:
            c.wait_recv()
        for c in self.back_a:
            c.start()

    def start_pass(self):
        for c in self.back_a:
            c.wait_recv()
        for c in self.pass_on:
            c.start()

    def finish(self):
        for c in self.pass_on:
            c.wait()
        for c in self.step_a + self.step_b + self.back_b + self.back_a:
            c.wait_send()


def gain_row(small_all, row):
    return jnp.concatenate(
        [small_all[s, row : row + 1, :].astype(F32) for s in range(4)], axis=1
    )


def back_kernel(
    tokens, cotangent, posm, share, small_all, n1, q, kv, o, r, cosine, sine,
    dr_rows, y_rows, wq, wkv, wo,
    mixed, g_tokens, out_o, out_q, out_kv, out_small,
    drv, y_in, wqv, wkvv, wov, acc, acc2, da, do, dqp, dkvp, dgate,
    part_o, part_q, part_kv, pair_o, pair_q, pair_kv, land_o, land_q, land_kv,
    cur_o, cur_q, cur_kv, pc_o, pc_q, pc_kv, la_o, la_q, la_kv, lb_o, lb_q, lb_kv,
    sm_part, sm_x, sm_z, sm_y, sm_c,
    ys, yr, ps, pr, ss, sr, ts, tr, ms, mr, ls,
):
    p = Place()
    peers = p.peers()
    sources = [p.peer(tuple((-v) % m for v, m in zip(o_, (4, 4, 2)))) for o_ in OFFSETS]
    barrier = greet([p.left, p.right, p.across] + [(p.x, t) for t in peers])
    loads = [
        pltpu.make_async_copy(s, d, ls.at[k])
        for k, (s, d) in enumerate([(dr_rows, drv), (wo, wov), (wq, wqv), (wkv, wkvv)])
    ]
    for c in loads:
        c.start()
    pl.semaphore_wait(barrier, len(peers) + 3)
    sends = [
        remote(y_rows.at[k], y_in.at[p.e], ys.at[k], yr.at[k], (p.x, sources[k]))
        for k in range(31)
    ]
    for c in sends:
        c.start()
    own_y = pltpu.make_async_copy(y_rows.at[31], y_in.at[p.e], ls.at[4])
    own_y.start()

    loads[0].wait()
    for i in range(4):
        hot = jnp.concatenate(slot_rows(posm, i * GROUP, GROUP), axis=0).astype(BF16)
        term = mm(hot, flatten(drv[i * GROUP : (i + 1) * GROUP]), 0, 0)
        if i == 0:
            acc[...] = term
        else:
            acc[...] += term
    back, g_two = norm_back(r[...], gain_row(small_all, 33), acc[...])
    dr = cotangent[...].astype(F32) + back
    g_tokens[...] = dr
    da[...] = dr.astype(BF16)

    names = ((part_o, pair_o, land_o), (part_q, pair_q, land_q), (part_kv, pair_kv, land_kv))
    pairs = [PairSum(p, a, b, ps.at[k], pr.at[k]) for k, (a, b, _) in enumerate(names)]
    scatters = [
        Scatter(p, a, c, ss.at[k], sr.at[k], p.core * HALF, HALF)
        for k, (a, _, c) in enumerate(names)
    ]

    def blocks(k, left, right):
        for i, x in enumerate(pairs[k].order):
            where = rows(x * SHARD, SHARD, 128)
            names[k][0][where, :] = mm(left[:, where], right[...], 0, 0).astype(BF16)
            pairs[k].moves[i].start()

    def sum_pairs(k):
        pairs[k].add(0)
        for c in scatters[k].far:
            c.start()
        pairs[k].add(1)
        scatters[k].near[0].start()
        pairs[k].add(2)
        scatters[k].near[1].start()
        pairs[k].add(3)

    blocks(0, o, da)
    loads[1].wait()
    do[...] = mm(da[...], wov[...], 1, 1).astype(BF16)
    sum_pairs(0)

    cos = cosine[...]
    sin = sine[...]
    causal = causal_mask()
    group = QUERY_HEADS // KEY_VALUE_HEADS
    for c in range(KEY_VALUE_HEADS):
        k_cut = slice(c * HEAD_SIZE, (c + 1) * HEAD_SIZE)
        v_cut = slice(KV + c * HEAD_SIZE, KV + (c + 1) * HEAD_SIZE)
        dk = dv = None
        for h in range(c * group, (c + 1) * group):
            cut = slice(h * HEAD_SIZE, (h + 1) * HEAD_SIZE)
            soft = softmax_parts(q[:, cut], kv[:, k_cut], causal)
            dp = mm(do[:, cut], kv[:, v_cut], 1, 1)
            ds = (soft * (dp - jnp.sum(soft * dp, axis=-1, keepdims=True))).astype(BF16)
            dqp[:, cut] = turn_back(mm(ds, kv[:, k_cut]) * SCALE, cos, sin).astype(BF16)
            k_term = mm(ds, q[:, cut], 0, 0)
            v_term = mm(soft.astype(BF16), do[:, cut], 0, 0)
            dk = k_term if dk is None else dk + k_term
            dv = v_term if dv is None else dv + v_term
        dkvp[:, k_cut] = turn_back(dk * SCALE, cos, sin).astype(BF16)
        dkvp[:, v_cut] = dv.astype(BF16)
        if c == 0:
            scatters[0].relay()

    blocks(1, n1, dqp)
    blocks(2, n1, dkvp)
    sum_pairs(1)
    sum_pairs(2)

    loads[2].wait()
    loads[3].wait()
    dn1 = mm(dqp[...], wqv[...], 1, 1) + mm(dkvp[...], wkvv[...], 1, 1)
    back, g_one = norm_back(tokens[...].astype(F32), gain_row(small_all, 32), dn1)
    g_tokens[...] += back

    work = (
        (cur_o, pc_o, out_o, la_o, lb_o, MODEL_WIDTH, True),
        (cur_q, pc_q, out_q, la_q, lb_q, MODEL_WIDTH, False),
        (cur_kv, pc_kv, out_kv, la_kv, lb_kv, 2 * KV, True),
    )
    planes = [PlaneSum(p, *w, ts.at[k], tr.at[k]) for k, w in enumerate(work)]
    planes[0].start_a(scatters[0])
    scatters[1].relay()
    scatters[2].relay()

    for c in sends:
        c.wait_recv()
    own_y.wait()
    for i in range(4):
        hot = slot_rows(posm, i * GROUP, GROUP)
        weighted = jnp.concatenate(
            [b * share[i * GROUP + j : i * GROUP + j + 1, :] for j, b in enumerate(hot)], axis=0
        )
        high = weighted.astype(BF16)
        low = (weighted - high.astype(F32)).astype(BF16)
        y_f32 = y_in[i * GROUP : (i + 1) * GROUP].astype(F32).reshape(BLOCK, MODEL_WIDTH)
        y_now = y_f32.astype(BF16)
        term = mm(high, y_now, 0, 0) + mm(low, y_now, 0, 0)
        if i == 0:
            acc2[...] = r[...] + term
        else:
            acc2[...] += term
        picked = mm(jnp.concatenate(hot, axis=0).astype(BF16), cotangent[...])
        dslot = jnp.sum(picked * y_f32, axis=-1, keepdims=True)
        for j, b in enumerate(hot):
            dgate[i * GROUP + j : i * GROUP + j + 1, :] = jnp.sum(
                b * dslot[j * CAP : (j + 1) * CAP], axis=0, keepdims=True
            )
    mixed[...] = acc2[...].astype(BF16)
    gates = share[...]
    dlogits = gates * (dgate[...] - jnp.sum(gates * dgate[...], axis=0, keepdims=True))
    dlogits = jnp.where(posm[...] >= 0.0, dlogits, 0.0).astype(BF16)
    g_router = mm(dlogits, tokens[...])
    for s in range(4):
        cut = slice(s * SHARD, (s + 1) * SHARD)
        g_tokens[:, cut] += mm(dlogits, small_all[s, 0:32, :], 0, 0)
        sm_part[s] = jnp.concatenate(
            [g_router[:, cut], g_one[:, cut], g_two[:, cut], jnp.zeros((14, SHARD), F32)], axis=0
        ).astype(BF16)

    small_x = [
        remote(sm_part.at[x], sm_x.at[k], ms.at[k], mr.at[k], (x, p.e))
        for k, x in enumerate([p.xr, p.xl, p.x2])
    ]
    small_z = [
        remote(sm_z.at[p.z], sm_z.at[p.z], ms.at[2 + d], mr.at[2 + d], (p.x, p.peer((d, 0, 0))))
        for d in (1, 2, 3)
    ]
    small_y = [
        remote(sm_y.at[p.y], sm_y.at[p.y], ms.at[5 + d], mr.at[5 + d], (p.x, p.peer((0, d, 0))))
        for d in (1, 2, 3)
    ]
    small_c = [remote(sm_c.at[p.core], sm_c.at[p.core], ms.at[9], mr.at[9], p.sibling)]

    def total(ref, count):
        value = ref[0].astype(F32)
        for k in range(1, count):
            value += ref[k].astype(F32)
        return value

    for c in small_x:
        c.start()
    planes[1].start_a(scatters[1])
    planes[2].start_a(scatters[2])
    planes[0].start_b()
    for c in small_x:
        c.wait_recv()
    sm_z[p.z] = (sm_part[p.x].astype(F32) + total(sm_x, 3)).astype(BF16)
    for c in small_z:
        c.start()
    planes[0].start_back_b()
    planes[1].start_b()
    planes[2].start_b()
    for c in small_z:
        c.wait_recv()
    sm_y[p.y] = total(sm_z, 4).astype(BF16)
    for c in small_y:
        c.start()
    planes[0].start_back_a()
    planes[1].start_back_b()
    planes[2].start_back_b()
    for c in small_y:
        c.wait_recv()
    sm_c[p.core] = total(sm_y, 4).astype(BF16)
    for c in small_c:
        c.start()
    planes[0].start_pass()
    planes[1].start_back_a()
    planes[2].start_back_a()
    for c in small_c:
        c.wait_recv()
    out_small[...] = total(sm_c, 2)
    planes[1].start_pass()
    planes[2].start_pass()

    for c in sends + small_x + small_z + small_y + small_c:
        c.wait_send()
    for g in pairs + scatters + planes:
        g.finish()


def back(tokens, cotangent, posm, share, small_all, n1, q, kv, o, r, dr_rows, y_rows, wq, wkv, wo):
    D = MODEL_WIDTH
    cosine, sine = rope_tables()

    def arr(shape, dtype=BF16):
        return jax.ShapeDtypeStruct(shape, dtype)

    vm = pl.BlockSpec(memory_space=VMEM)
    hb = pl.BlockSpec(memory_space=ANY)
    sem = pltpu.SemaphoreType.DMA
    widths = (D, D, 2 * KV)
    return pl.pallas_call(
        back_kernel,
        out_shape=[
            arr((SEQ, D)), arr((SEQ, D), F32), arr((SHARD, D)), arr((SHARD, D)), arr((SHARD, 2 * KV)),
            arr((48, SHARD), F32),
        ],
        in_specs=[vm] * 12 + [hb] * 5,
        out_specs=[vm] * 6,
        scratch_shapes=[
            VMEM((EXPERTS, CAP, D), BF16),
            VMEM((EXPERTS, CAP, D), BF16),
            VMEM((D, D), BF16),
            VMEM((D, 2 * KV), BF16),
            VMEM((D, D), BF16),
            VMEM((SEQ, D), F32),
            VMEM((SEQ, D), F32),
            VMEM((SEQ, D), BF16),
            VMEM((SEQ, D), BF16),
            VMEM((SEQ, D), BF16),
            VMEM((SEQ, 2 * KV), BF16),
            VMEM((EXPERTS, SEQ), F32),
            *[VMEM((D, w), BF16) for w in widths],
            *[VMEM((4, HALF, w), BF16) for w in widths],
            *[VMEM((6, HALF // 2, w), BF16) for w in widths],
            *[VMEM((HALF, w), BF16) for w in widths],
            *[VMEM((HALF, w // 4), BF16) for w in widths],
            *[VMEM((3, HALF, w // 4), BF16) for w in widths],
            *[VMEM((3, HALF // 4, w // 4), BF16) for w in widths],
            VMEM((4, 48, SHARD), BF16),
            VMEM((3, 48, SHARD), BF16),
            VMEM((4, 48, SHARD), BF16),
            VMEM((4, 48, SHARD), BF16),
            VMEM((2, 48, SHARD), BF16),
            sem((31,)),
            sem((31,)),
            sem((3, 4)),
            sem((3, 4)),
            sem((3, 6)),
            sem((3, 6)),
            sem((3, 13)),
            sem((3, 13)),
            sem((10,)),
            sem((10,)),
            sem((5,)),
        ],
        compiler_params=pltpu.CompilerParams(
            collective_id=2, has_side_effects=True, vmem_limit_bytes=LIMIT
        ),
        name="back",
    )(
        tokens, cotangent, posm, share, small_all, n1, q, kv, o, r,
        jnp.asarray(cosine), jnp.asarray(sine), dr_rows, y_rows, wq, wkv, wo,
    )


def pack_small(w_router, norm_one, norm_two):
    return jnp.concatenate(
        [w_router.T, norm_one[None], norm_two[None], jnp.zeros((14, SHARD), BF16)], axis=0
    )


def shards(
    tokens, routes, w_query, key_matrix, value_matrix, w_output, norm_one, norm_two,
    w_router, w_gate, w_up, w_down, cotangent,
):
    small = pack_small(w_router, norm_one, norm_two)
    wkv = jnp.concatenate([key_matrix, value_matrix], axis=1)
    (dy, fq, fkv, fo, small_all, posm, share, n1, q, kv, o, r, n2) = front(
        tokens, cotangent, routes.T, small, w_query, wkv, w_output
    )
    dr_rows, y_rows, g_gate, g_up, g_down = experts(n2, posm, w_gate[0], w_up[0], w_down[0], dy)
    mixed, g_tokens, g_o, g_q, g_kv, g_small = back(
        tokens, cotangent, posm, share, small_all, n1, q, kv, o, r, dr_rows, y_rows, fq, fkv, fo
    )
    return (
        mixed,
        g_tokens,
        g_q.astype(F32),
        g_kv[:, :KV].astype(F32),
        g_kv[:, KV:].astype(F32),
        g_o.astype(F32),
        g_small[32],
        g_small[33],
        g_small[:32].T,
        g_gate[None],
        g_up[None],
        g_down[None],
    )


def solution(mesh):
    rows_split = P(("dp", "expert"), None)
    flat = P("dp", None)
    vector = P("dp")
    owned = P("expert", "dp", None)
    return jax.shard_map(
        shards,
        mesh=mesh,
        in_specs=(
            rows_split, rows_split, flat, flat, flat, flat, vector, vector, flat, owned, owned, owned,
            rows_split,
        ),
        out_specs=(
            rows_split, rows_split, flat, flat, flat, flat, vector, vector, flat, owned, owned, owned,
        ),
        check_vma=False,
    )
```

```python
import functools
import itertools

import jax
import jax.numpy as jnp
import numpy as np
from jax import lax
from jax.experimental import pallas as pl
from jax.experimental.pallas import tpu as pltpu
from jax.sharding import PartitionSpec as P

MODEL_WIDTH = 1536
QUERY_HEADS = 12
KEY_VALUE_HEADS = 2
HEAD_SIZE = 128
TOPK = 4
SEQ = 256
EXPERTS = 32
CAP = 40
FF = 768
KV = KEY_VALUE_HEADS * HEAD_SIZE
SHARD = MODEL_WIDTH // 4
HALF = SHARD // 2
QUARTER = HALF // 2
EPSILON = 1e-06
ROPE_BASE = 10000.0
SCALE = HEAD_SIZE ** (-0.5)
MESH = pl.DeviceIdType.MESH
F32 = jnp.float32
BF16 = jnp.bfloat16
VMEM = pltpu.VMEM
ANY = pl.ANY
LIMIT = 60 * 1024 * 1024


def _offsets():
    def far(a):
        return min(a, 4 - a)

    every = [o for o in itertools.product(range(4), range(4), range(2)) if o != (0, 0, 0)]
    return sorted(every, key=lambda o: (far(o[0]) + far(o[1]), o))[::-1]


OFFSETS = _offsets()


def rope_tables():
    position = np.arange(SEQ, dtype=np.float32)
    frequency = (
        np.float32(ROPE_BASE) ** (-np.arange(64, dtype=np.float32) * np.float32(2.0 / HEAD_SIZE))
    ).astype(np.float32)
    angles = (position[:, None] * frequency[None, :]).astype(np.float32)
    cosine = np.cos(angles.astype(np.float64)).astype(np.float32)
    sine = np.sin(angles.astype(np.float64)).astype(np.float32)
    return (
        np.concatenate([cosine, cosine], axis=1),
        np.concatenate([-sine, sine], axis=1),
    )


def mm(left, right, left_dim=1, right_dim=0):
    return lax.dot_general(
        left, right, (((left_dim,), (right_dim,)), ((), ())), preferred_element_type=F32
    )


class Place:
    def __init__(self):
        self.x = lax.axis_index("dp")
        self.e = lax.axis_index("expert")
        self.core = lax.rem(self.e, 2)
        self.y = lax.rem(self.e // 2, 4)
        self.z = self.e // 8
        self.xl = lax.rem(self.x + 3, 4)
        self.xr = lax.rem(self.x + 1, 4)
        self.x2 = lax.rem(self.x + 2, 4)
        self.left = (self.xl, self.e)
        self.right = (self.xr, self.e)
        self.across = (self.x2, self.e)
        self.sibling = (self.x, self.e + 1 - 2 * self.core)

    def peer(self, offset):
        dz, dy, dc = offset
        return (
            lax.rem(self.z + dz, 4) * 8 + lax.rem(self.y + dy, 4) * 2 + lax.rem(self.core + dc, 2)
        )

    def peers(self):
        return [self.peer(o) for o in OFFSETS]


def greet(devices):
    barrier = pltpu.get_barrier_semaphore()
    for d in devices:
        pl.semaphore_signal(barrier, inc=1, device_id=d, device_id_type=MESH)
    return barrier


def remote(src, dst, send, recv, device):
    return pltpu.make_async_remote_copy(
        src_ref=src, dst_ref=dst, send_sem=send, recv_sem=recv, device_id=device, device_id_type=MESH
    )


def rows(start, count, align=16):
    return pl.ds(pl.multiple_of(start, align), count)


class Gather:
    def __init__(self, place, shard, region, send, recv):
        p = place
        half = p.core * HALF

        def move(k, src, dst, device):
            return remote(src, dst, send.at[k], recv.at[k], device)

        mine = shard.at[rows(half, HALF, 32)]
        self.direct = [
            move(0, mine, region(p.x, half, HALF), p.right),
            move(1, mine, region(p.x, half, HALF), p.left),
        ]
        from_left = region(p.xl, half, QUARTER)
        from_right = region(p.xr, half + QUARTER, QUARTER)
        self.forward = [
            move(2, from_left, from_left, p.right),
            move(3, from_right, from_right, p.left),
        ]
        whole_left = region(p.xl, half, HALF)
        whole_right = region(p.xr, half, HALF)
        far_one = region(p.x2, half, QUARTER)
        far_two = region(p.x2, half + QUARTER, QUARTER)
        self.near = [
            move(4, whole_left, whole_left, p.sibling),
            move(5, whole_right, whole_right, p.sibling),
        ]
        self.far = [
            move(6, far_one, far_one, p.sibling),
            move(7, far_two, far_two, p.sibling),
        ]

    def start(self):
        for c in self.direct:
            c.start()

    def relay(self):
        for k in range(2):
            self.direct[k].wait_recv()
            self.forward[k].start()
            self.near[k].start()

    def relay_far(self):
        for k in range(2):
            self.forward[k].wait_recv()
            self.far[k].start()

    def arrived_near(self):
        for c in self.near:
            c.wait_recv()

    def arrived_far(self):
        for c in self.far:
            c.wait_recv()

    def finish(self):
        for c in self.direct + self.forward + self.near + self.far:
            c.wait_send()


def slot_rows(posm_ref, first, count):
    slot = lax.broadcasted_iota(jnp.int32, (CAP, SEQ), 0).astype(F32)
    return [
        jnp.where(posm_ref[pl.ds(first + j, 1), :] == slot, 1.0, 0.0) for j in range(count)
    ]


def turn(values, cosine, sine):
    return values * cosine + pltpu.roll(values, 64, 1) * sine


def turn_back(values, cosine, sine):
    return values * cosine - pltpu.roll(values, 64, 1) * sine


def softmax_parts(q_head, k_head, causal):
    scores = mm(q_head, k_head, 1, 1) * SCALE
    scores = jnp.where(causal, scores, -jnp.inf)
    largest = jnp.max(scores, axis=-1, keepdims=True)
    exponent = jnp.exp(scores - largest)
    return exponent / jnp.sum(exponent, axis=-1, keepdims=True)


def causal_mask():
    row = lax.broadcasted_iota(jnp.int32, (SEQ, SEQ), 0)
    column = lax.broadcasted_iota(jnp.int32, (SEQ, SEQ), 1)
    return column <= row


def norm_back(v, gain, grad):
    scale = lax.rsqrt(jnp.mean(v * v, axis=-1, keepdims=True) + EPSILON)
    unit = v * scale
    w = grad * gain
    return (
        (w - unit * jnp.mean(w * unit, axis=-1, keepdims=True)) * scale,
        jnp.sum(grad * unit, axis=0, keepdims=True),
    )


def gelu_parts(a):
    inner = jnp.tanh(0.7978845608028654 * (a + 0.044715 * a * a * a))
    value = 0.5 * a * (1.0 + inner)
    slope = 0.5 * (1.0 + inner) + 0.5 * a * (1.0 - inner * inner) * 0.7978845608028654 * (
        1.0 + 3.0 * 0.044715 * a * a
    )
    return value, slope


class GatherOwn:
    def __init__(self, place, shard, region, send, recv):
        p = place

        def move(k, src, dst, device):
            return remote(src, dst, send.at[k], recv.at[k], device)

        self.direct = [
            move(0, shard, region(p.x, 0, SHARD), p.right),
            move(1, shard, region(p.x, 0, SHARD), p.left),
        ]
        from_left = region(p.xl, 0, HALF)
        from_right = region(p.xr, HALF, HALF)
        self.forward = [
            move(2, from_left, from_left, p.right),
            move(3, from_right, from_right, p.left),
        ]

    def start(self):
        for c in self.direct:
            c.start()

    def relay(self):
        for k in range(2):
            self.direct[k].wait_recv()
            self.forward[k].start()

    def arrived(self):
        for c in self.forward:
            c.wait_recv()

    def finish(self):
        for c in self.direct + self.forward:
            c.wait_send()


class Scatter:
    def __init__(self, place, partial, landing, send, recv, first=0, height=SHARD):
        p = self.p = place
        half = height // 2
        self.partial, self.landing, self.first, self.height = partial, landing, first, height

        def region(x, part):
            return partial.at[rows(x * SHARD + first + part * half, half, 32)]

        def move(k, src, device):
            return remote(src, landing.at[k], send.at[k], recv.at[k], device)

        self.far = [move(0, region(p.x2, 0), p.right), move(1, region(p.x2, 1), p.left)]
        self.near = [move(2, region(p.xr, 1), p.right), move(3, region(p.xl, 0), p.left)]
        self.summed = [move(4, region(p.xr, 0), p.right), move(5, region(p.xl, 1), p.left)]

    def relay(self):
        p, half = self.p, self.height // 2
        for k, x, part in ((0, p.xr, 0), (1, p.xl, 1)):
            self.far[k].wait_recv()
            where = rows(x * SHARD + self.first + part * half, half, 32)
            self.partial[where, :] = (
                self.partial[where, :].astype(F32) + self.landing[k].astype(F32)
            ).astype(BF16)
            self.summed[k].start()

    def result(self, part, columns=slice(None)):
        p, half = self.p, self.height // 2
        own = self.partial[rows(p.x * SHARD + self.first + part * half, half, 32), columns]
        one, two = ((4, 3), (2, 5))[part]
        return (
            own.astype(F32)
            + self.landing[one, :, columns].astype(F32)
            + self.landing[two, :, columns].astype(F32)
        )

    def arrived(self):
        for c in self.near + self.summed:
            c.wait_recv()

    def finish(self):
        for c in self.far + self.near + self.summed:
            c.wait_send()


GROUP = 8
BLOCK = GROUP * CAP


def flatten(slots):
    return slots.astype(F32).reshape(BLOCK, MODEL_WIDTH).astype(BF16)


def unflatten(values):
    return values.reshape(GROUP, CAP, MODEL_WIDTH).astype(BF16)


def forth_kernel(
    tokens, cotangent, routes, small, cosine, sine, wq, wk, wv, wo, wgate, wup, wdown,
    dy_in, dr_in, y_out, wq_full, wkv_full, wo_full,
    small_all, posm, share, n1, q, kv, o, r, g_gate, g_up, g_down,
    buf_a, buf_b, landing, dyflat, wqf, wkvf, wof, wgu, wd, hid, part_down, part_gu, land_down, land_gu,
    n2, qacc, kvacc,
    ag, ag_r, sg, sg_r, ds_, dr_, gs, gr, ns, nr, bs, br, ss, sr, ls,
):
    p = Place()
    peers = p.peers()
    sources = [p.peer(tuple((-v) % m for v, m in zip(o_, (4, 4, 2)))) for o_ in OFFSETS]
    barrier = greet([p.left, p.right, p.across] + [(p.x, t) for t in peers])

    def columns(full, first, count):
        return lambda x, start, height: full.at[
            rows(x * SHARD + start, height, 32), pl.ds(first, count)
        ]

    at_q = columns(wqf, 0, MODEL_WIDTH)
    at_k = columns(wkvf, 0, KV)
    at_v = columns(wkvf, KV, KV)
    at_o = columns(wof, 0, MODEL_WIDTH)
    at_gate = columns(wgu, 0, FF)
    at_up = columns(wgu, FF, FF)
    at_down = columns(wd, 0, FF)
    mine = [
        pltpu.make_async_copy(w, f(p.x, 0, SHARD), ls.at[k])
        for k, (w, f) in enumerate(
            [
                (wq, at_q), (wk, at_k), (wv, at_v), (wo, at_o),
                (wgate, at_gate), (wup, at_up), (wdown, at_down),
            ]
        )
    ]
    for c in mine:
        c.start()

    lane = lax.broadcasted_iota(jnp.int32, (EXPERTS, SEQ), 0)
    named = routes[0:1, :] == lane
    for j in range(1, TOPK):
        named = jnp.logical_or(named, routes[j : j + 1, :] == lane)
    earlier = (
        lax.broadcasted_iota(jnp.int32, (SEQ, SEQ), 0)
        < lax.broadcasted_iota(jnp.int32, (SEQ, SEQ), 1)
    ).astype(F32).astype(BF16)
    place_of = mm(named.astype(F32).astype(BF16), earlier)
    posm[...] = jnp.where(named, place_of, -1.0)

    small_all[p.x] = small[...]
    pl.semaphore_wait(barrier, len(peers) + 3)

    small_moves = [
        remote(small, small_all.at[p.x], sg.at[k], sg_r.at[k], d)
        for k, d in enumerate([p.right, p.left, p.across])
    ]
    for c in small_moves:
        c.start()
    gq, gk, gv, go = [
        Gather(p, w, f, ag.at[k], ag_r.at[k])
        for k, (w, f) in enumerate([(wq, at_q), (wk, at_k), (wv, at_v), (wo, at_o)])
    ]
    for g in (gq, gk, gv):
        g.start()

    x = tokens[...].astype(F32)
    unit = x * lax.rsqrt(jnp.mean(x * x, axis=-1, keepdims=True) + EPSILON)
    for c in small_moves:
        c.wait_recv()
    for s in range(4):
        cut = slice(s * SHARD, (s + 1) * SHARD)
        n1[:, cut] = (unit[:, cut] * small_all[s, 32:33, :].astype(F32)).astype(BF16)
    logits = mm(small_all[0, 0:32, :], tokens[:, 0:SHARD], 1, 1)
    for s in range(1, 4):
        logits += mm(small_all[s, 0:32, :], tokens[:, s * SHARD : (s + 1) * SHARD], 1, 1)
    top = jnp.max(jnp.where(named, logits, -jnp.inf), axis=0, keepdims=True)
    weight = jnp.where(named, jnp.exp(jnp.minimum(logits - top, 0.0)), 0.0)
    share[...] = weight / jnp.sum(weight, axis=0, keepdims=True)

    @pl.loop(0, EXPERTS // 4)
    def _(i):
        hot = slot_rows(posm, i * 4, 4)
        gain = jnp.concatenate(
            [
                jnp.sum(b * share[pl.ds(i * 4 + j, 1), :], axis=-1, keepdims=True)
                for j, b in enumerate(hot)
            ],
            axis=0,
        )
        picked = mm(jnp.concatenate(hot, axis=0).astype(BF16), cotangent[...])
        buf_a[pl.ds(i * 4, 4)] = (picked * gain).reshape(4, CAP, MODEL_WIDTH).astype(BF16)

    dy_sends = [
        remote(buf_a.at[t], dy_in.at[k], ds_.at[k], dr_.at[k], (p.x, t))
        for k, t in enumerate(peers)
    ]
    for c in dy_sends:
        c.start()
    own_dy = pltpu.make_async_copy(buf_a.at[p.e], dy_in.at[31], ls.at[7])
    own_dy.start()

    def part(x_index):
        return n1[:, rows(x_index * SHARD, SHARD, 128)]

    def block(full, x_index):
        return full[rows(x_index * SHARD, SHARD, 128), :]

    for c in mine[:3]:
        c.wait()
    qacc[...] = mm(part(p.x), block(wqf, p.x))
    kvacc[...] = mm(part(p.x), block(wkvf, p.x))
    for g in (gq, gk, gv):
        g.relay()
    go.start()
    for g in (gq, gk, gv):
        g.arrived_near()
    for s in (p.xl, p.xr):
        qacc[...] += mm(part(s), block(wqf, s))
        kvacc[...] += mm(part(s), block(wkvf, s))
    for g in (gq, gk, gv):
        g.relay_far()
    for g in (gq, gk, gv):
        g.arrived_far()
    qacc[...] += mm(part(p.x2), block(wqf, p.x2))
    kvacc[...] += mm(part(p.x2), block(wkvf, p.x2))
    keep = [
        pltpu.make_async_copy(f, out, ls.at[8 + k])
        for k, (f, out) in enumerate([(wqf, wq_full), (wkvf, wkv_full), (wof, wo_full)])
    ]
    keep[0].start()
    keep[1].start()

    cos = cosine[...]
    sin = sine[...]
    for h in range(KEY_VALUE_HEADS):
        cut = slice(h * HEAD_SIZE, (h + 1) * HEAD_SIZE)
        kv[:, cut] = turn(kvacc[:, cut], cos, sin).astype(BF16)
        cut = slice(KV + h * HEAD_SIZE, KV + (h + 1) * HEAD_SIZE)
        kv[:, cut] = kvacc[:, cut].astype(BF16)
    causal = causal_mask()
    for h in range(QUERY_HEADS):
        cut = slice(h * HEAD_SIZE, (h + 1) * HEAD_SIZE)
        c = h // (QUERY_HEADS // KEY_VALUE_HEADS)
        q_head = turn(qacc[:, cut], cos, sin).astype(BF16)
        q[:, cut] = q_head
        weights = softmax_parts(q_head, kv[:, c * HEAD_SIZE : (c + 1) * HEAD_SIZE], causal)
        o[:, cut] = mm(
            weights.astype(BF16), kv[:, KV + c * HEAD_SIZE : KV + (c + 1) * HEAD_SIZE]
        ).astype(BF16)

    def opart(x_index):
        return o[:, rows(x_index * SHARD, SHARD, 128)]

    for c in mine[3:]:
        c.wait()
    r[...] = tokens[...].astype(F32) + mm(opart(p.x), block(wof, p.x))
    go.relay()
    ggate = GatherOwn(p, wgate, at_gate, gs.at[0], gr.at[0])
    gup = GatherOwn(p, wup, at_up, gs.at[1], gr.at[1])
    gdown = GatherOwn(p, wdown, at_down, gs.at[2], gr.at[2])
    ggate.start()
    gup.start()
    go.arrived_near()
    for s in (p.xl, p.xr):
        r[...] += mm(opart(s), block(wof, s))
    go.relay_far()
    go.arrived_far()
    keep[2].start()
    residual = r[...] + mm(opart(p.x2), block(wof, p.x2))
    r[...] = residual
    unit = residual * lax.rsqrt(jnp.mean(residual * residual, axis=-1, keepdims=True) + EPSILON)
    for s in range(4):
        cut = slice(s * SHARD, (s + 1) * SHARD)
        n2[:, cut] = (unit[:, cut] * small_all[s, 33:34, :].astype(F32)).astype(BF16)

    @pl.loop(0, EXPERTS // 4)
    def _(i):
        hot = jnp.concatenate(slot_rows(posm, i * 4, 4), axis=0).astype(BF16)
        buf_b[pl.ds(i * 4, 4)] = mm(hot, n2[...]).reshape(4, CAP, MODEL_WIDTH).astype(BF16)

    sends = [
        remote(buf_b.at[t], landing.at[k], ns.at[k], nr.at[k], (p.x, t))
        for k, t in enumerate(peers)
    ]
    for c in sends:
        c.start()
    own_rows = pltpu.make_async_copy(buf_b.at[p.e], landing.at[31], ls.at[11])
    own_rows.start()

    ggate.relay()
    gup.relay()
    gdown.start()
    for c in dy_sends:
        c.wait()
    own_dy.wait()
    load_dy = pltpu.make_async_copy(dy_in, buf_a, ls.at[12])
    load_dy.start()
    for g in (gq, gk, gv, go):
        g.finish()
    for c in small_moves:
        c.wait_send()
    for c in keep:
        c.wait()
    rflat = wof
    dab = wqf
    load_dy.wait()

    @pl.loop(0, 4)
    def _(i):
        dyflat[rows(i * BLOCK, BLOCK), :] = flatten(buf_a[pl.ds(i * GROUP, GROUP)])

    ggate.arrived()
    gup.arrived()

    for i in range(4):
        if i == 3:
            gdown.relay()
            own_rows.wait()
        for c in sends[i * GROUP : (i + 1) * GROUP]:
            c.wait_recv()
        cut = slice(i * BLOCK, (i + 1) * BLOCK)
        rflat[cut, :] = flatten(landing[i * GROUP : (i + 1) * GROUP])
        ab = mm(rflat[cut, :], wgu[...])
        value, slope = gelu_parts(ab[:, :FF])
        b = ab[:, FF:]
        hid[cut, :] = (value * b).astype(BF16)
        dab[cut, :FF] = (slope * b).astype(BF16)
        dab[cut, FF:] = value.astype(BF16)

    sdown = Scatter(p, part_down, land_down, ss.at[0], sr.at[0])
    sgu = Scatter(p, part_gu, land_gu, ss.at[1], sr.at[1])

    def down_block(x):
        where = rows(x * SHARD, SHARD, 128)
        part_down[where, :] = mm(dyflat[:, where], hid[...], 0, 0).astype(BF16)

    down_block(p.x2)
    for c in sdown.far:
        c.start()
    down_block(p.xr)
    sdown.near[0].start()
    down_block(p.xl)
    sdown.near[1].start()
    down_block(p.x)
    gdown.arrived()

    backs = []
    for i in range(4):
        cut = slice(i * BLOCK, (i + 1) * BLOCK)
        dh = mm(dyflat[cut, :], wd[...])
        dab[cut, :FF] = (dh * dab[cut, :FF].astype(F32)).astype(BF16)
        dab[cut, FF:] = (dh * dab[cut, FF:].astype(F32)).astype(BF16)
        buf_a[i * GROUP : (i + 1) * GROUP] = unflatten(mm(dab[cut, :], wgu[...], 1, 1))
        for k in range(i * GROUP, min((i + 1) * GROUP, 31)):
            c = remote(buf_a.at[k], dr_in.at[p.e], bs.at[k], br.at[k], (p.x, sources[k]))
            c.start()
            backs.append(c)
        if i == 1:
            sdown.relay()
    own_back = pltpu.make_async_copy(buf_a.at[31], dr_in.at[p.e], ls.at[13])
    own_back.start()

    def gu_block(x):
        where = rows(x * SHARD, SHARD, 128)
        part_gu[where, :] = mm(rflat[0 : EXPERTS * CAP, where], dab[0 : EXPERTS * CAP, :], 0, 0).astype(
            BF16
        )

    gu_block(p.x2)
    for c in sgu.far:
        c.start()
    gu_block(p.xr)
    sgu.near[0].start()
    gu_block(p.xl)
    sgu.near[1].start()
    gu_block(p.x)

    for c in sends:
        c.wait_send()
    for i in range(4):
        cut = slice(i * BLOCK, (i + 1) * BLOCK)
        buf_b[i * GROUP : (i + 1) * GROUP] = unflatten(mm(hid[cut, :], wd[...], 1, 1))
    keep_y = pltpu.make_async_copy(buf_b, y_out, ls.at[14])
    keep_y.start()

    sdown.arrived()
    for half in range(2):
        g_down[half * HALF : (half + 1) * HALF, :] = sdown.result(half).astype(BF16)
    sgu.relay()
    sgu.arrived()
    for half in range(2):
        cut = slice(half * HALF, (half + 1) * HALF)
        g_gate[cut, :] = sgu.result(half, slice(0, FF)).astype(BF16)
        g_up[cut, :] = sgu.result(half, slice(FF, 2 * FF)).astype(BF16)

    for c in backs:
        c.wait()
    own_back.wait()
    keep_y.wait()
    for g in (ggate, gup, gdown, sdown, sgu):
        g.finish()


def forth(tokens, cotangent, routes, small, wq, wk, wv, wo, wgate, wup, wdown):
    cosine, sine = rope_tables()
    D = MODEL_WIDTH

    def arr(shape, dtype=BF16):
        return jax.ShapeDtypeStruct(shape, dtype)

    vm = pl.BlockSpec(memory_space=VMEM)
    hb = pl.BlockSpec(memory_space=ANY)
    sem = pltpu.SemaphoreType.DMA
    N = EXPERTS * CAP
    slots = (EXPERTS, CAP, D)
    return pl.pallas_call(
        forth_kernel,
        out_shape=[
            arr(slots), arr(slots), arr(slots), arr((D, D)), arr((D, 2 * KV)), arr((D, D)),
            arr((4, 48, SHARD)), arr((EXPERTS, SEQ), F32), arr((EXPERTS, SEQ), F32),
            arr((SEQ, D)), arr((SEQ, D)), arr((SEQ, 2 * KV)), arr((SEQ, D)), arr((SEQ, D), F32),
            arr((SHARD, FF)), arr((SHARD, FF)), arr((SHARD, FF)),
        ],
        in_specs=[vm] * 6 + [hb] * 7,
        out_specs=[hb] * 6 + [vm] * 11,
        scratch_shapes=[
            VMEM(slots, BF16),
            VMEM(slots, BF16),
            VMEM(slots, BF16),
            VMEM((N, D), BF16),
            VMEM((D, D), BF16),
            VMEM((D, 2 * KV), BF16),
            VMEM((D, D), BF16),
            VMEM((D, 2 * FF), BF16),
            VMEM((D, FF), BF16),
            VMEM((N, FF), BF16),
            VMEM((D, FF), BF16),
            VMEM((D, 2 * FF), BF16),
            VMEM((6, HALF, FF), BF16),
            VMEM((6, HALF, 2 * FF), BF16),
            VMEM((SEQ, D), BF16),
            VMEM((SEQ, D), F32),
            VMEM((SEQ, 2 * KV), F32),
            sem((4, 8)), sem((4, 8)), sem((3,)), sem((3,)), sem((31,)), sem((31,)),
            sem((3, 4)), sem((3, 4)), sem((31,)), sem((31,)), sem((31,)), sem((31,)),
            sem((2, 6)), sem((2, 6)), sem((15,)),
        ],
        compiler_params=pltpu.CompilerParams(
            collective_id=0, has_side_effects=True, vmem_limit_bytes=LIMIT
        ),
        name="forth",
    )(
        tokens, cotangent, routes, small, jnp.asarray(cosine), jnp.asarray(sine),
        wq, wk, wv, wo, wgate, wup, wdown,
    )


class PairSum:
    def __init__(self, place, partial, landing, send, recv):
        p = place
        self.order = [p.x2, p.xr, p.xl, p.x]
        self.partial, self.landing = partial, landing
        self.half = p.core * HALF
        self.moves = [
            remote(
                partial.at[rows(x * SHARD + HALF - self.half, HALF, 32)],
                landing.at[i],
                send.at[i],
                recv.at[i],
                p.sibling,
            )
            for i, x in enumerate(self.order)
        ]

    def add(self, i):
        self.moves[i].wait_recv()
        where = rows(self.order[i] * SHARD + self.half, HALF, 32)
        self.partial[where, :] = (
            self.partial[where, :].astype(F32) + self.landing[i].astype(F32)
        ).astype(BF16)

    def finish(self):
        for c in self.moves:
            c.wait_send()


class PlaneSum:
    def __init__(self, place, current, piece, out, land_a, land_b, width, z_first, send, recv):
        p = self.p = place
        self.current, self.piece, self.out = current, piece, out
        self.land_a, self.land_b = land_a, land_b
        w = self.w = width // 4
        t = HALF // 4
        a, b = (p.z, p.y) if z_first else (p.y, p.z)
        self.a, self.b = a, b

        def along_a(d):
            return (p.x, p.peer((d, 0, 0) if z_first else (0, d, 0)))

        def along_b(d):
            return (p.x, p.peer((0, d, 0) if z_first else (d, 0, 0)))

        def cut(i):
            return pl.ds(pl.multiple_of(i * w, 128), w)

        self.cut_a = cut(a)
        self.rows_b = rows(b * t, t)
        base = p.core * HALF
        self.mine = (rows(base + b * t, t), cut(a))
        spot = out.at[rows(base + b * t, t), cut(a)]
        strip = out.at[rows(base, HALF, 32), cut(a)]
        whole = out.at[rows(base, HALF, 32)]
        steps = (1, 2, 3)
        self.step_a = [
            remote(
                current.at[:, cut(lax.rem(a + d, 4))],
                land_a.at[d - 1],
                send.at[d - 1],
                recv.at[d - 1],
                along_a(d),
            )
            for d in steps
        ]
        self.step_b = [
            remote(
                piece.at[rows(lax.rem(b + d, 4) * t, t)],
                land_b.at[d - 1],
                send.at[2 + d],
                recv.at[2 + d],
                along_b(d),
            )
            for d in steps
        ]
        self.back_b = [remote(spot, spot, send.at[5 + d], recv.at[5 + d], along_b(d)) for d in steps]
        self.back_a = [
            remote(strip, strip, send.at[8 + d], recv.at[8 + d], along_a(d)) for d in steps
        ]
        self.pass_on = [remote(whole, whole, send.at[12], recv.at[12], p.sibling)]

    def start_a(self, scatter):
        part = HALF // 2
        scatter.arrived()
        for k in range(2):
            self.current[k * part : (k + 1) * part, :] = scatter.result(k).astype(BF16)
        for c in self.step_a:
            c.start()

    def start_b(self):
        for c in self.step_a:
            c.wait_recv()
        total = self.current[:, self.cut_a].astype(F32)
        for k in range(3):
            total += self.land_a[k].astype(F32)
        self.piece[...] = total.astype(BF16)
        for c in self.step_b:
            c.start()

    def start_back_b(self):
        for c in self.step_b:
            c.wait_recv()
        total = self.piece[self.rows_b, :].astype(F32)
        for k in range(3):
            total += self.land_b[k].astype(F32)
        self.out[self.mine] = total.astype(BF16)
        for c in self.back_b:
            c.start()

    def start_back_a(self):
        for c in self.back_b:
            c.wait_recv()
        for c in self.back_a:
            c.start()

    def start_pass(self):
        for c in self.back_a:
            c.wait_recv()
        for c in self.pass_on:
            c.start()

    def finish(self):
        for c in self.pass_on:
            c.wait()
        for c in self.step_a + self.step_b + self.back_b + self.back_a:
            c.wait_send()


def gain_row(small_all, row):
    return jnp.concatenate(
        [small_all[s, row : row + 1, :].astype(F32) for s in range(4)], axis=1
    )


def back_kernel(
    tokens, cotangent, posm, share, small_all, n1, q, kv, o, r, cosine, sine,
    dr_rows, y_rows, wq, wkv, wo,
    mixed, g_tokens, out_o, out_q, out_kv, out_small,
    drv, y_in, wqv, wkvv, wov, acc, acc2, da, do, dqp, dkvp, dgate,
    part_o, part_q, part_kv, pair_o, pair_q, pair_kv, land_o, land_q, land_kv,
    cur_o, cur_q, cur_kv, pc_o, pc_q, pc_kv, la_o, la_q, la_kv, lb_o, lb_q, lb_kv,
    sm_part, sm_x, sm_z, sm_y, sm_c,
    ys, yr, ps, pr, ss, sr, ts, tr, ms, mr, ls,
):
    p = Place()
    peers = p.peers()
    sources = [p.peer(tuple((-v) % m for v, m in zip(o_, (4, 4, 2)))) for o_ in OFFSETS]
    barrier = greet([p.left, p.right, p.across] + [(p.x, t) for t in peers])
    loads = [
        pltpu.make_async_copy(s, d, ls.at[k])
        for k, (s, d) in enumerate([(dr_rows, drv), (wo, wov), (wq, wqv), (wkv, wkvv)])
    ]
    for c in loads:
        c.start()
    pl.semaphore_wait(barrier, len(peers) + 3)
    sends = [
        remote(y_rows.at[k], y_in.at[p.e], ys.at[k], yr.at[k], (p.x, sources[k]))
        for k in range(31)
    ]
    for c in sends:
        c.start()
    own_y = pltpu.make_async_copy(y_rows.at[31], y_in.at[p.e], ls.at[4])
    own_y.start()

    loads[0].wait()
    for i in range(4):
        hot = jnp.concatenate(slot_rows(posm, i * GROUP, GROUP), axis=0).astype(BF16)
        term = mm(hot, flatten(drv[i * GROUP : (i + 1) * GROUP]), 0, 0)
        if i == 0:
            acc[...] = term
        else:
            acc[...] += term
    back, g_two = norm_back(r[...], gain_row(small_all, 33), acc[...])
    dr = cotangent[...].astype(F32) + back
    g_tokens[...] = dr
    da[...] = dr.astype(BF16)

    names = ((part_o, pair_o, land_o), (part_q, pair_q, land_q), (part_kv, pair_kv, land_kv))
    pairs = [PairSum(p, a, b, ps.at[k], pr.at[k]) for k, (a, b, _) in enumerate(names)]
    scatters = [
        Scatter(p, a, c, ss.at[k], sr.at[k], p.core * HALF, HALF)
        for k, (a, _, c) in enumerate(names)
    ]

    def blocks(k, left, right):
        for i, x in enumerate(pairs[k].order):
            where = rows(x * SHARD, SHARD, 128)
            names[k][0][where, :] = mm(left[:, where], right[...], 0, 0).astype(BF16)
            pairs[k].moves[i].start()

    def sum_pairs(k):
        pairs[k].add(0)
        for c in scatters[k].far:
            c.start()
        pairs[k].add(1)
        scatters[k].near[0].start()
        pairs[k].add(2)
        scatters[k].near[1].start()
        pairs[k].add(3)

    blocks(0, o, da)
    loads[1].wait()
    do[...] = mm(da[...], wov[...], 1, 1).astype(BF16)
    sum_pairs(0)

    cos = cosine[...]
    sin = sine[...]
    causal = causal_mask()
    group = QUERY_HEADS // KEY_VALUE_HEADS
    for c in range(KEY_VALUE_HEADS):
        k_cut = slice(c * HEAD_SIZE, (c + 1) * HEAD_SIZE)
        v_cut = slice(KV + c * HEAD_SIZE, KV + (c + 1) * HEAD_SIZE)
        dk = dv = None
        for h in range(c * group, (c + 1) * group):
            cut = slice(h * HEAD_SIZE, (h + 1) * HEAD_SIZE)
            soft = softmax_parts(q[:, cut], kv[:, k_cut], causal)
            dp = mm(do[:, cut], kv[:, v_cut], 1, 1)
            ds = (soft * (dp - jnp.sum(soft * dp, axis=-1, keepdims=True))).astype(BF16)
            dqp[:, cut] = turn_back(mm(ds, kv[:, k_cut]) * SCALE, cos, sin).astype(BF16)
            k_term = mm(ds, q[:, cut], 0, 0)
            v_term = mm(soft.astype(BF16), do[:, cut], 0, 0)
            dk = k_term if dk is None else dk + k_term
            dv = v_term if dv is None else dv + v_term
        dkvp[:, k_cut] = turn_back(dk * SCALE, cos, sin).astype(BF16)
        dkvp[:, v_cut] = dv.astype(BF16)
        if c == 0:
            scatters[0].relay()

    blocks(1, n1, dqp)
    blocks(2, n1, dkvp)
    sum_pairs(1)
    sum_pairs(2)

    loads[2].wait()
    loads[3].wait()
    dn1 = mm(dqp[...], wqv[...], 1, 1) + mm(dkvp[...], wkvv[...], 1, 1)
    back, g_one = norm_back(tokens[...].astype(F32), gain_row(small_all, 32), dn1)
    g_tokens[...] += back

    work = (
        (cur_o, pc_o, out_o, la_o, lb_o, MODEL_WIDTH, True),
        (cur_q, pc_q, out_q, la_q, lb_q, MODEL_WIDTH, False),
        (cur_kv, pc_kv, out_kv, la_kv, lb_kv, 2 * KV, True),
    )
    planes = [PlaneSum(p, *w, ts.at[k], tr.at[k]) for k, w in enumerate(work)]
    planes[0].start_a(scatters[0])
    scatters[1].relay()
    scatters[2].relay()

    def combine(i):
        hot = slot_rows(posm, i * GROUP, GROUP)
        weighted = jnp.concatenate(
            [b * share[i * GROUP + j : i * GROUP + j + 1, :] for j, b in enumerate(hot)], axis=0
        )
        high = weighted.astype(BF16)
        low = (weighted - high.astype(F32)).astype(BF16)
        y_f32 = y_in[i * GROUP : (i + 1) * GROUP].astype(F32).reshape(BLOCK, MODEL_WIDTH)
        y_now = y_f32.astype(BF16)
        term = mm(high, y_now, 0, 0) + mm(low, y_now, 0, 0)
        if i == 0:
            acc2[...] = r[...] + term
        else:
            acc2[...] += term
        picked = mm(jnp.concatenate(hot, axis=0).astype(BF16), cotangent[...])
        dslot = jnp.sum(picked * y_f32, axis=-1, keepdims=True)
        for j, b in enumerate(hot):
            dgate[i * GROUP + j : i * GROUP + j + 1, :] = jnp.sum(
                b * dslot[j * CAP : (j + 1) * CAP], axis=0, keepdims=True
            )

    def route_back():
        mixed[...] = acc2[...].astype(BF16)
        gates = share[...]
        dlogits = gates * (dgate[...] - jnp.sum(gates * dgate[...], axis=0, keepdims=True))
        dlogits = jnp.where(posm[...] >= 0.0, dlogits, 0.0).astype(BF16)
        g_router = mm(dlogits, tokens[...])
        for s in range(4):
            cut = slice(s * SHARD, (s + 1) * SHARD)
            g_tokens[:, cut] += mm(dlogits, small_all[s, 0:32, :], 0, 0)
            sm_part[s] = jnp.concatenate(
                [g_router[:, cut], g_one[:, cut], g_two[:, cut], jnp.zeros((14, SHARD), F32)],
                axis=0,
            ).astype(BF16)

    small_x = [
        remote(sm_part.at[x], sm_x.at[k], ms.at[k], mr.at[k], (x, p.e))
        for k, x in enumerate([p.xr, p.xl, p.x2])
    ]
    small_z = [
        remote(sm_z.at[p.z], sm_z.at[p.z], ms.at[2 + d], mr.at[2 + d], (p.x, p.peer((d, 0, 0))))
        for d in (1, 2, 3)
    ]
    small_y = [
        remote(sm_y.at[p.y], sm_y.at[p.y], ms.at[5 + d], mr.at[5 + d], (p.x, p.peer((0, d, 0))))
        for d in (1, 2, 3)
    ]
    small_c = [remote(sm_c.at[p.core], sm_c.at[p.core], ms.at[9], mr.at[9], p.sibling)]

    def total(ref, count):
        value = ref[0].astype(F32)
        for k in range(1, count):
            value += ref[k].astype(F32)
        return value

    for c in sends:
        c.wait_recv()
    own_y.wait()
    planes[0].start_b()
    combine(0)
    combine(1)
    planes[1].start_a(scatters[1])
    planes[2].start_a(scatters[2])
    combine(2)
    combine(3)
    planes[0].start_back_b()
    planes[1].start_b()
    planes[2].start_b()
    route_back()
    for c in small_x:
        c.start()
    planes[0].start_back_a()
    planes[1].start_back_b()
    planes[2].start_back_b()
    for c in small_x:
        c.wait_recv()
    sm_z[p.z] = (sm_part[p.x].astype(F32) + total(sm_x, 3)).astype(BF16)
    for c in small_z:
        c.start()
    planes[1].start_back_a()
    planes[2].start_back_a()
    for c in small_z:
        c.wait_recv()
    sm_y[p.y] = total(sm_z, 4).astype(BF16)
    for c in small_y:
        c.start()
    planes[0].start_pass()
    planes[1].start_pass()
    planes[2].start_pass()
    for c in small_y:
        c.wait_recv()
    sm_c[p.core] = total(sm_y, 4).astype(BF16)
    for c in small_c:
        c.start()
    for c in small_c:
        c.wait_recv()
    out_small[...] = total(sm_c, 2)

    for c in sends + small_x + small_z + small_y + small_c:
        c.wait_send()
    for g in pairs + scatters + planes:
        g.finish()


def back(tokens, cotangent, posm, share, small_all, n1, q, kv, o, r, dr_rows, y_rows, wq, wkv, wo):
    D = MODEL_WIDTH
    cosine, sine = rope_tables()

    def arr(shape, dtype=BF16):
        return jax.ShapeDtypeStruct(shape, dtype)

    vm = pl.BlockSpec(memory_space=VMEM)
    hb = pl.BlockSpec(memory_space=ANY)
    sem = pltpu.SemaphoreType.DMA
    widths = (D, D, 2 * KV)
    return pl.pallas_call(
        back_kernel,
        out_shape=[
            arr((SEQ, D)), arr((SEQ, D), F32), arr((SHARD, D)), arr((SHARD, D)), arr((SHARD, 2 * KV)),
            arr((48, SHARD), F32),
        ],
        in_specs=[vm] * 12 + [hb] * 5,
        out_specs=[vm] * 6,
        scratch_shapes=[
            VMEM((EXPERTS, CAP, D), BF16),
            VMEM((EXPERTS, CAP, D), BF16),
            VMEM((D, D), BF16),
            VMEM((D, 2 * KV), BF16),
            VMEM((D, D), BF16),
            VMEM((SEQ, D), F32),
            VMEM((SEQ, D), F32),
            VMEM((SEQ, D), BF16),
            VMEM((SEQ, D), BF16),
            VMEM((SEQ, D), BF16),
            VMEM((SEQ, 2 * KV), BF16),
            VMEM((EXPERTS, SEQ), F32),
            *[VMEM((D, w), BF16) for w in widths],
            *[VMEM((4, HALF, w), BF16) for w in widths],
            *[VMEM((6, HALF // 2, w), BF16) for w in widths],
            *[VMEM((HALF, w), BF16) for w in widths],
            *[VMEM((HALF, w // 4), BF16) for w in widths],
            *[VMEM((3, HALF, w // 4), BF16) for w in widths],
            *[VMEM((3, HALF // 4, w // 4), BF16) for w in widths],
            VMEM((4, 48, SHARD), BF16),
            VMEM((3, 48, SHARD), BF16),
            VMEM((4, 48, SHARD), BF16),
            VMEM((4, 48, SHARD), BF16),
            VMEM((2, 48, SHARD), BF16),
            sem((31,)),
            sem((31,)),
            sem((3, 4)),
            sem((3, 4)),
            sem((3, 6)),
            sem((3, 6)),
            sem((3, 13)),
            sem((3, 13)),
            sem((10,)),
            sem((10,)),
            sem((5,)),
        ],
        compiler_params=pltpu.CompilerParams(
            collective_id=1, has_side_effects=True, vmem_limit_bytes=LIMIT
        ),
        name="back",
    )(
        tokens, cotangent, posm, share, small_all, n1, q, kv, o, r,
        jnp.asarray(cosine), jnp.asarray(sine), dr_rows, y_rows, wq, wkv, wo,
    )


def finish_kernel(mixed, tokens, q, o, kv, gate, up, down, small, mixed_, tokens_, q_, k_, v_, o_, gate_, up_, down_, router_):
    mixed_[...] = mixed[...]
    tokens_[...] = tokens[...]
    q_[...] = q[...].astype(F32)
    o_[...] = o[...].astype(F32)
    k_[...] = kv[:, :KV].astype(F32)
    v_[...] = kv[:, KV:].astype(F32)
    gate_[0] = gate[...].astype(F32)
    up_[0] = up[...].astype(F32)
    down_[0] = down[...].astype(F32)
    router_[...] = small[0:32, :]


def finish(mixed, tokens, q, o, kv, gate, up, down, small):
    steps = 4

    def tall(count, width):
        return pl.BlockSpec((count // steps, width), lambda i: (i, 0))

    def owned():
        return pl.BlockSpec((1, SHARD // steps, FF), lambda i: (0, i, 0))

    def arr(*shape, dtype=F32):
        return jax.ShapeDtypeStruct(shape, dtype)

    D = MODEL_WIDTH
    return pl.pallas_call(
        finish_kernel,
        grid=(steps,),
        in_specs=[
            tall(SEQ, D), tall(SEQ, D), tall(SHARD, D), tall(SHARD, D), tall(SHARD, 2 * KV),
            tall(SHARD, FF), tall(SHARD, FF), tall(SHARD, FF), pl.BlockSpec((48, SHARD), lambda i: (0, 0)),
        ],
        out_specs=[
            tall(SEQ, D), tall(SEQ, D), tall(SHARD, D), tall(SHARD, KV), tall(SHARD, KV), tall(SHARD, D),
            owned(), owned(), owned(), pl.BlockSpec((EXPERTS, SHARD), lambda i: (0, 0)),
        ],
        out_shape=[
            arr(SEQ, D, dtype=BF16), arr(SEQ, D), arr(SHARD, D), arr(SHARD, KV), arr(SHARD, KV), arr(SHARD, D),
            arr(1, SHARD, FF), arr(1, SHARD, FF), arr(1, SHARD, FF), arr(EXPERTS, SHARD),
        ],
        compiler_params=pltpu.CompilerParams(vmem_limit_bytes=LIMIT),
        name="finish",
    )(mixed, tokens, q, o, kv, gate, up, down, small)


def pack_small(w_router, norm_one, norm_two):
    row = lax.broadcasted_iota(jnp.int32, (48, SHARD), 0)
    router = jnp.pad(w_router.T, ((0, 16), (0, 0)))
    gains = jnp.where(row == 32, norm_one[None, :], jnp.where(row == 33, norm_two[None, :], 0))
    return jnp.where(row < 32, router, gains).astype(BF16)


def shards(
    tokens, routes, w_query, key_matrix, value_matrix, w_output, norm_one, norm_two,
    w_router, w_gate, w_up, w_down, cotangent,
):
    small = pack_small(w_router, norm_one, norm_two)
    (_, dr_rows, y_rows, fq, fkv, fo, small_all, posm, share, n1, q, kv, o, r, g_gate, g_up, g_down) = forth(
        tokens, cotangent, routes.T, small, w_query, key_matrix, value_matrix, w_output,
        w_gate[0], w_up[0], w_down[0],
    )
    mixed, g_tokens, g_o, g_q, g_kv, g_small = back(
        tokens, cotangent, posm, share, small_all, n1, q, kv, o, r, dr_rows, y_rows, fq, fkv, fo
    )
    mixed, g_tokens, g_q, g_k, g_v, g_o, g_gate, g_up, g_down, g_router = finish(
        mixed, g_tokens, g_q, g_o, g_kv, g_gate, g_up, g_down, g_small
    )
    return (
        mixed, g_tokens, g_q, g_k, g_v, g_o, g_small[32], g_small[33], g_router.T, g_gate, g_up, g_down
    )


def solution(mesh):
    rows_split = P(("dp", "expert"), None)
    flat = P("dp", None)
    vector = P("dp")
    owned = P("expert", "dp", None)
    return jax.shard_map(
        shards,
        mesh=mesh,
        in_specs=(
            rows_split, rows_split, flat, flat, flat, flat, vector, vector, flat, owned, owned, owned,
            rows_split,
        ),
        out_specs=(
            rows_split, rows_split, flat, flat, flat, flat, vector, vector, flat, owned, owned, owned,
        ),
        check_vma=False,
    )
```

```python
import functools
import itertools

import jax
import jax.numpy as jnp
import numpy as np
from jax import lax
from jax.experimental import pallas as pl
from jax.experimental.pallas import tpu as pltpu
from jax.sharding import PartitionSpec as P

MODEL_WIDTH = 1536
QUERY_HEADS = 12
KEY_VALUE_HEADS = 2
HEAD_SIZE = 128
TOPK = 4
SEQ = 256
EXPERTS = 32
CAP = 40
FF = 768
KV = KEY_VALUE_HEADS * HEAD_SIZE
SHARD = MODEL_WIDTH // 4
HALF = SHARD // 2
QUARTER = HALF // 2
EPSILON = 1e-06
ROPE_BASE = 10000.0
SCALE = HEAD_SIZE ** (-0.5)
MESH = pl.DeviceIdType.MESH
F32 = jnp.float32
BF16 = jnp.bfloat16
VMEM = pltpu.VMEM
ANY = pl.ANY
LIMIT = 60 * 1024 * 1024


def _offsets():
    def far(a):
        return min(a, 4 - a)

    every = [o for o in itertools.product(range(4), range(4), range(2)) if o != (0, 0, 0)]
    return sorted(every, key=lambda o: (far(o[0]) + far(o[1]), o))[::-1]


OFFSETS = _offsets()


def rope_tables():
    position = np.arange(SEQ, dtype=np.float32)
    frequency = (
        np.float32(ROPE_BASE) ** (-np.arange(64, dtype=np.float32) * np.float32(2.0 / HEAD_SIZE))
    ).astype(np.float32)
    angles = (position[:, None] * frequency[None, :]).astype(np.float32)
    cosine = np.cos(angles.astype(np.float64)).astype(np.float32)
    sine = np.sin(angles.astype(np.float64)).astype(np.float32)
    return (
        np.concatenate([cosine, cosine], axis=1),
        np.concatenate([-sine, sine], axis=1),
    )


def mm(left, right, left_dim=1, right_dim=0):
    return lax.dot_general(
        left, right, (((left_dim,), (right_dim,)), ((), ())), preferred_element_type=F32
    )


class Place:
    def __init__(self):
        self.x = lax.axis_index("dp")
        self.e = lax.axis_index("expert")
        self.core = lax.rem(self.e, 2)
        self.y = lax.rem(self.e // 2, 4)
        self.z = self.e // 8
        self.xl = lax.rem(self.x + 3, 4)
        self.xr = lax.rem(self.x + 1, 4)
        self.x2 = lax.rem(self.x + 2, 4)
        self.left = (self.xl, self.e)
        self.right = (self.xr, self.e)
        self.across = (self.x2, self.e)
        self.sibling = (self.x, self.e + 1 - 2 * self.core)

    def peer(self, offset):
        dz, dy, dc = offset
        return (
            lax.rem(self.z + dz, 4) * 8 + lax.rem(self.y + dy, 4) * 2 + lax.rem(self.core + dc, 2)
        )

    def peers(self):
        return [self.peer(o) for o in OFFSETS]


def greet(devices):
    barrier = pltpu.get_barrier_semaphore()
    for d in devices:
        pl.semaphore_signal(barrier, inc=1, device_id=d, device_id_type=MESH)
    return barrier


def remote(src, dst, send, recv, device):
    return pltpu.make_async_remote_copy(
        src_ref=src, dst_ref=dst, send_sem=send, recv_sem=recv, device_id=device, device_id_type=MESH
    )


def rows(start, count, align=16):
    return pl.ds(pl.multiple_of(start, align), count)


class Gather:
    def __init__(self, place, shard, region, send, recv):
        p = place
        half = p.core * HALF

        def move(k, src, dst, device):
            return remote(src, dst, send.at[k], recv.at[k], device)

        mine = shard.at[rows(half, HALF, 32)]
        self.direct = [
            move(0, mine, region(p.x, half, HALF), p.right),
            move(1, mine, region(p.x, half, HALF), p.left),
        ]
        from_left = region(p.xl, half, QUARTER)
        from_right = region(p.xr, half + QUARTER, QUARTER)
        self.forward = [
            move(2, from_left, from_left, p.right),
            move(3, from_right, from_right, p.left),
        ]
        whole_left = region(p.xl, half, HALF)
        whole_right = region(p.xr, half, HALF)
        far_one = region(p.x2, half, QUARTER)
        far_two = region(p.x2, half + QUARTER, QUARTER)
        self.near = [
            move(4, whole_left, whole_left, p.sibling),
            move(5, whole_right, whole_right, p.sibling),
        ]
        self.far = [
            move(6, far_one, far_one, p.sibling),
            move(7, far_two, far_two, p.sibling),
        ]

    def start(self):
        for c in self.direct:
            c.start()

    def relay(self):
        for k in range(2):
            self.direct[k].wait_recv()
            self.forward[k].start()
            self.near[k].start()

    def relay_far(self):
        for k in range(2):
            self.forward[k].wait_recv()
            self.far[k].start()

    def arrived_near(self):
        for c in self.near:
            c.wait_recv()

    def arrived_far(self):
        for c in self.far:
            c.wait_recv()

    def finish(self):
        for c in self.direct + self.forward + self.near + self.far:
            c.wait_send()


def slot_rows(posm_ref, first, count):
    slot = lax.broadcasted_iota(jnp.int32, (CAP, SEQ), 0).astype(F32)
    return [
        jnp.where(posm_ref[pl.ds(first + j, 1), :] == slot, 1.0, 0.0) for j in range(count)
    ]


def turn(values, cosine, sine):
    return values * cosine + pltpu.roll(values, 64, 1) * sine


def turn_back(values, cosine, sine):
    return values * cosine - pltpu.roll(values, 64, 1) * sine


def softmax_parts(q_head, k_head, causal):
    scores = mm(q_head, k_head, 1, 1) * SCALE
    scores = jnp.where(causal, scores, -jnp.inf)
    largest = jnp.max(scores, axis=-1, keepdims=True)
    exponent = jnp.exp(scores - largest)
    return exponent / jnp.sum(exponent, axis=-1, keepdims=True)


def causal_mask():
    row = lax.broadcasted_iota(jnp.int32, (SEQ, SEQ), 0)
    column = lax.broadcasted_iota(jnp.int32, (SEQ, SEQ), 1)
    return column <= row


def norm_back(v, gain, grad):
    scale = lax.rsqrt(jnp.mean(v * v, axis=-1, keepdims=True) + EPSILON)
    unit = v * scale
    w = grad * gain
    return (
        (w - unit * jnp.mean(w * unit, axis=-1, keepdims=True)) * scale,
        jnp.sum(grad * unit, axis=0, keepdims=True),
    )


def gelu_parts(a):
    inner = jnp.tanh(0.7978845608028654 * (a + 0.044715 * a * a * a))
    value = 0.5 * a * (1.0 + inner)
    slope = 0.5 * (1.0 + inner) + 0.5 * a * (1.0 - inner * inner) * 0.7978845608028654 * (
        1.0 + 3.0 * 0.044715 * a * a
    )
    return value, slope


class GatherOwn:
    def __init__(self, place, shard, region, send, recv):
        p = place

        def move(k, src, dst, device):
            return remote(src, dst, send.at[k], recv.at[k], device)

        self.direct = [
            move(0, shard, region(p.x, 0, SHARD), p.right),
            move(1, shard, region(p.x, 0, SHARD), p.left),
        ]
        from_left = region(p.xl, 0, HALF)
        from_right = region(p.xr, HALF, HALF)
        self.forward = [
            move(2, from_left, from_left, p.right),
            move(3, from_right, from_right, p.left),
        ]

    def start(self):
        for c in self.direct:
            c.start()

    def relay(self):
        for k in range(2):
            self.direct[k].wait_recv()
            self.forward[k].start()

    def arrived(self):
        for c in self.forward:
            c.wait_recv()

    def finish(self):
        for c in self.direct + self.forward:
            c.wait_send()


class Scatter:
    def __init__(self, place, partial, landing, send, recv, first=0, height=SHARD, width=None):
        p = self.p = place
        half = height // 2
        self.partial, self.landing, self.first, self.height = partial, landing, first, height
        self.cut = cut = pl.ds(0, width or partial.shape[1])

        def region(x, part):
            return partial.at[rows(x * SHARD + first + part * half, half, 32), cut]

        def move(k, src, device):
            return remote(src, landing.at[k], send.at[k], recv.at[k], device)

        self.far = [move(0, region(p.x2, 0), p.right), move(1, region(p.x2, 1), p.left)]
        self.near = [move(2, region(p.xr, 1), p.right), move(3, region(p.xl, 0), p.left)]
        self.summed = [move(4, region(p.xr, 0), p.right), move(5, region(p.xl, 1), p.left)]

    def relay(self):
        p, half = self.p, self.height // 2
        for k, x, part in ((0, p.xr, 0), (1, p.xl, 1)):
            self.far[k].wait_recv()
            where = rows(x * SHARD + self.first + part * half, half, 32)
            self.partial[where, self.cut] = (
                self.partial[where, self.cut].astype(F32) + self.landing[k].astype(F32)
            ).astype(BF16)
            self.summed[k].start()

    def result(self, part):
        p, half = self.p, self.height // 2
        own = self.partial[rows(p.x * SHARD + self.first + part * half, half, 32), self.cut]
        one, two = ((4, 3), (2, 5))[part]
        return (
            own.astype(F32)
            + self.landing[one].astype(F32)
            + self.landing[two].astype(F32)
        )

    def arrived(self):
        for c in self.near + self.summed:
            c.wait_recv()

    def finish(self):
        for c in self.far + self.near + self.summed:
            c.wait_send()


GROUP = 8
BLOCK = GROUP * CAP


def flatten(slots):
    return slots.astype(F32).reshape(BLOCK, MODEL_WIDTH).astype(BF16)


def unflatten(values):
    return values.reshape(GROUP, CAP, MODEL_WIDTH).astype(BF16)


def forth_kernel(
    tokens, cotangent, routes, small, cosine, sine, wq, wk, wv, wo, wgate, wup, wdown,
    dy_in, dr_in, y_out, wq_full, wkv_full, wo_full, gate_out,
    small_all, posm, share, n1, q, kv, o, r, g_up, g_down,
    buf_a, buf_b, landing, dyflat, wqf, wkvf, wof, wgu, wd, hid, part_down, part_gate, part_up, land_down, land_up,
    n2, qacc, kvacc,
    ag, ag_r, sg, sg_r, ds_, dr_, gs, gr, ns, nr, bs, br, ss, sr, ls,
):
    p = Place()
    peers = p.peers()
    sources = [p.peer(tuple((-v) % m for v, m in zip(o_, (4, 4, 2)))) for o_ in OFFSETS]
    barrier = greet([p.left, p.right, p.across] + [(p.x, t) for t in peers])

    def columns(full, first, count):
        return lambda x, start, height: full.at[
            rows(x * SHARD + start, height, 32), pl.ds(first, count)
        ]

    at_q = columns(wqf, 0, MODEL_WIDTH)
    at_k = columns(wkvf, 0, KV)
    at_v = columns(wkvf, KV, KV)
    at_o = columns(wof, 0, MODEL_WIDTH)
    at_gate = columns(wgu, 0, FF)
    at_up = columns(wgu, FF, FF)
    at_down = columns(wd, 0, FF)
    mine = [
        pltpu.make_async_copy(w, f(p.x, 0, SHARD), ls.at[k])
        for k, (w, f) in enumerate(
            [
                (wq, at_q), (wk, at_k), (wv, at_v), (wo, at_o),
                (wgate, at_gate), (wup, at_up), (wdown, at_down),
            ]
        )
    ]
    for c in mine:
        c.start()

    lane = lax.broadcasted_iota(jnp.int32, (EXPERTS, SEQ), 0)
    named = routes[0:1, :] == lane
    for j in range(1, TOPK):
        named = jnp.logical_or(named, routes[j : j + 1, :] == lane)
    earlier = (
        lax.broadcasted_iota(jnp.int32, (SEQ, SEQ), 0)
        < lax.broadcasted_iota(jnp.int32, (SEQ, SEQ), 1)
    ).astype(F32).astype(BF16)
    place_of = mm(named.astype(F32).astype(BF16), earlier)
    posm[...] = jnp.where(named, place_of, -1.0)

    small_all[p.x] = small[...]
    pl.semaphore_wait(barrier, len(peers) + 3)

    small_moves = [
        remote(small, small_all.at[p.x], sg.at[k], sg_r.at[k], d)
        for k, d in enumerate([p.right, p.left, p.across])
    ]
    for c in small_moves:
        c.start()
    gq, gk, gv, go = [
        Gather(p, w, f, ag.at[k], ag_r.at[k])
        for k, (w, f) in enumerate([(wq, at_q), (wk, at_k), (wv, at_v), (wo, at_o)])
    ]
    for g in (gq, gk, gv):
        g.start()

    for c in small_moves:
        c.wait_recv()
    logits = mm(small_all[0, 0:32, :], tokens[:, 0:SHARD], 1, 1)
    for s in range(1, 4):
        logits += mm(small_all[s, 0:32, :], tokens[:, s * SHARD : (s + 1) * SHARD], 1, 1)
    top = jnp.max(jnp.where(named, logits, -jnp.inf), axis=0, keepdims=True)
    weight = jnp.where(named, jnp.exp(jnp.minimum(logits - top, 0.0)), 0.0)
    share[...] = weight / jnp.sum(weight, axis=0, keepdims=True)

    places = peers + [p.e]
    dy_sends = [
        remote(buf_a.at[k], dy_in.at[k], ds_.at[k], dr_.at[k], (p.x, t))
        for k, t in enumerate(peers)
    ]
    own_dy = pltpu.make_async_copy(buf_a.at[31], dy_in.at[31], ls.at[7])
    for i in range(0, EXPERTS, 4):
        hot = [slot_rows(posm, t, 1)[0] for t in places[i : i + 4]]
        gain = jnp.concatenate(
            [
                jnp.sum(b * share[pl.ds(t, 1), :], axis=-1, keepdims=True)
                for t, b in zip(places[i : i + 4], hot)
            ],
            axis=0,
        )
        picked = mm(jnp.concatenate(hot, axis=0).astype(BF16), cotangent[...])
        buf_a[i : i + 4] = (picked * gain).reshape(4, CAP, MODEL_WIDTH).astype(BF16)
        for c in dy_sends[i : i + 4]:
            c.start()
    own_dy.start()

    x = tokens[...].astype(F32)
    unit = x * lax.rsqrt(jnp.mean(x * x, axis=-1, keepdims=True) + EPSILON)
    for s in range(4):
        cut = slice(s * SHARD, (s + 1) * SHARD)
        n1[:, cut] = (unit[:, cut] * small_all[s, 32:33, :].astype(F32)).astype(BF16)

    def part(x_index):
        return n1[:, rows(x_index * SHARD, SHARD, 128)]

    def block(full, x_index):
        return full[rows(x_index * SHARD, SHARD, 128), :]

    for c in mine[:3]:
        c.wait()
    qacc[...] = mm(part(p.x), block(wqf, p.x))
    kvacc[...] = mm(part(p.x), block(wkvf, p.x))
    for g in (gq, gk, gv):
        g.relay()
    go.start()
    for g in (gq, gk, gv):
        g.arrived_near()
    for s in (p.xl, p.xr):
        qacc[...] += mm(part(s), block(wqf, s))
        kvacc[...] += mm(part(s), block(wkvf, s))
    for g in (gq, gk, gv):
        g.relay_far()
    for g in (gq, gk, gv):
        g.arrived_far()
    qacc[...] += mm(part(p.x2), block(wqf, p.x2))
    kvacc[...] += mm(part(p.x2), block(wkvf, p.x2))
    keep = [
        pltpu.make_async_copy(f, out, ls.at[8 + k])
        for k, (f, out) in enumerate([(wqf, wq_full), (wkvf, wkv_full), (wof, wo_full)])
    ]
    keep[0].start()
    keep[1].start()

    cos = cosine[...]
    sin = sine[...]
    for h in range(KEY_VALUE_HEADS):
        cut = slice(h * HEAD_SIZE, (h + 1) * HEAD_SIZE)
        kv[:, cut] = turn(kvacc[:, cut], cos, sin).astype(BF16)
        cut = slice(KV + h * HEAD_SIZE, KV + (h + 1) * HEAD_SIZE)
        kv[:, cut] = kvacc[:, cut].astype(BF16)
    causal = causal_mask()
    for h in range(QUERY_HEADS):
        cut = slice(h * HEAD_SIZE, (h + 1) * HEAD_SIZE)
        c = h // (QUERY_HEADS // KEY_VALUE_HEADS)
        q_head = turn(qacc[:, cut], cos, sin).astype(BF16)
        q[:, cut] = q_head
        weights = softmax_parts(q_head, kv[:, c * HEAD_SIZE : (c + 1) * HEAD_SIZE], causal)
        o[:, cut] = mm(
            weights.astype(BF16), kv[:, KV + c * HEAD_SIZE : KV + (c + 1) * HEAD_SIZE]
        ).astype(BF16)

    def opart(x_index):
        return o[:, rows(x_index * SHARD, SHARD, 128)]

    for c in mine[3:]:
        c.wait()
    r[...] = tokens[...].astype(F32) + mm(opart(p.x), block(wof, p.x))
    go.relay()
    ggate = GatherOwn(p, wgate, at_gate, gs.at[0], gr.at[0])
    gup = GatherOwn(p, wup, at_up, gs.at[1], gr.at[1])
    gdown = GatherOwn(p, wdown, at_down, gs.at[2], gr.at[2])
    ggate.start()
    gup.start()
    go.arrived_near()
    for s in (p.xl, p.xr):
        r[...] += mm(opart(s), block(wof, s))
    go.relay_far()
    go.arrived_far()
    keep[2].start()
    residual = r[...] + mm(opart(p.x2), block(wof, p.x2))
    r[...] = residual
    unit = residual * lax.rsqrt(jnp.mean(residual * residual, axis=-1, keepdims=True) + EPSILON)
    for s in range(4):
        cut = slice(s * SHARD, (s + 1) * SHARD)
        n2[:, cut] = (unit[:, cut] * small_all[s, 33:34, :].astype(F32)).astype(BF16)

    sends = [
        remote(buf_b.at[k], landing.at[k], ns.at[k], nr.at[k], (p.x, t))
        for k, t in enumerate(peers)
    ]
    own_rows = pltpu.make_async_copy(buf_b.at[31], landing.at[31], ls.at[11])
    for i in range(0, EXPERTS, 4):
        hot = [slot_rows(posm, t, 1)[0] for t in places[i : i + 4]]
        picked = mm(jnp.concatenate(hot, axis=0).astype(BF16), n2[...])
        buf_b[i : i + 4] = picked.reshape(4, CAP, MODEL_WIDTH).astype(BF16)
        for c in sends[i : i + 4]:
            c.start()
    own_rows.start()

    ggate.relay()
    gup.relay()
    gdown.start()
    for c in dy_sends:
        c.wait()
    own_dy.wait()
    load_dy = pltpu.make_async_copy(dy_in, buf_a, ls.at[12])
    load_dy.start()
    for g in (gq, gk, gv, go):
        g.finish()
    for c in small_moves:
        c.wait_send()
    for c in keep:
        c.wait()
    rflat = wof
    dab = wqf
    load_dy.wait()

    @pl.loop(0, 4)
    def _(i):
        dyflat[rows(i * BLOCK, BLOCK), :] = flatten(buf_a[pl.ds(i * GROUP, GROUP)])

    ggate.arrived()
    gup.arrived()

    def forward(i):
        if i == 3:
            own_rows.wait()
        for c in sends[i * GROUP : (i + 1) * GROUP]:
            c.wait_recv()
        cut = slice(i * BLOCK, (i + 1) * BLOCK)
        rflat[cut, :] = flatten(landing[i * GROUP : (i + 1) * GROUP])
        ab = mm(rflat[cut, :], wgu[...])
        value, slope = gelu_parts(ab[:, :FF])
        b = ab[:, FF:]
        hid[cut, :] = (value * b).astype(BF16)
        dab[cut, :FF] = (slope * b).astype(BF16)
        dab[cut, FF:] = value.astype(BF16)

    backs = [
        remote(buf_a.at[k], dr_in.at[p.e], bs.at[k], br.at[k], (p.x, sources[k])) for k in range(31)
    ]

    def backward(i):
        cut = slice(i * BLOCK, (i + 1) * BLOCK)
        dh = mm(dyflat[cut, :], wd[...])
        dab[cut, :FF] = (dh * dab[cut, :FF].astype(F32)).astype(BF16)
        dab[cut, FF:] = (dh * dab[cut, FF:].astype(F32)).astype(BF16)
        buf_a[i * GROUP : (i + 1) * GROUP] = unflatten(mm(dab[cut, :], wgu[...], 1, 1))
        for c in backs[i * GROUP : (i + 1) * GROUP]:
            c.start()

    forward(0)
    forward(1)
    gdown.relay()
    forward(2)
    gdown.arrived()
    backward(0)
    backward(1)
    backward(2)
    forward(3)
    backward(3)
    own_back = pltpu.make_async_copy(buf_a.at[31], dr_in.at[p.e], ls.at[13])
    own_back.start()

    sdown = Scatter(p, part_down, land_down, ss.at[0], sr.at[0])
    sup = Scatter(p, part_up, land_up, ss.at[1], sr.at[1])

    def down_block(x):
        where = rows(x * SHARD, SHARD, 128)
        part_down[where, :] = mm(dyflat[:, where], hid[...], 0, 0).astype(BF16)

    def gate_up_block(x):
        where = rows(x * SHARD, SHARD, 128)
        both = mm(rflat[0 : EXPERTS * CAP, where], dab[0 : EXPERTS * CAP, :], 0, 0)
        part_gate[where, :] = both[:, :FF].astype(BF16)
        part_up[where, :] = both[:, FF:].astype(BF16)

    def start_scatter(scatter, fill):
        fill(p.x2)
        for c in scatter.far:
            c.start()
        fill(p.xr)
        scatter.near[0].start()
        fill(p.xl)
        scatter.near[1].start()
        fill(p.x)

    start_scatter(sdown, down_block)
    start_scatter(sup, gate_up_block)
    keep_gate = pltpu.make_async_copy(part_gate, gate_out, ls.at[15])
    keep_gate.start()
    sdown.relay()

    for c in sends:
        c.wait_send()
    for i in range(4):
        cut = slice(i * BLOCK, (i + 1) * BLOCK)
        buf_b[i * GROUP : (i + 1) * GROUP] = unflatten(mm(hid[cut, :], wd[...], 1, 1))
    keep_y = pltpu.make_async_copy(buf_b, y_out, ls.at[14])
    keep_y.start()

    sup.relay()
    sdown.arrived()
    for half in range(2):
        g_down[half * HALF : (half + 1) * HALF, :] = sdown.result(half).astype(BF16)
    sup.arrived()
    for half in range(2):
        g_up[half * HALF : (half + 1) * HALF, :] = sup.result(half).astype(BF16)

    keep_gate.wait()
    for c in backs:
        c.wait()
    own_back.wait()
    keep_y.wait()
    for g in (ggate, gup, gdown, sdown, sup):
        g.finish()


def forth(tokens, cotangent, routes, small, wq, wk, wv, wo, wgate, wup, wdown):
    cosine, sine = rope_tables()
    D = MODEL_WIDTH

    def arr(shape, dtype=BF16):
        return jax.ShapeDtypeStruct(shape, dtype)

    vm = pl.BlockSpec(memory_space=VMEM)
    hb = pl.BlockSpec(memory_space=ANY)
    sem = pltpu.SemaphoreType.DMA
    N = EXPERTS * CAP
    slots = (EXPERTS, CAP, D)
    return pl.pallas_call(
        forth_kernel,
        out_shape=[
            arr(slots), arr(slots), arr(slots), arr((D, D)), arr((D, 2 * KV)), arr((D, D)), arr((D, FF)),
            arr((4, 48, SHARD)), arr((EXPERTS, SEQ), F32), arr((EXPERTS, SEQ), F32),
            arr((SEQ, D)), arr((SEQ, D)), arr((SEQ, 2 * KV)), arr((SEQ, D)), arr((SEQ, D), F32),
            arr((SHARD, FF)), arr((SHARD, FF)),
        ],
        in_specs=[vm] * 6 + [hb] * 7,
        out_specs=[hb] * 7 + [vm] * 10,
        scratch_shapes=[
            VMEM(slots, BF16),
            VMEM(slots, BF16),
            VMEM(slots, BF16),
            VMEM((N, D), BF16),
            VMEM((D, D), BF16),
            VMEM((D, 2 * KV), BF16),
            VMEM((D, D), BF16),
            VMEM((D, 2 * FF), BF16),
            VMEM((D, FF), BF16),
            VMEM((N, FF), BF16),
            VMEM((D, FF), BF16),
            VMEM((D, FF), BF16),
            VMEM((D, FF), BF16),
            VMEM((6, HALF, FF), BF16),
            VMEM((6, HALF, FF), BF16),
            VMEM((SEQ, D), BF16),
            VMEM((SEQ, D), F32),
            VMEM((SEQ, 2 * KV), F32),
            sem((4, 8)), sem((4, 8)), sem((3,)), sem((3,)), sem((31,)), sem((31,)),
            sem((3, 4)), sem((3, 4)), sem((31,)), sem((31,)), sem((31,)), sem((31,)),
            sem((2, 6)), sem((2, 6)), sem((16,)),
        ],
        compiler_params=pltpu.CompilerParams(
            collective_id=0, has_side_effects=True, vmem_limit_bytes=LIMIT
        ),
        name="forth",
    )(
        tokens, cotangent, routes, small, jnp.asarray(cosine), jnp.asarray(sine),
        wq, wk, wv, wo, wgate, wup, wdown,
    )


WIDE = 8 * HEAD_SIZE

class PairSum:
    def __init__(self, place, partial, landing, send, recv):
        p = place
        self.order = [p.x2, p.xr, p.xl, p.x]
        self.partial, self.landing = partial, landing
        self.half = p.core * HALF
        self.moves = [
            remote(
                partial.at[rows(x * SHARD + HALF - self.half, HALF, 32)],
                landing.at[i],
                send.at[i],
                recv.at[i],
                p.sibling,
            )
            for i, x in enumerate(self.order)
        ]

    def add(self, i):
        self.moves[i].wait_recv()
        where = rows(self.order[i] * SHARD + self.half, HALF, 32)
        self.partial[where, :] = (
            self.partial[where, :].astype(F32) + self.landing[i].astype(F32)
        ).astype(BF16)

    def finish(self):
        for c in self.moves:
            c.wait_send()


class PlaneSum:
    def __init__(self, place, current, piece, out, land_a, land_b, width, z_first, send, recv):
        p = self.p = place
        self.current, self.piece, self.out = current, piece, out
        self.land_a, self.land_b = land_a, land_b
        w = self.w = width // 4
        t = HALF // 4
        a, b = (p.z, p.y) if z_first else (p.y, p.z)
        self.a, self.b = a, b

        def along_a(d):
            return (p.x, p.peer((d, 0, 0) if z_first else (0, d, 0)))

        def along_b(d):
            return (p.x, p.peer((0, d, 0) if z_first else (d, 0, 0)))

        def cut(i):
            return pl.ds(pl.multiple_of(i * w, 128), w)

        self.cut_a = cut(a)
        self.rows_b = rows(b * t, t)
        base = p.core * HALF
        self.mine = (rows(base + b * t, t), cut(a))
        spot = out.at[rows(base + b * t, t), cut(a)]
        strip = out.at[rows(base, HALF, 32), cut(a)]
        whole = out.at[rows(base, HALF, 32)]
        steps = (1, 2, 3)
        self.step_a = [
            remote(
                current.at[:, cut(lax.rem(a + d, 4))],
                land_a.at[d - 1],
                send.at[d - 1],
                recv.at[d - 1],
                along_a(d),
            )
            for d in steps
        ]
        self.step_b = [
            remote(
                piece.at[rows(lax.rem(b + d, 4) * t, t)],
                land_b.at[d - 1],
                send.at[2 + d],
                recv.at[2 + d],
                along_b(d),
            )
            for d in steps
        ]
        self.back_b = [remote(spot, spot, send.at[5 + d], recv.at[5 + d], along_b(d)) for d in steps]
        self.back_a = [
            remote(strip, strip, send.at[8 + d], recv.at[8 + d], along_a(d)) for d in steps
        ]
        self.pass_on = [remote(whole, whole, send.at[12], recv.at[12], p.sibling)]

    def start_a(self, scatter):
        part = HALF // 2
        scatter.arrived()
        for k in range(2):
            self.current[k * part : (k + 1) * part, :] = scatter.result(k).astype(BF16)
        for c in self.step_a:
            c.start()

    def start_b(self):
        for c in self.step_a:
            c.wait_recv()
        total = self.current[:, self.cut_a].astype(F32)
        for k in range(3):
            total += self.land_a[k].astype(F32)
        self.piece[...] = total.astype(BF16)
        for c in self.step_b:
            c.start()

    def start_back_b(self):
        for c in self.step_b:
            c.wait_recv()
        total = self.piece[self.rows_b, :].astype(F32)
        for k in range(3):
            total += self.land_b[k].astype(F32)
        self.out[self.mine] = total.astype(BF16)
        for c in self.back_b:
            c.start()

    def start_back_a(self):
        for c in self.back_b:
            c.wait_recv()
        for c in self.back_a:
            c.start()

    def start_pass(self):
        for c in self.back_a:
            c.wait_recv()
        for c in self.pass_on:
            c.start()

    def finish(self):
        for c in self.pass_on:
            c.wait()
        for c in self.step_a + self.step_b + self.back_b + self.back_a:
            c.wait_send()


def gain_row(small_all, row):
    return jnp.concatenate(
        [small_all[s, row : row + 1, :].astype(F32) for s in range(4)], axis=1
    )


def back_kernel(
    tokens, cotangent, posm, share, small_all, n1, q, kv, o, r, cosine, sine,
    dr_rows, y_rows, wq, wkv, wo, gate_rows,
    mixed, g_tokens, out_o, out_q, out_r, out_small, g_gate,
    drv, y_in, wqv, wkvv, wov, acc, da, do, dqp, drp, dgate, land_gate,
    part_o, part_q, part_r, pair_o, pair_q, pair_r, land_o, land_q, land_r,
    cur_o, cur_q, cur_r, pc_o, pc_q, pc_r, la_o, la_q, la_r, lb_o, lb_q, lb_r,
    sm_part, sm_x, sm_z, sm_y, sm_c,
    ys, yr, ps, pr, ss, sr, es, er, ts, tr, ms, mr, ls,
):
    p = Place()
    peers = p.peers()
    sources = [p.peer(tuple((-v) % m for v, m in zip(o_, (4, 4, 2)))) for o_ in OFFSETS]
    barrier = greet([p.left, p.right, p.across] + [(p.x, t) for t in peers])
    loads = [
        pltpu.make_async_copy(s, d, ls.at[k])
        for k, (s, d) in enumerate([(wo, wov), (wq, wqv), (wkv, wkvv)])
    ]
    groups = [
        pltpu.make_async_copy(
            dr_rows.at[pl.ds(i * GROUP, GROUP)], drv.at[i % 2], ls.at[6 + i]
        )
        for i in range(4)
    ]
    for c in groups[:2] + loads:
        c.start()
    pl.semaphore_wait(barrier, len(peers) + 3)
    sends = [
        remote(y_rows.at[k], y_in.at[p.e], ys.at[k], yr.at[k], (p.x, sources[k]))
        for k in range(31)
    ]
    own_y = pltpu.make_async_copy(y_rows.at[31], y_in.at[p.e], ls.at[5])
    own_y.start()

    for i in range(4):
        groups[i].wait()
        for c in sends[i * GROUP : (i + 1) * GROUP]:
            c.start()
        hot = jnp.concatenate(slot_rows(posm, i * GROUP, GROUP), axis=0).astype(BF16)
        term = mm(hot, flatten(drv[i % 2]), 0, 0)
        if i < 2:
            groups[i + 2].start()
        if i == 0:
            acc[...] = term
        else:
            acc[...] += term
    back, g_two = norm_back(r[...], gain_row(small_all, 33), acc[...])
    dr = cotangent[...].astype(F32) + back
    g_tokens[...] = dr
    da[...] = dr.astype(BF16)

    names = ((part_o, pair_o, land_o), (part_q, pair_q, land_q), (part_r, pair_r, land_r))
    pairs = [PairSum(p, a, b, ps.at[k], pr.at[k]) for k, (a, b, _) in enumerate(names)]
    scatters = [
        Scatter(p, a, c, ss.at[k], sr.at[k], p.core * HALF, HALF)
        for k, (a, _, c) in enumerate(names)
    ]

    def blocks(k, left, right):
        for i, x in enumerate(pairs[k].order):
            where = rows(x * SHARD, SHARD, 128)
            names[k][0][where, :] = mm(left[:, where], right[...], 0, 0).astype(BF16)
            pairs[k].moves[i].start()

    def sum_pairs(k):
        pairs[k].add(0)
        for c in scatters[k].far:
            c.start()
        pairs[k].add(1)
        scatters[k].near[0].start()
        pairs[k].add(2)
        scatters[k].near[1].start()
        pairs[k].add(3)

    blocks(0, o, da)
    sum_pairs(0)
    loads[0].wait()
    do[...] = mm(da[...], wov[...], 1, 1).astype(BF16)
    part_gate = wov
    load_gate = pltpu.make_async_copy(gate_rows, part_gate.at[:, pl.ds(0, FF)], ls.at[4])
    load_gate.start()

    cos = cosine[...]
    sin = sine[...]
    causal = causal_mask()
    group = QUERY_HEADS // KEY_VALUE_HEADS
    for c in range(KEY_VALUE_HEADS):
        k_cut = slice(c * HEAD_SIZE, (c + 1) * HEAD_SIZE)
        v_cut = slice(KV + c * HEAD_SIZE, KV + (c + 1) * HEAD_SIZE)
        dk = dv = None
        for h in range(c * group, (c + 1) * group):
            cut = slice(h * HEAD_SIZE, (h + 1) * HEAD_SIZE)
            soft = softmax_parts(q[:, cut], kv[:, k_cut], causal)
            dp = mm(do[:, cut], kv[:, v_cut], 1, 1)
            ds = (soft * (dp - jnp.sum(soft * dp, axis=-1, keepdims=True))).astype(BF16)
            dq = turn_back(mm(ds, kv[:, k_cut]) * SCALE, cos, sin).astype(BF16)
            if h < 8:
                dqp[:, cut] = dq
            else:
                drp[:, 2 * KV + (h - 8) * HEAD_SIZE : 2 * KV + (h - 7) * HEAD_SIZE] = dq
            k_term = mm(ds, q[:, cut], 0, 0)
            v_term = mm(soft.astype(BF16), do[:, cut], 0, 0)
            dk = k_term if dk is None else dk + k_term
            dv = v_term if dv is None else dv + v_term
        drp[:, k_cut] = turn_back(dk * SCALE, cos, sin).astype(BF16)
        drp[:, v_cut] = dv.astype(BF16)
    scatters[0].relay()

    blocks(1, n1, dqp)
    blocks(2, n1, drp)
    sum_pairs(1)
    sum_pairs(2)

    loads[1].wait()
    loads[2].wait()
    dn1 = (
        mm(dqp[...], wqv[:, :WIDE], 1, 1)
        + mm(drp[:, 2 * KV :], wqv[:, WIDE:], 1, 1)
        + mm(drp[:, : 2 * KV], wkvv[...], 1, 1)
    )
    back, g_one = norm_back(tokens[...].astype(F32), gain_row(small_all, 32), dn1)
    g_tokens[...] += back

    work = (
        (cur_o, pc_o, out_o, la_o, lb_o, MODEL_WIDTH, True),
        (cur_q, pc_q, out_q, la_q, lb_q, WIDE, False),
        (cur_r, pc_r, out_r, la_r, lb_r, WIDE, True),
    )
    planes = [PlaneSum(p, *w, ts.at[k], tr.at[k]) for k, w in enumerate(work)]
    scatters[1].relay()
    scatters[2].relay()
    load_gate.wait()
    sgate = Scatter(p, part_gate, land_gate, es, er, width=FF)
    for c in sgate.far + sgate.near:
        c.start()

    def combine(i):
        hot = slot_rows(posm, i * GROUP, GROUP)
        weighted = jnp.concatenate(
            [b * share[i * GROUP + j : i * GROUP + j + 1, :] for j, b in enumerate(hot)], axis=0
        )
        high = weighted.astype(BF16)
        low = (weighted - high.astype(F32)).astype(BF16)
        y_f32 = y_in[i * GROUP : (i + 1) * GROUP].astype(F32).reshape(BLOCK, MODEL_WIDTH)
        y_now = y_f32.astype(BF16)
        term = mm(high, y_now, 0, 0) + mm(low, y_now, 0, 0)
        if i == 0:
            acc[...] = r[...] + term
        else:
            acc[...] += term
        picked = mm(jnp.concatenate(hot, axis=0).astype(BF16), cotangent[...])
        dslot = jnp.sum(picked * y_f32, axis=-1, keepdims=True)
        for j, b in enumerate(hot):
            dgate[i * GROUP + j : i * GROUP + j + 1, :] = jnp.sum(
                b * dslot[j * CAP : (j + 1) * CAP], axis=0, keepdims=True
            )

    def route_back():
        mixed[...] = acc[...].astype(BF16)
        gates = share[...]
        dlogits = gates * (dgate[...] - jnp.sum(gates * dgate[...], axis=0, keepdims=True))
        dlogits = jnp.where(posm[...] >= 0.0, dlogits, 0.0).astype(BF16)
        g_router = mm(dlogits, tokens[...])
        for s in range(4):
            cut = slice(s * SHARD, (s + 1) * SHARD)
            g_tokens[:, cut] += mm(dlogits, small_all[s, 0:32, :], 0, 0)
            sm_part[s] = jnp.concatenate(
                [g_router[:, cut], g_one[:, cut], g_two[:, cut], jnp.zeros((14, SHARD), F32)],
                axis=0,
            ).astype(BF16)

    small_x = [
        remote(sm_part.at[x], sm_x.at[k], ms.at[k], mr.at[k], (x, p.e))
        for k, x in enumerate([p.xr, p.xl, p.x2])
    ]
    small_z = [
        remote(sm_z.at[p.z], sm_z.at[p.z], ms.at[2 + d], mr.at[2 + d], (p.x, p.peer((d, 0, 0))))
        for d in (1, 2, 3)
    ]
    small_y = [
        remote(sm_y.at[p.y], sm_y.at[p.y], ms.at[5 + d], mr.at[5 + d], (p.x, p.peer((0, d, 0))))
        for d in (1, 2, 3)
    ]
    small_c = [remote(sm_c.at[p.core], sm_c.at[p.core], ms.at[9], mr.at[9], p.sibling)]

    def total(ref, count):
        value = ref[0].astype(F32)
        for k in range(1, count):
            value += ref[k].astype(F32)
        return value

    planes[1].start_a(scatters[1])
    planes[2].start_a(scatters[2])
    planes[0].start_a(scatters[0])
    for c in sends:
        c.wait_recv()
    own_y.wait()
    combine(0)
    combine(1)
    planes[1].start_b()
    planes[2].start_b()
    combine(2)
    combine(3)
    planes[0].start_b()
    planes[1].start_back_b()
    planes[2].start_back_b()
    route_back()
    for c in small_x:
        c.start()
    planes[1].start_back_a()
    planes[2].start_back_a()
    planes[0].start_back_b()
    sgate.relay()
    for c in small_x:
        c.wait_recv()
    sm_z[p.z] = (sm_part[p.x].astype(F32) + total(sm_x, 3)).astype(BF16)
    for c in small_z:
        c.start()
    planes[0].start_back_a()
    for c in small_z:
        c.wait_recv()
    sm_y[p.y] = total(sm_z, 4).astype(BF16)
    for c in small_y:
        c.start()
    sgate.arrived()
    for half in range(2):
        g_gate[half * HALF : (half + 1) * HALF, :] = sgate.result(half).astype(BF16)
    for c in small_y:
        c.wait_recv()
    sm_c[p.core] = total(sm_y, 4).astype(BF16)
    for c in small_c:
        c.start()
    planes[1].start_pass()
    planes[2].start_pass()
    planes[0].start_pass()
    for c in small_c:
        c.wait_recv()
    out_small[...] = total(sm_c, 2)

    for c in sends + small_x + small_z + small_y + small_c:
        c.wait_send()
    for g in pairs + scatters + planes + [sgate]:
        g.finish()


def back(
    tokens, cotangent, posm, share, small_all, n1, q, kv, o, r, dr_rows, y_rows, wq, wkv, wo, gate
):
    D = MODEL_WIDTH
    cosine, sine = rope_tables()

    def arr(shape, dtype=BF16):
        return jax.ShapeDtypeStruct(shape, dtype)

    vm = pl.BlockSpec(memory_space=VMEM)
    hb = pl.BlockSpec(memory_space=ANY)
    sem = pltpu.SemaphoreType.DMA
    widths = (D, WIDE, WIDE)
    return pl.pallas_call(
        back_kernel,
        out_shape=[
            arr((SEQ, D)), arr((SEQ, D), F32), arr((SHARD, D)), arr((SHARD, WIDE)), arr((SHARD, WIDE)),
            arr((48, SHARD), F32), arr((SHARD, FF)),
        ],
        in_specs=[vm] * 12 + [hb] * 6,
        out_specs=[vm] * 7,
        scratch_shapes=[
            VMEM((2, GROUP, CAP, D), BF16),
            VMEM((EXPERTS, CAP, D), BF16),
            VMEM((D, D), BF16),
            VMEM((D, 2 * KV), BF16),
            VMEM((D, D), BF16),
            VMEM((SEQ, D), F32),
            VMEM((SEQ, D), BF16),
            VMEM((SEQ, D), BF16),
            VMEM((SEQ, WIDE), BF16),
            VMEM((SEQ, WIDE), BF16),
            VMEM((EXPERTS, SEQ), F32),
            VMEM((6, HALF, FF), BF16),
            *[VMEM((D, w), BF16) for w in widths],
            *[VMEM((4, HALF, w), BF16) for w in widths],
            *[VMEM((6, HALF // 2, w), BF16) for w in widths],
            *[VMEM((HALF, w), BF16) for w in widths],
            *[VMEM((HALF, w // 4), BF16) for w in widths],
            *[VMEM((3, HALF, w // 4), BF16) for w in widths],
            *[VMEM((3, HALF // 4, w // 4), BF16) for w in widths],
            VMEM((4, 48, SHARD), BF16),
            VMEM((3, 48, SHARD), BF16),
            VMEM((4, 48, SHARD), BF16),
            VMEM((4, 48, SHARD), BF16),
            VMEM((2, 48, SHARD), BF16),
            sem((31,)),
            sem((31,)),
            sem((3, 4)),
            sem((3, 4)),
            sem((3, 6)),
            sem((3, 6)),
            sem((6,)),
            sem((6,)),
            sem((3, 13)),
            sem((3, 13)),
            sem((10,)),
            sem((10,)),
            sem((10,)),
        ],
        compiler_params=pltpu.CompilerParams(
            collective_id=1, has_side_effects=True, vmem_limit_bytes=LIMIT
        ),
        name="back",
    )(
        tokens, cotangent, posm, share, small_all, n1, q, kv, o, r,
        jnp.asarray(cosine), jnp.asarray(sine), dr_rows, y_rows, wq, wkv, wo, gate,
    )


def finish_kernel(mixed, tokens, q, o, r, gate, up, down, small, mixed_, tokens_, q_, k_, v_, o_, gate_, up_, down_, router_, one_, two_):
    mixed_[...] = mixed[...]
    tokens_[...] = tokens[...]
    q_[:, :WIDE] = q[...].astype(F32)
    q_[:, WIDE:] = r[:, 2 * KV :].astype(F32)
    o_[...] = o[...].astype(F32)
    k_[...] = r[:, :KV].astype(F32)
    v_[...] = r[:, KV : 2 * KV].astype(F32)
    gate_[0] = gate[...].astype(F32)
    up_[0] = up[...].astype(F32)
    down_[0] = down[...].astype(F32)
    router_[...] = small[0:32, :]
    one_[...] = small[32, :]
    two_[...] = small[33, :]


def finish(mixed, tokens, q, o, r, gate, up, down, small):
    steps = 4

    def tall(count, width):
        return pl.BlockSpec((count // steps, width), lambda i: (i, 0))

    def owned():
        return pl.BlockSpec((1, SHARD // steps, FF), lambda i: (0, i, 0))

    def arr(*shape, dtype=F32):
        return jax.ShapeDtypeStruct(shape, dtype)

    D = MODEL_WIDTH
    return pl.pallas_call(
        finish_kernel,
        grid=(steps,),
        in_specs=[
            tall(SEQ, D), tall(SEQ, D), tall(SHARD, WIDE), tall(SHARD, D), tall(SHARD, WIDE),
            tall(SHARD, FF), tall(SHARD, FF), tall(SHARD, FF), pl.BlockSpec((48, SHARD), lambda i: (0, 0)),
        ],
        out_specs=[
            tall(SEQ, D), tall(SEQ, D), tall(SHARD, D), tall(SHARD, KV), tall(SHARD, KV), tall(SHARD, D),
            owned(), owned(), owned(), pl.BlockSpec((EXPERTS, SHARD), lambda i: (0, 0)),
            pl.BlockSpec((SHARD,), lambda i: (0,)), pl.BlockSpec((SHARD,), lambda i: (0,)),
        ],
        out_shape=[
            arr(SEQ, D, dtype=BF16), arr(SEQ, D), arr(SHARD, D), arr(SHARD, KV), arr(SHARD, KV), arr(SHARD, D),
            arr(1, SHARD, FF), arr(1, SHARD, FF), arr(1, SHARD, FF), arr(EXPERTS, SHARD),
            arr(SHARD), arr(SHARD),
        ],
        compiler_params=pltpu.CompilerParams(vmem_limit_bytes=LIMIT),
        name="finish",
    )(mixed, tokens, q, o, r, gate, up, down, small)


def pack_small(w_router, norm_one, norm_two):
    row = lax.broadcasted_iota(jnp.int32, (48, SHARD), 0)
    router = jnp.pad(w_router.T, ((0, 16), (0, 0)))
    gains = jnp.where(row == 32, norm_one[None, :], jnp.where(row == 33, norm_two[None, :], 0))
    return jnp.where(row < 32, router, gains).astype(BF16)


def shards(
    tokens, routes, w_query, key_matrix, value_matrix, w_output, norm_one, norm_two,
    w_router, w_gate, w_up, w_down, cotangent,
):
    small = pack_small(w_router, norm_one, norm_two)
    (_, dr_rows, y_rows, fq, fkv, fo, gate, small_all, posm, share, n1, q, kv, o, r, g_up, g_down) = forth(
        tokens, cotangent, routes.T, small, w_query, key_matrix, value_matrix, w_output,
        w_gate[0], w_up[0], w_down[0],
    )
    mixed, g_tokens, g_o, g_q, g_r, g_small, g_gate = back(
        tokens, cotangent, posm, share, small_all, n1, q, kv, o, r, dr_rows, y_rows, fq, fkv, fo, gate
    )
    mixed, g_tokens, g_q, g_k, g_v, g_o, g_gate, g_up, g_down, g_router, g_one, g_two = finish(
        mixed, g_tokens, g_q, g_o, g_r, g_gate, g_up, g_down, g_small
    )
    return (
        mixed, g_tokens, g_q, g_k, g_v, g_o, g_one, g_two, g_router.T, g_gate, g_up, g_down
    )


def solution(mesh):
    rows_split = P(("dp", "expert"), None)
    flat = P("dp", None)
    vector = P("dp")
    owned = P("expert", "dp", None)
    return jax.shard_map(
        shards,
        mesh=mesh,
        in_specs=(
            rows_split, rows_split, flat, flat, flat, flat, vector, vector, flat, owned, owned, owned,
            rows_split,
        ),
        out_specs=(
            rows_split, rows_split, flat, flat, flat, flat, vector, vector, flat, owned, owned, owned,
        ),
        check_vma=False,
    )
```

```python
import functools
import itertools

import jax
import jax.numpy as jnp
import numpy as np
from jax import lax
from jax.experimental import pallas as pl
from jax.experimental.pallas import tpu as pltpu
from jax.sharding import PartitionSpec as P

MODEL_WIDTH = 1536
QUERY_HEADS = 12
KEY_VALUE_HEADS = 2
HEAD_SIZE = 128
TOPK = 4
SEQ = 256
EXPERTS = 32
CAP = 40
FF = 768
KV = KEY_VALUE_HEADS * HEAD_SIZE
SHARD = MODEL_WIDTH // 4
HALF = SHARD // 2
QUARTER = HALF // 2
EPSILON = 1e-06
ROPE_BASE = 10000.0
SCALE = HEAD_SIZE ** (-0.5)
MESH = pl.DeviceIdType.MESH
F32 = jnp.float32
BF16 = jnp.bfloat16
VMEM = pltpu.VMEM
ANY = pl.ANY
LIMIT = 60 * 1024 * 1024


def _offsets():
    def far(a):
        return min(a, 4 - a)

    def spread(core):
        every = [(z, y, core) for z in range(4) for y in range(4) if (z, y, core) != (0, 0, 0)]
        every = sorted(every, key=lambda o: (far(o[0]) + far(o[1]), o), reverse=True)
        groups, taken = [], set()
        for z, y, _ in every:
            group = []
            for o in ((z, y), (-z % 4, -y % 4), (y, z), (-y % 4, -z % 4)):
                if o not in taken:
                    taken.add(o)
                    group.append((*o, core))
            if group:
                groups.append(group)
        order = []
        while groups:
            order += groups.pop(0)
            if groups:
                order += groups.pop()
        return order

    return spread(0) + spread(1)


OFFSETS = _offsets()


def rope_tables():
    position = np.arange(SEQ, dtype=np.float32)
    frequency = (
        np.float32(ROPE_BASE) ** (-np.arange(64, dtype=np.float32) * np.float32(2.0 / HEAD_SIZE))
    ).astype(np.float32)
    angles = (position[:, None] * frequency[None, :]).astype(np.float32)
    cosine = np.cos(angles.astype(np.float64)).astype(np.float32)
    sine = np.sin(angles.astype(np.float64)).astype(np.float32)
    return (
        np.concatenate([cosine, cosine], axis=1),
        np.concatenate([-sine, sine], axis=1),
    )


def mm(left, right, left_dim=1, right_dim=0):
    return lax.dot_general(
        left, right, (((left_dim,), (right_dim,)), ((), ())), preferred_element_type=F32
    )


class Place:
    def __init__(self):
        self.x = lax.axis_index("dp")
        self.e = lax.axis_index("expert")
        self.core = lax.rem(self.e, 2)
        self.y = lax.rem(self.e // 2, 4)
        self.z = self.e // 8
        self.xl = lax.rem(self.x + 3, 4)
        self.xr = lax.rem(self.x + 1, 4)
        self.x2 = lax.rem(self.x + 2, 4)
        self.left = (self.xl, self.e)
        self.right = (self.xr, self.e)
        self.across = (self.x2, self.e)
        self.sibling = (self.x, self.e + 1 - 2 * self.core)

    def peer(self, offset):
        dz, dy, dc = offset
        return (
            lax.rem(self.z + dz, 4) * 8 + lax.rem(self.y + dy, 4) * 2 + lax.rem(self.core + dc, 2)
        )

    def peers(self):
        return [self.peer(o) for o in OFFSETS]


def greet(devices):
    barrier = pltpu.get_barrier_semaphore()
    for d in devices:
        pl.semaphore_signal(barrier, inc=1, device_id=d, device_id_type=MESH)
    return barrier


def remote(src, dst, send, recv, device):
    return pltpu.make_async_remote_copy(
        src_ref=src, dst_ref=dst, send_sem=send, recv_sem=recv, device_id=device, device_id_type=MESH
    )


def rows(start, count, align=16):
    return pl.ds(pl.multiple_of(start, align), count)


class Gather:
    def __init__(self, place, shard, region, send, recv):
        p = place
        half = p.core * HALF

        def move(k, src, dst, device):
            return remote(src, dst, send.at[k], recv.at[k], device)

        mine = shard.at[rows(half, HALF, 32)]
        self.direct = [
            move(0, mine, region(p.x, half, HALF), p.right),
            move(1, mine, region(p.x, half, HALF), p.left),
        ]
        from_left = region(p.xl, half, QUARTER)
        from_right = region(p.xr, half + QUARTER, QUARTER)
        self.forward = [
            move(2, from_left, from_left, p.right),
            move(3, from_right, from_right, p.left),
        ]
        whole_left = region(p.xl, half, HALF)
        whole_right = region(p.xr, half, HALF)
        far_one = region(p.x2, half, QUARTER)
        far_two = region(p.x2, half + QUARTER, QUARTER)
        self.near = [
            move(4, whole_left, whole_left, p.sibling),
            move(5, whole_right, whole_right, p.sibling),
        ]
        self.far = [
            move(6, far_one, far_one, p.sibling),
            move(7, far_two, far_two, p.sibling),
        ]

    def start(self):
        for c in self.direct:
            c.start()

    def relay(self):
        for k in range(2):
            self.direct[k].wait_recv()
            self.forward[k].start()
            self.near[k].start()

    def relay_far(self):
        for k in range(2):
            self.forward[k].wait_recv()
            self.far[k].start()

    def arrived_near(self):
        for c in self.near:
            c.wait_recv()

    def arrived_far(self):
        for c in self.far:
            c.wait_recv()

    def finish(self):
        for c in self.direct + self.forward + self.near + self.far:
            c.wait_send()


def slot_rows(posm_ref, first, count):
    slot = lax.broadcasted_iota(jnp.int32, (CAP, SEQ), 0).astype(F32)
    return [
        jnp.where(posm_ref[pl.ds(first + j, 1), :] == slot, 1.0, 0.0) for j in range(count)
    ]


def turn(values, cosine, sine):
    return values * cosine + pltpu.roll(values, 64, 1) * sine


def turn_back(values, cosine, sine):
    return values * cosine - pltpu.roll(values, 64, 1) * sine


def softmax_parts(q_head, k_head, causal):
    scores = mm(q_head, k_head, 1, 1) * SCALE
    scores = jnp.where(causal, scores, -jnp.inf)
    largest = jnp.max(scores, axis=-1, keepdims=True)
    exponent = jnp.exp(scores - largest)
    return exponent / jnp.sum(exponent, axis=-1, keepdims=True)


def causal_mask():
    row = lax.broadcasted_iota(jnp.int32, (SEQ, SEQ), 0)
    column = lax.broadcasted_iota(jnp.int32, (SEQ, SEQ), 1)
    return column <= row


def norm_back(v, gain, grad):
    scale = lax.rsqrt(jnp.mean(v * v, axis=-1, keepdims=True) + EPSILON)
    unit = v * scale
    w = grad * gain
    return (
        (w - unit * jnp.mean(w * unit, axis=-1, keepdims=True)) * scale,
        jnp.sum(grad * unit, axis=0, keepdims=True),
    )


def gelu_parts(a):
    inner = jnp.tanh(0.7978845608028654 * (a + 0.044715 * a * a * a))
    value = 0.5 * a * (1.0 + inner)
    slope = 0.5 * (1.0 + inner) + 0.5 * a * (1.0 - inner * inner) * 0.7978845608028654 * (
        1.0 + 3.0 * 0.044715 * a * a
    )
    return value, slope


class GatherOwn:
    def __init__(self, place, shard, region, send, recv):
        p = place

        def move(k, src, dst, device):
            return remote(src, dst, send.at[k], recv.at[k], device)

        self.direct = [
            move(0, shard, region(p.x, 0, SHARD), p.right),
            move(1, shard, region(p.x, 0, SHARD), p.left),
        ]
        from_left = region(p.xl, 0, HALF)
        from_right = region(p.xr, HALF, HALF)
        self.forward = [
            move(2, from_left, from_left, p.right),
            move(3, from_right, from_right, p.left),
        ]

    def start(self):
        for c in self.direct:
            c.start()

    def relay(self):
        for k in range(2):
            self.direct[k].wait_recv()
            self.forward[k].start()

    def arrived(self):
        for c in self.forward:
            c.wait_recv()

    def finish(self):
        for c in self.direct + self.forward:
            c.wait_send()


class Scatter:
    def __init__(self, place, partial, landing, send, recv, first=0, height=SHARD, width=None):
        p = self.p = place
        half = height // 2
        self.partial, self.landing, self.first, self.height = partial, landing, first, height
        self.cut = cut = pl.ds(0, width or partial.shape[1])

        def region(x, part):
            return partial.at[rows(x * SHARD + first + part * half, half, 32), cut]

        def move(k, src, device):
            return remote(src, landing.at[k], send.at[k], recv.at[k], device)

        self.far = [move(0, region(p.x2, 0), p.right), move(1, region(p.x2, 1), p.left)]
        self.near = [move(2, region(p.xr, 1), p.right), move(3, region(p.xl, 0), p.left)]
        self.summed = [move(4, region(p.xr, 0), p.right), move(5, region(p.xl, 1), p.left)]

    def relay(self):
        p, half = self.p, self.height // 2
        for k, x, part in ((0, p.xr, 0), (1, p.xl, 1)):
            self.far[k].wait_recv()
            where = rows(x * SHARD + self.first + part * half, half, 32)
            self.partial[where, self.cut] = (
                self.partial[where, self.cut].astype(F32) + self.landing[k].astype(F32)
            ).astype(BF16)
            self.summed[k].start()

    def result(self, part):
        p, half = self.p, self.height // 2
        own = self.partial[rows(p.x * SHARD + self.first + part * half, half, 32), self.cut]
        one, two = ((4, 3), (2, 5))[part]
        return (
            own.astype(F32)
            + self.landing[one].astype(F32)
            + self.landing[two].astype(F32)
        )

    def arrived(self):
        for c in self.near + self.summed:
            c.wait_recv()

    def finish(self):
        for c in self.far + self.near + self.summed:
            c.wait_send()


GROUP = 8
BLOCK = GROUP * CAP


def flatten(slots):
    return slots.astype(F32).reshape(BLOCK, MODEL_WIDTH).astype(BF16)


def unflatten(values):
    return values.reshape(GROUP, CAP, MODEL_WIDTH).astype(BF16)


def forth_kernel(
    tokens, cotangent, routes, small, cosine, sine, wq, wk, wv, wo, wgate, wup, wdown,
    dy_in, dr_in, y_out, wq_full, wkv_full, wo_full, gate_out, n1_out, q_out, kv_out, o_out, r_out,
    small_all, posm, share, dots_in, g_up, g_down,
    buf_a, buf_b, landing, dyflat, wqf, wkvf, wof, wgu, wd, hid, part_down, part_gate, part_up, land_down, land_up,
    n1, q, kv, o, r, n2, qacc, kvacc, dots,
    ag, ag_r, sg, sg_r, ds_, dr_, gs, gr, ns, nr, bs, br, cs, cr, ss, sr, ls,
):
    p = Place()
    peers = p.peers()
    sources = [p.peer(tuple((-v) % m for v, m in zip(o_, (4, 4, 2)))) for o_ in OFFSETS]
    barrier = greet([p.left, p.right, p.across] + [(p.x, t) for t in peers])

    def columns(full, first, count):
        return lambda x, start, height: full.at[
            rows(x * SHARD + start, height, 32), pl.ds(first, count)
        ]

    at_q = columns(wqf, 0, MODEL_WIDTH)
    at_k = columns(wkvf, 0, KV)
    at_v = columns(wkvf, KV, KV)
    at_o = columns(wof, 0, MODEL_WIDTH)
    at_gate = columns(wgu, 0, FF)
    at_up = columns(wgu, FF, FF)
    at_down = columns(wd, 0, FF)
    mine = [
        pltpu.make_async_copy(w, f(p.x, 0, SHARD), ls.at[k])
        for k, (w, f) in enumerate(
            [
                (wq, at_q), (wk, at_k), (wv, at_v), (wo, at_o),
                (wgate, at_gate), (wup, at_up), (wdown, at_down),
            ]
        )
    ]
    for c in mine:
        c.start()

    lane = lax.broadcasted_iota(jnp.int32, (EXPERTS, SEQ), 0)
    named = routes[0:1, :] == lane
    for j in range(1, TOPK):
        named = jnp.logical_or(named, routes[j : j + 1, :] == lane)
    earlier = (
        lax.broadcasted_iota(jnp.int32, (SEQ, SEQ), 0)
        < lax.broadcasted_iota(jnp.int32, (SEQ, SEQ), 1)
    ).astype(F32).astype(BF16)
    place_of = mm(named.astype(F32).astype(BF16), earlier)
    posm[...] = jnp.where(named, place_of, -1.0)

    small_all[p.x] = small[...]
    pl.semaphore_wait(barrier, len(peers) + 3)

    small_moves = [
        remote(small, small_all.at[p.x], sg.at[k], sg_r.at[k], d)
        for k, d in enumerate([p.right, p.left, p.across])
    ]
    for c in small_moves:
        c.start()
    gq, gk, gv, go = [
        Gather(p, w, f, ag.at[k], ag_r.at[k])
        for k, (w, f) in enumerate([(wq, at_q), (wk, at_k), (wv, at_v), (wo, at_o)])
    ]
    for g in (gq, gk, gv):
        g.start()

    for c in small_moves:
        c.wait_recv()
    logits = mm(small_all[0, 0:32, :], tokens[:, 0:SHARD], 1, 1)
    for s in range(1, 4):
        logits += mm(small_all[s, 0:32, :], tokens[:, s * SHARD : (s + 1) * SHARD], 1, 1)
    top = jnp.max(jnp.where(named, logits, -jnp.inf), axis=0, keepdims=True)
    weight = jnp.where(named, jnp.exp(jnp.minimum(logits - top, 0.0)), 0.0)
    share[...] = weight / jnp.sum(weight, axis=0, keepdims=True)

    places = peers + [p.e]
    dy_sends = [
        remote(buf_a.at[k], dy_in.at[k], ds_.at[k], dr_.at[k], (p.x, t))
        for k, t in enumerate(peers)
    ]
    own_dy = pltpu.make_async_copy(buf_a.at[31], dy_in.at[31], ls.at[7])
    for i in range(0, EXPERTS, 4):
        hot = [slot_rows(posm, t, 1)[0] for t in places[i : i + 4]]
        gain = jnp.concatenate(
            [
                jnp.sum(b * share[pl.ds(t, 1), :], axis=-1, keepdims=True)
                for t, b in zip(places[i : i + 4], hot)
            ],
            axis=0,
        )
        picked = mm(jnp.concatenate(hot, axis=0).astype(BF16), cotangent[...])
        buf_a[i : i + 4] = (picked * gain).reshape(4, CAP, MODEL_WIDTH).astype(BF16)
        for c in dy_sends[i : i + 4]:
            c.start()
    own_dy.start()

    x = tokens[...].astype(F32)
    unit = x * lax.rsqrt(jnp.mean(x * x, axis=-1, keepdims=True) + EPSILON)
    for s in range(4):
        cut = slice(s * SHARD, (s + 1) * SHARD)
        n1[:, cut] = (unit[:, cut] * small_all[s, 32:33, :].astype(F32)).astype(BF16)
    saves = [
        pltpu.make_async_copy(a, b, ls.at[16 + k])
        for k, (a, b) in enumerate([(n1, n1_out), (q, q_out), (kv, kv_out), (o, o_out), (r, r_out)])
    ]
    saves[0].start()

    def part(x_index):
        return n1[:, rows(x_index * SHARD, SHARD, 128)]

    def block(full, x_index):
        return full[rows(x_index * SHARD, SHARD, 128), :]

    for c in mine[:3]:
        c.wait()
    qacc[...] = mm(part(p.x), block(wqf, p.x))
    kvacc[...] = mm(part(p.x), block(wkvf, p.x))
    for g in (gq, gk, gv):
        g.relay()
    go.start()
    for g in (gq, gk, gv):
        g.arrived_near()
    for s in (p.xl, p.xr):
        qacc[...] += mm(part(s), block(wqf, s))
        kvacc[...] += mm(part(s), block(wkvf, s))
    for g in (gq, gk, gv):
        g.relay_far()
    for g in (gq, gk, gv):
        g.arrived_far()
    qacc[...] += mm(part(p.x2), block(wqf, p.x2))
    kvacc[...] += mm(part(p.x2), block(wkvf, p.x2))
    keep = [
        pltpu.make_async_copy(f, out, ls.at[8 + k])
        for k, (f, out) in enumerate([(wqf, wq_full), (wkvf, wkv_full), (wof, wo_full)])
    ]
    keep[0].start()
    keep[1].start()

    cos = cosine[...]
    sin = sine[...]
    for h in range(KEY_VALUE_HEADS):
        cut = slice(h * HEAD_SIZE, (h + 1) * HEAD_SIZE)
        kv[:, cut] = turn(kvacc[:, cut], cos, sin).astype(BF16)
        cut = slice(KV + h * HEAD_SIZE, KV + (h + 1) * HEAD_SIZE)
        kv[:, cut] = kvacc[:, cut].astype(BF16)
    causal = causal_mask()
    for h in range(QUERY_HEADS):
        cut = slice(h * HEAD_SIZE, (h + 1) * HEAD_SIZE)
        c = h // (QUERY_HEADS // KEY_VALUE_HEADS)
        q_head = turn(qacc[:, cut], cos, sin).astype(BF16)
        q[:, cut] = q_head
        weights = softmax_parts(q_head, kv[:, c * HEAD_SIZE : (c + 1) * HEAD_SIZE], causal)
        o[:, cut] = mm(
            weights.astype(BF16), kv[:, KV + c * HEAD_SIZE : KV + (c + 1) * HEAD_SIZE]
        ).astype(BF16)

    for c in saves[1:4]:
        c.start()

    def opart(x_index):
        return o[:, rows(x_index * SHARD, SHARD, 128)]

    for c in mine[3:]:
        c.wait()
    r[...] = tokens[...].astype(F32) + mm(opart(p.x), block(wof, p.x))
    go.relay()
    ggate = GatherOwn(p, wgate, at_gate, gs.at[0], gr.at[0])
    gup = GatherOwn(p, wup, at_up, gs.at[1], gr.at[1])
    gdown = GatherOwn(p, wdown, at_down, gs.at[2], gr.at[2])
    ggate.start()
    gup.start()
    go.arrived_near()
    for s in (p.xl, p.xr):
        r[...] += mm(opart(s), block(wof, s))
    go.relay_far()
    go.arrived_far()
    keep[2].start()
    residual = r[...] + mm(opart(p.x2), block(wof, p.x2))
    r[...] = residual
    saves[4].start()
    unit = residual * lax.rsqrt(jnp.mean(residual * residual, axis=-1, keepdims=True) + EPSILON)
    for s in range(4):
        cut = slice(s * SHARD, (s + 1) * SHARD)
        n2[:, cut] = (unit[:, cut] * small_all[s, 33:34, :].astype(F32)).astype(BF16)

    sends = [
        remote(buf_b.at[k], landing.at[k], ns.at[k], nr.at[k], (p.x, t))
        for k, t in enumerate(peers)
    ]
    own_rows = pltpu.make_async_copy(buf_b.at[31], landing.at[31], ls.at[11])
    for i in range(0, EXPERTS, 4):
        hot = [slot_rows(posm, t, 1)[0] for t in places[i : i + 4]]
        picked = mm(jnp.concatenate(hot, axis=0).astype(BF16), n2[...])
        buf_b[i : i + 4] = picked.reshape(4, CAP, MODEL_WIDTH).astype(BF16)
        for c in sends[i : i + 4]:
            c.start()
    own_rows.start()

    ggate.relay()
    gup.relay()
    gdown.start()
    for c in dy_sends:
        c.wait()
    own_dy.wait()
    load_dy = pltpu.make_async_copy(dy_in, buf_a, ls.at[12])
    load_dy.start()
    for g in (gq, gk, gv, go):
        g.finish()
    for c in small_moves:
        c.wait_send()
    for c in keep:
        c.wait()
    rflat = wof
    dab = wqf
    load_dy.wait()

    @pl.loop(0, 4)
    def _(i):
        dyflat[rows(i * BLOCK, BLOCK), :] = flatten(buf_a[pl.ds(i * GROUP, GROUP)])

    ggate.arrived()
    gup.arrived()

    def forward(i):
        if i == 3:
            own_rows.wait()
        for c in sends[i * GROUP : (i + 1) * GROUP]:
            c.wait_recv()
        cut = slice(i * BLOCK, (i + 1) * BLOCK)
        rflat[cut, :] = flatten(landing[i * GROUP : (i + 1) * GROUP])
        ab = mm(rflat[cut, :], wgu[...])
        value, slope = gelu_parts(ab[:, :FF])
        b = ab[:, FF:]
        hid[cut, :] = (value * b).astype(BF16)
        dab[cut, :FF] = (slope * b).astype(BF16)
        dab[cut, FF:] = value.astype(BF16)

    backs = [
        remote(buf_a.at[k], dr_in.at[p.e], bs.at[k], br.at[k], (p.x, sources[k])) for k in range(31)
    ]

    def backward(i):
        cut = slice(i * BLOCK, (i + 1) * BLOCK)
        dh = mm(dyflat[cut, :], wd[...])
        dab[cut, :FF] = (dh * dab[cut, :FF].astype(F32)).astype(BF16)
        dab[cut, FF:] = (dh * dab[cut, FF:].astype(F32)).astype(BF16)
        buf_a[i * GROUP : (i + 1) * GROUP] = unflatten(mm(dab[cut, :], wgu[...], 1, 1))
        for c in backs[i * GROUP : (i + 1) * GROUP]:
            c.start()

    forward(0)
    forward(1)
    gdown.relay()
    forward(2)
    gdown.arrived()
    backward(0)
    backward(1)
    backward(2)
    forward(3)
    backward(3)
    own_back = pltpu.make_async_copy(buf_a.at[31], dr_in.at[p.e], ls.at[13])
    own_back.start()

    sdown = Scatter(p, part_down, land_down, ss.at[0], sr.at[0])
    sup = Scatter(p, part_up, land_up, ss.at[1], sr.at[1])

    def down_block(x):
        where = rows(x * SHARD, SHARD, 128)
        part_down[where, :] = mm(dyflat[:, where], hid[...], 0, 0).astype(BF16)

    def gate_up_block(x):
        where = rows(x * SHARD, SHARD, 128)
        both = mm(rflat[0 : EXPERTS * CAP, where], dab[0 : EXPERTS * CAP, :], 0, 0)
        part_gate[where, :] = both[:, :FF].astype(BF16)
        part_up[where, :] = both[:, FF:].astype(BF16)

    def start_scatter(scatter, fill):
        fill(p.x2)
        for c in scatter.far:
            c.start()
        fill(p.xr)
        scatter.near[0].start()
        fill(p.xl)
        scatter.near[1].start()
        fill(p.x)

    start_scatter(sdown, down_block)
    start_scatter(sup, gate_up_block)
    keep_gate = pltpu.make_async_copy(part_gate, gate_out, ls.at[15])
    keep_gate.start()
    sdown.relay()

    for c in sends:
        c.wait_send()
    back_dots = [
        remote(dots.at[k], dots_in.at[k], cs.at[k], cr.at[k], (p.x, sources[k])) for k in range(31)
    ]
    diagonal = lax.broadcasted_iota(jnp.int32, (CAP, 128), 0) == lax.broadcasted_iota(
        jnp.int32, (CAP, 128), 1
    )
    for i in range(4):
        cut = slice(i * BLOCK, (i + 1) * BLOCK)
        y = mm(hid[cut, :], wd[...], 1, 1)
        buf_b[i * GROUP : (i + 1) * GROUP] = unflatten(y)
        products = dyflat[cut, :].astype(F32) * y.astype(BF16).astype(F32)
        column = jnp.sum(products, axis=-1, keepdims=True)
        for j in range(GROUP):
            line = jnp.where(diagonal, column[j * CAP : (j + 1) * CAP], 0.0)
            line = jnp.sum(line, axis=0, keepdims=True)
            dots[i * GROUP + j] = jnp.broadcast_to(line, (8, 128))
        for c in back_dots[i * GROUP : (i + 1) * GROUP]:
            c.start()
    dots_in[31] = dots[31]
    keep_y = pltpu.make_async_copy(buf_b, y_out, ls.at[14])
    keep_y.start()

    sup.relay()
    sdown.arrived()
    for half in range(2):
        g_down[half * HALF : (half + 1) * HALF, :] = sdown.result(half).astype(BF16)
    sup.arrived()
    for half in range(2):
        g_up[half * HALF : (half + 1) * HALF, :] = sup.result(half).astype(BF16)

    keep_gate.wait()
    for c in saves:
        c.wait()
    for c in backs + back_dots:
        c.wait()
    own_back.wait()
    keep_y.wait()
    for g in (ggate, gup, gdown, sdown, sup):
        g.finish()


def forth(tokens, cotangent, routes, small, wq, wk, wv, wo, wgate, wup, wdown):
    cosine, sine = rope_tables()
    D = MODEL_WIDTH

    def arr(shape, dtype=BF16):
        return jax.ShapeDtypeStruct(shape, dtype)

    vm = pl.BlockSpec(memory_space=VMEM)
    hb = pl.BlockSpec(memory_space=ANY)
    sem = pltpu.SemaphoreType.DMA
    N = EXPERTS * CAP
    slots = (EXPERTS, CAP, D)
    return pl.pallas_call(
        forth_kernel,
        out_shape=[
            arr(slots), arr(slots), arr(slots), arr((D, D)), arr((D, 2 * KV)), arr((D, D)), arr((D, FF)),
            arr((SEQ, D)), arr((SEQ, D)), arr((SEQ, 2 * KV)), arr((SEQ, D)), arr((SEQ, D), F32),
            arr((4, 48, SHARD)), arr((EXPERTS, SEQ), F32), arr((EXPERTS, SEQ), F32),
            arr((EXPERTS, 8, 128), F32),
            arr((SHARD, FF)), arr((SHARD, FF)),
        ],
        in_specs=[vm] * 6 + [hb] * 7,
        out_specs=[hb] * 12 + [vm] * 6,
        scratch_shapes=[
            VMEM(slots, BF16),
            VMEM(slots, BF16),
            VMEM(slots, BF16),
            VMEM((N, D), BF16),
            VMEM((D, D), BF16),
            VMEM((D, 2 * KV), BF16),
            VMEM((D, D), BF16),
            VMEM((D, 2 * FF), BF16),
            VMEM((D, FF), BF16),
            VMEM((N, FF), BF16),
            VMEM((D, FF), BF16),
            VMEM((D, FF), BF16),
            VMEM((D, FF), BF16),
            VMEM((6, HALF, FF), BF16),
            VMEM((6, HALF, FF), BF16),
            VMEM((SEQ, D), BF16),
            VMEM((SEQ, D), BF16),
            VMEM((SEQ, 2 * KV), BF16),
            VMEM((SEQ, D), BF16),
            VMEM((SEQ, D), F32),
            VMEM((SEQ, D), BF16),
            VMEM((SEQ, D), F32),
            VMEM((SEQ, 2 * KV), F32),
            VMEM((EXPERTS, 8, 128), F32),
            sem((4, 8)), sem((4, 8)), sem((3,)), sem((3,)), sem((31,)), sem((31,)),
            sem((3, 4)), sem((3, 4)), sem((31,)), sem((31,)), sem((31,)), sem((31,)),
            sem((31,)), sem((31,)), sem((2, 6)), sem((2, 6)), sem((21,)),
        ],
        compiler_params=pltpu.CompilerParams(
            collective_id=0, has_side_effects=True, vmem_limit_bytes=LIMIT
        ),
        name="forth",
    )(
        tokens, cotangent, routes, small, jnp.asarray(cosine), jnp.asarray(sine),
        wq, wk, wv, wo, wgate, wup, wdown,
    )


WIDE = 8 * HEAD_SIZE

class PairSum:
    def __init__(self, place, partial, landing, send, recv):
        p = place
        self.order = [p.x2, p.xr, p.xl, p.x]
        self.partial, self.landing = partial, landing
        self.half = p.core * HALF
        self.moves = [
            remote(
                partial.at[rows(x * SHARD + HALF - self.half, HALF, 32)],
                landing.at[i],
                send.at[i],
                recv.at[i],
                p.sibling,
            )
            for i, x in enumerate(self.order)
        ]

    def add(self, i):
        self.moves[i].wait_recv()
        where = rows(self.order[i] * SHARD + self.half, HALF, 32)
        self.partial[where, :] = (
            self.partial[where, :].astype(F32) + self.landing[i].astype(F32)
        ).astype(BF16)

    def finish(self):
        for c in self.moves:
            c.wait_send()


class PlaneSum:
    def __init__(self, place, current, piece, out, land_a, land_b, width, z_first, send, recv):
        p = self.p = place
        self.current, self.piece, self.out = current, piece, out
        self.land_a, self.land_b = land_a, land_b
        w = self.w = width // 4
        t = HALF // 4
        a, b = (p.z, p.y) if z_first else (p.y, p.z)
        self.a, self.b = a, b

        def along_a(d):
            return (p.x, p.peer((d, 0, 0) if z_first else (0, d, 0)))

        def along_b(d):
            return (p.x, p.peer((0, d, 0) if z_first else (d, 0, 0)))

        def cut(i):
            return pl.ds(pl.multiple_of(i * w, 128), w)

        self.cut_a = cut(a)
        self.rows_b = rows(b * t, t)
        base = p.core * HALF
        self.mine = (rows(base + b * t, t), cut(a))
        spot = out.at[rows(base + b * t, t), cut(a)]
        strip = out.at[rows(base, HALF, 32), cut(a)]
        whole = out.at[rows(base, HALF, 32)]
        steps = (1, 2, 3)
        self.step_a = [
            remote(
                current.at[:, cut(lax.rem(a + d, 4))],
                land_a.at[d - 1],
                send.at[d - 1],
                recv.at[d - 1],
                along_a(d),
            )
            for d in steps
        ]
        self.step_b = [
            remote(
                piece.at[rows(lax.rem(b + d, 4) * t, t)],
                land_b.at[d - 1],
                send.at[2 + d],
                recv.at[2 + d],
                along_b(d),
            )
            for d in steps
        ]
        self.back_b = [remote(spot, spot, send.at[5 + d], recv.at[5 + d], along_b(d)) for d in steps]
        self.back_a = [
            remote(strip, strip, send.at[8 + d], recv.at[8 + d], along_a(d)) for d in steps
        ]
        self.pass_on = [remote(whole, whole, send.at[12], recv.at[12], p.sibling)]

    def start_a(self, scatter):
        part = HALF // 2
        scatter.arrived()
        for k in range(2):
            self.current[k * part : (k + 1) * part, :] = scatter.result(k).astype(BF16)
        for c in self.step_a:
            c.start()

    def start_b(self):
        for c in self.step_a:
            c.wait_recv()
        total = self.current[:, self.cut_a].astype(F32)
        for k in range(3):
            total += self.land_a[k].astype(F32)
        self.piece[...] = total.astype(BF16)
        for c in self.step_b:
            c.start()

    def start_back_b(self):
        for c in self.step_b:
            c.wait_recv()
        total = self.piece[self.rows_b, :].astype(F32)
        for k in range(3):
            total += self.land_b[k].astype(F32)
        self.out[self.mine] = total.astype(BF16)
        for c in self.back_b:
            c.start()

    def start_back_a(self):
        for c in self.back_b:
            c.wait_recv()
        for c in self.back_a:
            c.start()

    def start_pass(self):
        for c in self.back_a:
            c.wait_recv()
        for c in self.pass_on:
            c.start()

    def finish(self):
        for c in self.pass_on:
            c.wait()
        for c in self.step_a + self.step_b + self.back_b + self.back_a:
            c.wait_send()


def gain_row(small_all, row):
    return jnp.concatenate(
        [small_all[s, row : row + 1, :].astype(F32) for s in range(4)], axis=1
    )


def back_kernel(
    posm, share, dots_in, small_all, cosine, sine,
    tokens_in, cotangent_in, n1_in, q_in, kv_in, o_in, r_in, dr_rows, y_rows, wq, wkv, wo, gate_rows,
    mixed_out, tokens_out, out_o, out_q, out_r, out_small, g_gate,
    mixed, g_tokens, tokens, cotangent, n1, q, kv, o, r,
    drv, y_in, wqv, wkvv, wov, acc, da, do, dqp, drp, dgate, land_gate,
    part_o, part_q, part_r, pair_o, pair_q, pair_r, land_o, land_q, land_r,
    cur_o, cur_q, cur_r, pc_o, pc_q, pc_r, la_o, la_q, la_r, lb_o, lb_q, lb_r,
    sm_part, sm_x, sm_z, sm_y, sm_c,
    ys, yr, ps, pr, ss, sr, es, er, ts, tr, ms, mr, ls,
):
    p = Place()
    peers = p.peers()
    sources = [p.peer(tuple((-v) % m for v, m in zip(o_, (4, 4, 2)))) for o_ in OFFSETS]
    barrier = greet([p.left, p.right, p.across] + [(p.x, t) for t in peers])
    loads = [
        pltpu.make_async_copy(s, d, ls.at[12 + k])
        for k, (s, d) in enumerate(
            [
                (wo, wov), (wq, wqv), (wkv, wkvv), (r_in, r), (cotangent_in, cotangent), (o_in, o),
                (q_in, q), (kv_in, kv), (n1_in, n1), (tokens_in, tokens),
            ]
        )
    ]
    groups = [
        pltpu.make_async_copy(
            dr_rows.at[pl.ds(i * GROUP, GROUP)], drv.at[i % 2], ls.at[6 + i]
        )
        for i in range(4)
    ]
    for c in groups[:2] + loads[3:6] + loads[:1] + loads[6:] + loads[1:3]:
        c.start()
    pl.semaphore_wait(barrier, len(peers) + 3)
    sends = [
        remote(y_rows.at[k], y_in.at[k], ys.at[k], yr.at[k], (p.x, sources[k]))
        for k in range(31)
    ]
    own_y = pltpu.make_async_copy(y_rows.at[31], y_in.at[31], ls.at[5])
    own_y.start()
    places = peers + [p.e]

    def send_y(first, end):
        for c in sends[first:end]:
            c.start()

    send_y(0, 18)

    for i in range(4):
        groups[i].wait()
        hot = jnp.concatenate(slot_rows(posm, i * GROUP, GROUP), axis=0).astype(BF16)
        term = mm(hot, flatten(drv[i % 2]), 0, 0)
        if i < 2:
            groups[i + 2].start()
        if i == 0:
            acc[...] = term
        else:
            acc[...] += term
    for c in loads[3:5]:
        c.wait()
    back, g_two = norm_back(r[...], gain_row(small_all, 33), acc[...])
    dr = cotangent[...].astype(F32) + back
    g_tokens[...] = dr
    da[...] = dr.astype(BF16)

    names = ((part_o, pair_o, land_o), (part_q, pair_q, land_q), (part_r, pair_r, land_r))
    pairs = [PairSum(p, a, b, ps.at[k], pr.at[k]) for k, (a, b, _) in enumerate(names)]
    scatters = [
        Scatter(p, a, c, ss.at[k], sr.at[k], p.core * HALF, HALF)
        for k, (a, _, c) in enumerate(names)
    ]

    def blocks(k, left, right):
        for i, x in enumerate(pairs[k].order):
            where = rows(x * SHARD, SHARD, 128)
            names[k][0][where, :] = mm(left[:, where], right[...], 0, 0).astype(BF16)
            pairs[k].moves[i].start()

    def sum_pairs(k):
        pairs[k].add(0)
        for c in scatters[k].far:
            c.start()
        pairs[k].add(1)
        scatters[k].near[0].start()
        pairs[k].add(2)
        scatters[k].near[1].start()
        pairs[k].add(3)

    loads[5].wait()
    blocks(0, o, da)
    sum_pairs(0)
    loads[0].wait()
    do[...] = mm(da[...], wov[...], 1, 1).astype(BF16)
    part_gate = wov
    load_gate = pltpu.make_async_copy(gate_rows, part_gate.at[:, pl.ds(0, FF)], ls.at[4])
    load_gate.start()

    loads[6].wait()
    loads[7].wait()
    cos = cosine[...]
    sin = sine[...]
    causal = causal_mask()
    group = QUERY_HEADS // KEY_VALUE_HEADS
    for c in range(KEY_VALUE_HEADS):
        k_cut = slice(c * HEAD_SIZE, (c + 1) * HEAD_SIZE)
        v_cut = slice(KV + c * HEAD_SIZE, KV + (c + 1) * HEAD_SIZE)
        dk = dv = None
        for h in range(c * group, (c + 1) * group):
            cut = slice(h * HEAD_SIZE, (h + 1) * HEAD_SIZE)
            soft = softmax_parts(q[:, cut], kv[:, k_cut], causal)
            dp = mm(do[:, cut], kv[:, v_cut], 1, 1)
            ds = (soft * (dp - jnp.sum(soft * dp, axis=-1, keepdims=True))).astype(BF16)
            dq = turn_back(mm(ds, kv[:, k_cut]) * SCALE, cos, sin).astype(BF16)
            if h < 8:
                dqp[:, cut] = dq
            else:
                drp[:, 2 * KV + (h - 8) * HEAD_SIZE : 2 * KV + (h - 7) * HEAD_SIZE] = dq
            k_term = mm(ds, q[:, cut], 0, 0)
            v_term = mm(soft.astype(BF16), do[:, cut], 0, 0)
            dk = k_term if dk is None else dk + k_term
            dv = v_term if dv is None else dv + v_term
        drp[:, k_cut] = turn_back(dk * SCALE, cos, sin).astype(BF16)
        drp[:, v_cut] = dv.astype(BF16)
    scatters[0].relay()

    loads[8].wait()
    blocks(1, n1, dqp)
    blocks(2, n1, drp)
    sum_pairs(1)
    sum_pairs(2)

    loads[1].wait()
    loads[2].wait()
    loads[9].wait()
    dn1 = (
        mm(dqp[...], wqv[:, :WIDE], 1, 1)
        + mm(drp[:, 2 * KV :], wqv[:, WIDE:], 1, 1)
        + mm(drp[:, : 2 * KV], wkvv[...], 1, 1)
    )
    back, g_one = norm_back(tokens[...].astype(F32), gain_row(small_all, 32), dn1)
    g_tokens[...] += back

    work = (
        (cur_o, pc_o, out_o, la_o, lb_o, MODEL_WIDTH, True),
        (cur_q, pc_q, out_q, la_q, lb_q, WIDE, False),
        (cur_r, pc_r, out_r, la_r, lb_r, WIDE, True),
    )
    planes = [PlaneSum(p, *w, ts.at[k], tr.at[k]) for k, w in enumerate(work)]
    sgate = Scatter(p, part_gate, land_gate, es, er, width=FF)

    def relay_q():
        scatters[1].relay()

    def relay_r():
        scatters[2].relay()
        load_gate.wait()
        for c in sgate.far + sgate.near:
            c.start()


    def combine(i):
        group = sends[i * GROUP : (i + 1) * GROUP]
        for c in group:
            c.wait_recv()
        if i == 3:
            own_y.wait()
        weighted = jnp.concatenate(
            [
                slot_rows(posm, t, 1)[0] * share[pl.ds(t, 1), :]
                for t in places[i * GROUP : (i + 1) * GROUP]
            ],
            axis=0,
        )
        high = weighted.astype(BF16)
        low = (weighted - high.astype(F32)).astype(BF16)
        y_now = flatten(y_in[i * GROUP : (i + 1) * GROUP])
        term = mm(high, y_now, 0, 0) + mm(low, y_now, 0, 0)
        if i == 0:
            acc[...] = r[...] + term
        else:
            acc[...] += term

    diagonal = lax.broadcasted_iota(jnp.int32, (CAP, 128), 0) == lax.broadcasted_iota(
        jnp.int32, (CAP, 128), 1
    )
    for k, t in enumerate(places):
        line = jnp.where(diagonal, dots_in[k, 0:1, :], 0.0)
        column = jnp.sum(line, axis=-1, keepdims=True)
        dgate[pl.ds(t, 1), :] = jnp.sum(slot_rows(posm, t, 1)[0] * column, axis=0, keepdims=True)
    dlogits = dgate[...] - share[...] * jnp.sum(dgate[...], axis=0, keepdims=True)
    dlogits = jnp.where(posm[...] >= 0.0, dlogits, 0.0).astype(BF16)
    g_router = mm(dlogits, tokens[...])
    for s in range(4):
        cut = slice(s * SHARD, (s + 1) * SHARD)
        g_tokens[:, cut] += mm(dlogits, small_all[s, 0:32, :], 0, 0)
        sm_part[s] = jnp.concatenate(
            [g_router[:, cut], g_one[:, cut], g_two[:, cut], jnp.zeros((14, SHARD), F32)], axis=0
        ).astype(BF16)
    save_tokens = pltpu.make_async_copy(g_tokens, tokens_out, ls.at[10])
    save_tokens.start()

    small_x = [
        remote(sm_part.at[x], sm_x.at[k], ms.at[k], mr.at[k], (x, p.e))
        for k, x in enumerate([p.xr, p.xl, p.x2])
    ]
    small_z = [
        remote(sm_z.at[p.z], sm_z.at[p.z], ms.at[2 + d], mr.at[2 + d], (p.x, p.peer((d, 0, 0))))
        for d in (1, 2, 3)
    ]
    small_y = [
        remote(sm_y.at[p.y], sm_y.at[p.y], ms.at[5 + d], mr.at[5 + d], (p.x, p.peer((0, d, 0))))
        for d in (1, 2, 3)
    ]
    small_c = [remote(sm_c.at[p.core], sm_c.at[p.core], ms.at[9], mr.at[9], p.sibling)]

    def total(ref, count):
        value = ref[0].astype(F32)
        for k in range(1, count):
            value += ref[k].astype(F32)
        return value

    for c in small_x:
        c.start()
    planes[0].start_a(scatters[0])
    send_y(18, 21)
    relay_q()
    combine(0)
    planes[0].start_b()
    send_y(21, 25)
    relay_r()
    combine(1)
    planes[0].start_back_b()
    send_y(25, 28)
    for c in small_x:
        c.wait_recv()
    sm_z[p.z] = (sm_part[p.x].astype(F32) + total(sm_x, 3)).astype(BF16)
    for c in small_z:
        c.start()
    planes[0].start_back_a()
    send_y(28, 29)
    planes[1].start_a(scatters[1])
    combine(2)
    planes[2].start_a(scatters[2])
    send_y(29, 31)
    for c in small_z:
        c.wait_recv()
    sm_y[p.y] = total(sm_z, 4).astype(BF16)
    for c in small_y:
        c.start()
    planes[1].start_b()
    planes[2].start_b()
    sgate.relay()
    for c in small_y:
        c.wait_recv()
    sm_c[p.core] = total(sm_y, 4).astype(BF16)
    for c in small_c:
        c.start()
    planes[1].start_back_b()
    planes[2].start_back_b()
    combine(3)
    mixed[...] = acc[...].astype(BF16)
    save_mixed = pltpu.make_async_copy(mixed, mixed_out, ls.at[11])
    save_mixed.start()
    planes[1].start_back_a()
    planes[2].start_back_a()
    planes[0].start_pass()
    for c in small_c:
        c.wait_recv()
    out_small[...] = total(sm_c, 2)
    sgate.arrived()
    for half in range(2):
        g_gate[half * HALF : (half + 1) * HALF, :] = sgate.result(half).astype(BF16)
    planes[1].start_pass()
    planes[2].start_pass()
    save_tokens.wait()
    save_mixed.wait()

    for c in sends + small_x + small_z + small_y + small_c:
        c.wait_send()
    for g in pairs + scatters + planes + [sgate]:
        g.finish()


def back(
    tokens, cotangent, posm, share, dots, small_all, n1, q, kv, o, r, dr_rows, y_rows, wq, wkv, wo, gate
):
    D = MODEL_WIDTH
    cosine, sine = rope_tables()

    def arr(shape, dtype=BF16):
        return jax.ShapeDtypeStruct(shape, dtype)

    vm = pl.BlockSpec(memory_space=VMEM)
    hb = pl.BlockSpec(memory_space=ANY)
    sem = pltpu.SemaphoreType.DMA
    widths = (D, WIDE, WIDE)
    return pl.pallas_call(
        back_kernel,
        out_shape=[
            arr((SEQ, D)), arr((SEQ, D), F32), arr((SHARD, D)), arr((SHARD, WIDE)), arr((SHARD, WIDE)),
            arr((48, SHARD), F32), arr((SHARD, FF)),
        ],
        in_specs=[vm] * 6 + [hb] * 13,
        out_specs=[hb] * 2 + [vm] * 5,
        scratch_shapes=[
            VMEM((SEQ, D), BF16),
            VMEM((SEQ, D), F32),
            VMEM((SEQ, D), BF16),
            VMEM((SEQ, D), BF16),
            VMEM((SEQ, D), BF16),
            VMEM((SEQ, D), BF16),
            VMEM((SEQ, 2 * KV), BF16),
            VMEM((SEQ, D), BF16),
            VMEM((SEQ, D), F32),
            VMEM((2, GROUP, CAP, D), BF16),
            VMEM((EXPERTS, CAP, D), BF16),
            VMEM((D, D), BF16),
            VMEM((D, 2 * KV), BF16),
            VMEM((D, D), BF16),
            VMEM((SEQ, D), F32),
            VMEM((SEQ, D), BF16),
            VMEM((SEQ, D), BF16),
            VMEM((SEQ, WIDE), BF16),
            VMEM((SEQ, WIDE), BF16),
            VMEM((EXPERTS, SEQ), F32),
            VMEM((6, HALF, FF), BF16),
            *[VMEM((D, w), BF16) for w in widths],
            *[VMEM((4, HALF, w), BF16) for w in widths],
            *[VMEM((6, HALF // 2, w), BF16) for w in widths],
            *[VMEM((HALF, w), BF16) for w in widths],
            *[VMEM((HALF, w // 4), BF16) for w in widths],
            *[VMEM((3, HALF, w // 4), BF16) for w in widths],
            *[VMEM((3, HALF // 4, w // 4), BF16) for w in widths],
            VMEM((4, 48, SHARD), BF16),
            VMEM((3, 48, SHARD), BF16),
            VMEM((4, 48, SHARD), BF16),
            VMEM((4, 48, SHARD), BF16),
            VMEM((2, 48, SHARD), BF16),
            sem((31,)),
            sem((31,)),
            sem((3, 4)),
            sem((3, 4)),
            sem((3, 6)),
            sem((3, 6)),
            sem((6,)),
            sem((6,)),
            sem((3, 13)),
            sem((3, 13)),
            sem((10,)),
            sem((10,)),
            sem((22,)),
        ],
        compiler_params=pltpu.CompilerParams(
            collective_id=1, has_side_effects=True, vmem_limit_bytes=LIMIT
        ),
        name="back",
    )(
        posm, share, dots, small_all, jnp.asarray(cosine), jnp.asarray(sine),
        tokens, cotangent, n1, q, kv, o, r, dr_rows, y_rows, wq, wkv, wo, gate,
    )


def finish_kernel(mixed, tokens, q, o, r, gate, up, down, small, mixed_, tokens_, q_, k_, v_, o_, gate_, up_, down_, router_, one_, two_):
    mixed_[...] = mixed[...]
    tokens_[...] = tokens[...]
    q_[:, :WIDE] = q[...].astype(F32)
    q_[:, WIDE:] = r[:, 2 * KV :].astype(F32)
    o_[...] = o[...].astype(F32)
    k_[...] = r[:, :KV].astype(F32)
    v_[...] = r[:, KV : 2 * KV].astype(F32)
    gate_[0] = gate[...].astype(F32)
    up_[0] = up[...].astype(F32)
    down_[0] = down[...].astype(F32)
    router_[...] = small[0:32, :]
    one_[...] = small[32, :]
    two_[...] = small[33, :]


def finish(mixed, tokens, q, o, r, gate, up, down, small):
    steps = 4

    def tall(count, width):
        return pl.BlockSpec((count // steps, width), lambda i: (i, 0))

    def owned():
        return pl.BlockSpec((1, SHARD // steps, FF), lambda i: (0, i, 0))

    def arr(*shape, dtype=F32):
        return jax.ShapeDtypeStruct(shape, dtype)

    D = MODEL_WIDTH
    return pl.pallas_call(
        finish_kernel,
        grid=(steps,),
        in_specs=[
            tall(SEQ, D), tall(SEQ, D), tall(SHARD, WIDE), tall(SHARD, D), tall(SHARD, WIDE),
            tall(SHARD, FF), tall(SHARD, FF), tall(SHARD, FF), pl.BlockSpec((48, SHARD), lambda i: (0, 0)),
        ],
        out_specs=[
            tall(SEQ, D), tall(SEQ, D), tall(SHARD, D), tall(SHARD, KV), tall(SHARD, KV), tall(SHARD, D),
            owned(), owned(), owned(), pl.BlockSpec((EXPERTS, SHARD), lambda i: (0, 0)),
            pl.BlockSpec((SHARD,), lambda i: (0,)), pl.BlockSpec((SHARD,), lambda i: (0,)),
        ],
        out_shape=[
            arr(SEQ, D, dtype=BF16), arr(SEQ, D), arr(SHARD, D), arr(SHARD, KV), arr(SHARD, KV), arr(SHARD, D),
            arr(1, SHARD, FF), arr(1, SHARD, FF), arr(1, SHARD, FF), arr(EXPERTS, SHARD),
            arr(SHARD), arr(SHARD),
        ],
        compiler_params=pltpu.CompilerParams(vmem_limit_bytes=LIMIT),
        name="finish",
    )(mixed, tokens, q, o, r, gate, up, down, small)


def pack_small(w_router, norm_one, norm_two):
    row = lax.broadcasted_iota(jnp.int32, (48, SHARD), 0)
    router = jnp.pad(w_router.T, ((0, 16), (0, 0)))
    gains = jnp.where(row == 32, norm_one[None, :], jnp.where(row == 33, norm_two[None, :], 0))
    return jnp.where(row < 32, router, gains).astype(BF16)


def shards(
    tokens, routes, w_query, key_matrix, value_matrix, w_output, norm_one, norm_two,
    w_router, w_gate, w_up, w_down, cotangent,
):
    small = pack_small(w_router, norm_one, norm_two)
    (_, dr_rows, y_rows, fq, fkv, fo, gate, n1, q, kv, o, r, small_all, posm, share, dots, g_up, g_down) = forth(
        tokens, cotangent, routes.T, small, w_query, key_matrix, value_matrix, w_output,
        w_gate[0], w_up[0], w_down[0],
    )
    mixed, g_tokens, g_o, g_q, g_r, g_small, g_gate = back(
        tokens, cotangent, posm, share, dots, small_all, n1, q, kv, o, r, dr_rows, y_rows, fq, fkv, fo, gate
    )
    mixed, g_tokens, g_q, g_k, g_v, g_o, g_gate, g_up, g_down, g_router, g_one, g_two = finish(
        mixed, g_tokens, g_q, g_o, g_r, g_gate, g_up, g_down, g_small
    )
    return (
        mixed, g_tokens, g_q, g_k, g_v, g_o, g_one, g_two, g_router.T, g_gate, g_up, g_down
    )


def solution(mesh):
    rows_split = P(("dp", "expert"), None)
    flat = P("dp", None)
    vector = P("dp")
    owned = P("expert", "dp", None)
    return jax.shard_map(
        shards,
        mesh=mesh,
        in_specs=(
            rows_split, rows_split, flat, flat, flat, flat, vector, vector, flat, owned, owned, owned,
            rows_split,
        ),
        out_specs=(
            rows_split, rows_split, flat, flat, flat, flat, vector, vector, flat, owned, owned, owned,
        ),
        check_vma=False,
    )
```

```python
import functools
import itertools

import jax
import jax.numpy as jnp
import numpy as np
from jax import lax
from jax.experimental import pallas as pl
from jax.experimental.pallas import tpu as pltpu
from jax.sharding import PartitionSpec as P

MODEL_WIDTH = 1536
QUERY_HEADS = 12
KEY_VALUE_HEADS = 2
HEAD_SIZE = 128
TOPK = 4
SEQ = 256
EXPERTS = 32
CAP = 40
FF = 768
KV = KEY_VALUE_HEADS * HEAD_SIZE
SHARD = MODEL_WIDTH // 4
HALF = SHARD // 2
QUARTER = HALF // 2
EPSILON = 1e-06
ROPE_BASE = 10000.0
SCALE = HEAD_SIZE ** (-0.5)
MESH = pl.DeviceIdType.MESH
F32 = jnp.float32
BF16 = jnp.bfloat16
VMEM = pltpu.VMEM
ANY = pl.ANY
LIMIT = 60 * 1024 * 1024


def _offsets():
    def far(a):
        return min(a, 4 - a)

    def spread(core):
        every = [(z, y, core) for z in range(4) for y in range(4) if (z, y, core) != (0, 0, 0)]
        every = sorted(every, key=lambda o: (far(o[0]) + far(o[1]), o), reverse=True)
        groups, taken = [], set()
        for z, y, _ in every:
            group = []
            for o in ((z, y), (-z % 4, -y % 4), (y, z), (-y % 4, -z % 4)):
                if o not in taken:
                    taken.add(o)
                    group.append((*o, core))
            if group:
                groups.append(group)
        order = []
        while groups:
            order += groups.pop(0)
            if groups:
                order += groups.pop()
        return order

    return spread(0) + spread(1)


OFFSETS = _offsets()


def rope_tables():
    position = np.arange(SEQ, dtype=np.float32)
    frequency = (
        np.float32(ROPE_BASE) ** (-np.arange(64, dtype=np.float32) * np.float32(2.0 / HEAD_SIZE))
    ).astype(np.float32)
    angles = (position[:, None] * frequency[None, :]).astype(np.float32)
    cosine = np.cos(angles.astype(np.float64)).astype(np.float32)
    sine = np.sin(angles.astype(np.float64)).astype(np.float32)
    return (
        np.concatenate([cosine, cosine], axis=1),
        np.concatenate([-sine, sine], axis=1),
    )


def mm(left, right, left_dim=1, right_dim=0):
    return lax.dot_general(
        left, right, (((left_dim,), (right_dim,)), ((), ())), preferred_element_type=F32
    )


class Place:
    def __init__(self):
        self.x = lax.axis_index("dp")
        self.e = lax.axis_index("expert")
        self.core = lax.rem(self.e, 2)
        self.y = lax.rem(self.e // 2, 4)
        self.z = self.e // 8
        self.xl = lax.rem(self.x + 3, 4)
        self.xr = lax.rem(self.x + 1, 4)
        self.x2 = lax.rem(self.x + 2, 4)
        self.left = (self.xl, self.e)
        self.right = (self.xr, self.e)
        self.across = (self.x2, self.e)
        self.sibling = (self.x, self.e + 1 - 2 * self.core)

    def peer(self, offset):
        dz, dy, dc = offset
        return (
            lax.rem(self.z + dz, 4) * 8 + lax.rem(self.y + dy, 4) * 2 + lax.rem(self.core + dc, 2)
        )

    def peers(self):
        return [self.peer(o) for o in OFFSETS]


def greet(devices):
    barrier = pltpu.get_barrier_semaphore()
    for d in devices:
        pl.semaphore_signal(barrier, inc=1, device_id=d, device_id_type=MESH)
    return barrier


def remote(src, dst, send, recv, device):
    return pltpu.make_async_remote_copy(
        src_ref=src, dst_ref=dst, send_sem=send, recv_sem=recv, device_id=device, device_id_type=MESH
    )


def rows(start, count, align=16):
    return pl.ds(pl.multiple_of(start, align), count)


class Gather:
    def __init__(self, place, shard, region, send, recv):
        p = place
        half = p.core * HALF

        def move(k, src, dst, device):
            return remote(src, dst, send.at[k], recv.at[k], device)

        mine = shard.at[rows(half, HALF, 32)]
        self.direct = [
            move(0, mine, region(p.x, half, HALF), p.right),
            move(1, mine, region(p.x, half, HALF), p.left),
        ]
        from_left = region(p.xl, half, QUARTER)
        from_right = region(p.xr, half + QUARTER, QUARTER)
        self.forward = [
            move(2, from_left, from_left, p.right),
            move(3, from_right, from_right, p.left),
        ]
        whole_left = region(p.xl, half, HALF)
        whole_right = region(p.xr, half, HALF)
        far_one = region(p.x2, half, QUARTER)
        far_two = region(p.x2, half + QUARTER, QUARTER)
        self.near = [
            move(4, whole_left, whole_left, p.sibling),
            move(5, whole_right, whole_right, p.sibling),
        ]
        self.far = [
            move(6, far_one, far_one, p.sibling),
            move(7, far_two, far_two, p.sibling),
        ]

    def start(self):
        for c in self.direct:
            c.start()

    def relay(self):
        for k in range(2):
            self.direct[k].wait_recv()
            self.forward[k].start()
            self.near[k].start()

    def relay_far(self):
        for k in range(2):
            self.forward[k].wait_recv()
            self.far[k].start()

    def arrived_near(self):
        for c in self.near:
            c.wait_recv()

    def arrived_far(self):
        for c in self.far:
            c.wait_recv()

    def finish(self):
        for c in self.direct + self.forward + self.near + self.far:
            c.wait_send()


def slot_rows(posm_ref, first, count):
    slot = lax.broadcasted_iota(jnp.int32, (CAP, SEQ), 0).astype(F32)
    return [
        jnp.where(posm_ref[pl.ds(first + j, 1), :] == slot, 1.0, 0.0) for j in range(count)
    ]


def turn(values, cosine, sine):
    return values * cosine + pltpu.roll(values, 64, 1) * sine


def turn_back(values, cosine, sine):
    return values * cosine - pltpu.roll(values, 64, 1) * sine


def softmax_parts(q_head, k_head, causal):
    scores = mm(q_head, k_head, 1, 1) * SCALE
    scores = jnp.where(causal, scores, -jnp.inf)
    largest = jnp.max(scores, axis=-1, keepdims=True)
    exponent = jnp.exp(scores - largest)
    return exponent / jnp.sum(exponent, axis=-1, keepdims=True)


def causal_mask():
    row = lax.broadcasted_iota(jnp.int32, (SEQ, SEQ), 0)
    column = lax.broadcasted_iota(jnp.int32, (SEQ, SEQ), 1)
    return column <= row


def norm_back(v, gain, grad):
    scale = lax.rsqrt(jnp.mean(v * v, axis=-1, keepdims=True) + EPSILON)
    unit = v * scale
    w = grad * gain
    return (
        (w - unit * jnp.mean(w * unit, axis=-1, keepdims=True)) * scale,
        jnp.sum(grad * unit, axis=0, keepdims=True),
    )


def gelu_parts(a):
    inner = jnp.tanh(0.7978845608028654 * (a + 0.044715 * a * a * a))
    value = 0.5 * a * (1.0 + inner)
    slope = 0.5 * (1.0 + inner) + 0.5 * a * (1.0 - inner * inner) * 0.7978845608028654 * (
        1.0 + 3.0 * 0.044715 * a * a
    )
    return value, slope


class GatherOwn:
    def __init__(self, place, shard, region, send, recv):
        p = place

        def move(k, src, dst, device):
            return remote(src, dst, send.at[k], recv.at[k], device)

        self.direct = [
            move(0, shard, region(p.x, 0, SHARD), p.right),
            move(1, shard, region(p.x, 0, SHARD), p.left),
        ]
        from_left = region(p.xl, 0, HALF)
        from_right = region(p.xr, HALF, HALF)
        self.forward = [
            move(2, from_left, from_left, p.right),
            move(3, from_right, from_right, p.left),
        ]

    def start(self):
        for c in self.direct:
            c.start()

    def relay(self):
        for k in range(2):
            self.direct[k].wait_recv()
            self.forward[k].start()

    def arrived(self):
        for c in self.forward:
            c.wait_recv()

    def finish(self):
        for c in self.direct + self.forward:
            c.wait_send()


class Scatter:
    def __init__(self, place, partial, landing, send, recv, first=0, height=SHARD, width=None):
        p = self.p = place
        half = height // 2
        self.partial, self.landing, self.first, self.height = partial, landing, first, height
        self.cut = cut = pl.ds(0, width or partial.shape[1])

        def region(x, part):
            return partial.at[rows(x * SHARD + first + part * half, half, 32), cut]

        def move(k, src, device):
            return remote(src, landing.at[k], send.at[k], recv.at[k], device)

        self.far = [move(0, region(p.x2, 0), p.right), move(1, region(p.x2, 1), p.left)]
        self.near = [move(2, region(p.xr, 1), p.right), move(3, region(p.xl, 0), p.left)]
        self.summed = [move(4, region(p.xr, 0), p.right), move(5, region(p.xl, 1), p.left)]

    def relay(self):
        p, half = self.p, self.height // 2
        for k, x, part in ((0, p.xr, 0), (1, p.xl, 1)):
            self.far[k].wait_recv()
            where = rows(x * SHARD + self.first + part * half, half, 32)
            self.partial[where, self.cut] = (
                self.partial[where, self.cut].astype(F32) + self.landing[k].astype(F32)
            ).astype(BF16)
            self.summed[k].start()

    def result(self, part):
        p, half = self.p, self.height // 2
        own = self.partial[rows(p.x * SHARD + self.first + part * half, half, 32), self.cut]
        one, two = ((4, 3), (2, 5))[part]
        return (
            own.astype(F32)
            + self.landing[one].astype(F32)
            + self.landing[two].astype(F32)
        )

    def arrived(self):
        for c in self.near + self.summed:
            c.wait_recv()

    def finish(self):
        for c in self.far + self.near + self.summed:
            c.wait_send()


GROUP = 8
BLOCK = GROUP * CAP


def flatten(slots):
    return slots.astype(F32).reshape(BLOCK, MODEL_WIDTH).astype(BF16)


def unflatten(values):
    return values.reshape(GROUP, CAP, MODEL_WIDTH).astype(BF16)


def forth_kernel(
    tokens, cotangent, routes, router, gain_one, gain_two, cosine, sine, wq, wk, wv, wo, wgate, wup, wdown,
    dy_in, dr_in, y_out, wq_full, wkv_full, wo_full, gate_out, n1_out, q_out, kv_out, o_out, r_out,
    small_all, posm, share, dots_in, g_up, g_down,
    buf_a, buf_b, landing, dyflat, wqf, wkvf, wof, wgu, wd, hid, part_down, part_gate, part_up, land_down, land_up,
    small, n1, q, kv, o, r, n2, qacc, kvacc, dots,
    ag, ag_r, sg, sg_r, ds_, dr_, gs, gr, ns, nr, bs, br, cs, cr, ss, sr, ls,
):
    p = Place()
    peers = p.peers()
    sources = [p.peer(tuple((-v) % m for v, m in zip(o_, (4, 4, 2)))) for o_ in OFFSETS]
    barrier = greet([p.left, p.right, p.across] + [(p.x, t) for t in peers])

    def columns(full, first, count):
        return lambda x, start, height: full.at[
            rows(x * SHARD + start, height, 32), pl.ds(first, count)
        ]

    at_q = columns(wqf, 0, MODEL_WIDTH)
    at_k = columns(wkvf, 0, KV)
    at_v = columns(wkvf, KV, KV)
    at_o = columns(wof, 0, MODEL_WIDTH)
    at_gate = columns(wgu, 0, FF)
    at_up = columns(wgu, FF, FF)
    at_down = columns(wd, 0, FF)
    mine = [
        pltpu.make_async_copy(w, f(p.x, 0, SHARD), ls.at[k])
        for k, (w, f) in enumerate(
            [
                (wq, at_q), (wk, at_k), (wv, at_v), (wo, at_o),
                (wgate, at_gate), (wup, at_up), (wdown, at_down),
            ]
        )
    ]
    for c in mine:
        c.start()

    lane = lax.broadcasted_iota(jnp.int32, (EXPERTS, SEQ), 0)
    named = routes[0:1, :] == lane
    for j in range(1, TOPK):
        named = jnp.logical_or(named, routes[j : j + 1, :] == lane)
    earlier = (
        lax.broadcasted_iota(jnp.int32, (SEQ, SEQ), 0)
        < lax.broadcasted_iota(jnp.int32, (SEQ, SEQ), 1)
    ).astype(F32).astype(BF16)
    place_of = mm(named.astype(F32).astype(BF16), earlier)
    posm[...] = jnp.where(named, place_of, -1.0)

    small[0:32, :] = router[...]
    gains = [g[...].astype(F32).reshape(1, SHARD) for g in (gain_one, gain_two)]
    small[32:48, :] = jnp.concatenate(gains + [jnp.zeros((14, SHARD), F32)], axis=0).astype(BF16)
    small_all[p.x] = small[...]
    pl.semaphore_wait(barrier, len(peers) + 3)

    small_moves = [
        remote(small, small_all.at[p.x], sg.at[k], sg_r.at[k], d)
        for k, d in enumerate([p.right, p.left, p.across])
    ]
    for c in small_moves:
        c.start()
    gq, gk, gv, go = [
        Gather(p, w, f, ag.at[k], ag_r.at[k])
        for k, (w, f) in enumerate([(wq, at_q), (wk, at_k), (wv, at_v), (wo, at_o)])
    ]
    for g in (gq, gk, gv):
        g.start()

    for c in small_moves:
        c.wait_recv()
    logits = mm(small_all[0, 0:32, :], tokens[:, 0:SHARD], 1, 1)
    for s in range(1, 4):
        logits += mm(small_all[s, 0:32, :], tokens[:, s * SHARD : (s + 1) * SHARD], 1, 1)
    top = jnp.max(jnp.where(named, logits, -jnp.inf), axis=0, keepdims=True)
    weight = jnp.where(named, jnp.exp(jnp.minimum(logits - top, 0.0)), 0.0)
    share[...] = weight / jnp.sum(weight, axis=0, keepdims=True)

    places = peers + [p.e]
    dy_sends = [
        remote(buf_a.at[k], dy_in.at[k], ds_.at[k], dr_.at[k], (p.x, t))
        for k, t in enumerate(peers)
    ]
    own_dy = pltpu.make_async_copy(buf_a.at[31], dy_in.at[31], ls.at[7])
    for i in range(0, EXPERTS, 4):
        hot = [slot_rows(posm, t, 1)[0] for t in places[i : i + 4]]
        gain = jnp.concatenate(
            [
                jnp.sum(b * share[pl.ds(t, 1), :], axis=-1, keepdims=True)
                for t, b in zip(places[i : i + 4], hot)
            ],
            axis=0,
        )
        picked = mm(jnp.concatenate(hot, axis=0).astype(BF16), cotangent[...])
        buf_a[i : i + 4] = (picked * gain).reshape(4, CAP, MODEL_WIDTH).astype(BF16)
        for c in dy_sends[i : i + 4]:
            c.start()
    own_dy.start()

    x = tokens[...].astype(F32)
    unit = x * lax.rsqrt(jnp.mean(x * x, axis=-1, keepdims=True) + EPSILON)
    for s in range(4):
        cut = slice(s * SHARD, (s + 1) * SHARD)
        n1[:, cut] = (unit[:, cut] * small_all[s, 32:33, :].astype(F32)).astype(BF16)
    saves = [
        pltpu.make_async_copy(a, b, ls.at[16 + k])
        for k, (a, b) in enumerate([(n1, n1_out), (q, q_out), (kv, kv_out), (o, o_out), (r, r_out)])
    ]
    saves[0].start()

    def part(x_index):
        return n1[:, rows(x_index * SHARD, SHARD, 128)]

    def block(full, x_index):
        return full[rows(x_index * SHARD, SHARD, 128), :]

    for c in mine[:3]:
        c.wait()
    qacc[...] = mm(part(p.x), block(wqf, p.x))
    kvacc[...] = mm(part(p.x), block(wkvf, p.x))
    for g in (gq, gk, gv):
        g.relay()
    go.start()
    for g in (gq, gk, gv):
        g.arrived_near()
    for s in (p.xl, p.xr):
        qacc[...] += mm(part(s), block(wqf, s))
        kvacc[...] += mm(part(s), block(wkvf, s))
    for g in (gq, gk, gv):
        g.relay_far()
    for g in (gq, gk, gv):
        g.arrived_far()
    qacc[...] += mm(part(p.x2), block(wqf, p.x2))
    kvacc[...] += mm(part(p.x2), block(wkvf, p.x2))
    keep = [
        pltpu.make_async_copy(f, out, ls.at[8 + k])
        for k, (f, out) in enumerate([(wqf, wq_full), (wkvf, wkv_full), (wof, wo_full)])
    ]
    keep[0].start()
    keep[1].start()

    cos = cosine[...]
    sin = sine[...]
    for h in range(KEY_VALUE_HEADS):
        cut = slice(h * HEAD_SIZE, (h + 1) * HEAD_SIZE)
        kv[:, cut] = turn(kvacc[:, cut], cos, sin).astype(BF16)
        cut = slice(KV + h * HEAD_SIZE, KV + (h + 1) * HEAD_SIZE)
        kv[:, cut] = kvacc[:, cut].astype(BF16)
    causal = causal_mask()
    for h in range(QUERY_HEADS):
        cut = slice(h * HEAD_SIZE, (h + 1) * HEAD_SIZE)
        c = h // (QUERY_HEADS // KEY_VALUE_HEADS)
        q_head = turn(qacc[:, cut], cos, sin).astype(BF16)
        q[:, cut] = q_head
        weights = softmax_parts(q_head, kv[:, c * HEAD_SIZE : (c + 1) * HEAD_SIZE], causal)
        o[:, cut] = mm(
            weights.astype(BF16), kv[:, KV + c * HEAD_SIZE : KV + (c + 1) * HEAD_SIZE]
        ).astype(BF16)

    for c in saves[1:4]:
        c.start()

    def opart(x_index):
        return o[:, rows(x_index * SHARD, SHARD, 128)]

    for c in mine[3:]:
        c.wait()
    r[...] = tokens[...].astype(F32) + mm(opart(p.x), block(wof, p.x))
    go.relay()
    ggate = GatherOwn(p, wgate, at_gate, gs.at[0], gr.at[0])
    gup = GatherOwn(p, wup, at_up, gs.at[1], gr.at[1])
    gdown = GatherOwn(p, wdown, at_down, gs.at[2], gr.at[2])
    ggate.start()
    gup.start()
    go.arrived_near()
    for s in (p.xl, p.xr):
        r[...] += mm(opart(s), block(wof, s))
    go.relay_far()
    go.arrived_far()
    keep[2].start()
    residual = r[...] + mm(opart(p.x2), block(wof, p.x2))
    r[...] = residual
    saves[4].start()
    unit = residual * lax.rsqrt(jnp.mean(residual * residual, axis=-1, keepdims=True) + EPSILON)
    for s in range(4):
        cut = slice(s * SHARD, (s + 1) * SHARD)
        n2[:, cut] = (unit[:, cut] * small_all[s, 33:34, :].astype(F32)).astype(BF16)

    sends = [
        remote(buf_b.at[k], landing.at[k], ns.at[k], nr.at[k], (p.x, t))
        for k, t in enumerate(peers)
    ]
    own_rows = pltpu.make_async_copy(buf_b.at[31], landing.at[31], ls.at[11])
    for i in range(0, EXPERTS, 4):
        hot = [slot_rows(posm, t, 1)[0] for t in places[i : i + 4]]
        picked = mm(jnp.concatenate(hot, axis=0).astype(BF16), n2[...])
        buf_b[i : i + 4] = picked.reshape(4, CAP, MODEL_WIDTH).astype(BF16)
        for c in sends[i : i + 4]:
            c.start()
    own_rows.start()

    ggate.relay()
    gup.relay()
    gdown.start()
    for c in dy_sends:
        c.wait()
    own_dy.wait()
    load_dy = pltpu.make_async_copy(dy_in, buf_a, ls.at[12])
    load_dy.start()
    for g in (gq, gk, gv, go):
        g.finish()
    for c in small_moves:
        c.wait_send()
    for c in keep:
        c.wait()
    rflat = wof
    dab = wqf
    load_dy.wait()

    @pl.loop(0, 4)
    def _(i):
        dyflat[rows(i * BLOCK, BLOCK), :] = flatten(buf_a[pl.ds(i * GROUP, GROUP)])

    ggate.arrived()
    gup.arrived()

    def forward(i):
        if i == 3:
            own_rows.wait()
        for c in sends[i * GROUP : (i + 1) * GROUP]:
            c.wait_recv()
        cut = slice(i * BLOCK, (i + 1) * BLOCK)
        rflat[cut, :] = flatten(landing[i * GROUP : (i + 1) * GROUP])
        ab = mm(rflat[cut, :], wgu[...])
        value, slope = gelu_parts(ab[:, :FF])
        b = ab[:, FF:]
        hid[cut, :] = (value * b).astype(BF16)
        dab[cut, :FF] = (slope * b).astype(BF16)
        dab[cut, FF:] = value.astype(BF16)

    backs = [
        remote(buf_a.at[k], dr_in.at[p.e], bs.at[k], br.at[k], (p.x, sources[k])) for k in range(31)
    ]

    def backward(i):
        cut = slice(i * BLOCK, (i + 1) * BLOCK)
        dh = mm(dyflat[cut, :], wd[...])
        dab[cut, :FF] = (dh * dab[cut, :FF].astype(F32)).astype(BF16)
        dab[cut, FF:] = (dh * dab[cut, FF:].astype(F32)).astype(BF16)
        buf_a[i * GROUP : (i + 1) * GROUP] = unflatten(mm(dab[cut, :], wgu[...], 1, 1))
        for c in backs[i * GROUP : (i + 1) * GROUP]:
            c.start()

    forward(0)
    forward(1)
    gdown.relay()
    forward(2)
    gdown.arrived()
    backward(0)
    backward(1)
    backward(2)
    forward(3)
    backward(3)
    own_back = pltpu.make_async_copy(buf_a.at[31], dr_in.at[p.e], ls.at[13])
    own_back.start()

    sdown = Scatter(p, part_down, land_down, ss.at[0], sr.at[0])
    sup = Scatter(p, part_up, land_up, ss.at[1], sr.at[1])

    def down_block(x):
        where = rows(x * SHARD, SHARD, 128)
        part_down[where, :] = mm(dyflat[:, where], hid[...], 0, 0).astype(BF16)

    def gate_up_block(x):
        where = rows(x * SHARD, SHARD, 128)
        both = mm(rflat[0 : EXPERTS * CAP, where], dab[0 : EXPERTS * CAP, :], 0, 0)
        part_gate[where, :] = both[:, :FF].astype(BF16)
        part_up[where, :] = both[:, FF:].astype(BF16)

    def start_scatter(scatter, fill):
        fill(p.x2)
        for c in scatter.far:
            c.start()
        fill(p.xr)
        scatter.near[0].start()
        fill(p.xl)
        scatter.near[1].start()
        fill(p.x)

    start_scatter(sdown, down_block)
    start_scatter(sup, gate_up_block)
    keep_gate = pltpu.make_async_copy(part_gate, gate_out, ls.at[15])
    keep_gate.start()
    sdown.relay()

    for c in sends:
        c.wait_send()
    back_dots = [
        remote(dots.at[k], dots_in.at[k], cs.at[k], cr.at[k], (p.x, sources[k])) for k in range(31)
    ]
    diagonal = lax.broadcasted_iota(jnp.int32, (CAP, 128), 0) == lax.broadcasted_iota(
        jnp.int32, (CAP, 128), 1
    )
    for i in range(4):
        cut = slice(i * BLOCK, (i + 1) * BLOCK)
        y = mm(hid[cut, :], wd[...], 1, 1)
        buf_b[i * GROUP : (i + 1) * GROUP] = unflatten(y)
        products = dyflat[cut, :].astype(F32) * y.astype(BF16).astype(F32)
        column = jnp.sum(products, axis=-1, keepdims=True)
        for j in range(GROUP):
            line = jnp.where(diagonal, column[j * CAP : (j + 1) * CAP], 0.0)
            line = jnp.sum(line, axis=0, keepdims=True)
            dots[i * GROUP + j] = jnp.broadcast_to(line, (8, 128))
        for c in back_dots[i * GROUP : (i + 1) * GROUP]:
            c.start()
    dots_in[31] = dots[31]
    keep_y = pltpu.make_async_copy(buf_b, y_out, ls.at[14])
    keep_y.start()

    sup.relay()
    sdown.arrived()
    for half in range(2):
        g_down[half * HALF : (half + 1) * HALF, :] = sdown.result(half).astype(BF16)
    sup.arrived()
    for half in range(2):
        g_up[half * HALF : (half + 1) * HALF, :] = sup.result(half).astype(BF16)

    keep_gate.wait()
    for c in saves:
        c.wait()
    for c in backs + back_dots:
        c.wait()
    own_back.wait()
    keep_y.wait()
    for g in (ggate, gup, gdown, sdown, sup):
        g.finish()


def forth(tokens, cotangent, routes, router, one, two, wq, wk, wv, wo, wgate, wup, wdown):
    cosine, sine = rope_tables()
    D = MODEL_WIDTH

    def arr(shape, dtype=BF16):
        return jax.ShapeDtypeStruct(shape, dtype)

    vm = pl.BlockSpec(memory_space=VMEM)
    hb = pl.BlockSpec(memory_space=ANY)
    sem = pltpu.SemaphoreType.DMA
    N = EXPERTS * CAP
    slots = (EXPERTS, CAP, D)
    return pl.pallas_call(
        forth_kernel,
        out_shape=[
            arr(slots), arr(slots), arr(slots), arr((D, D)), arr((D, 2 * KV)), arr((D, D)), arr((D, FF)),
            arr((SEQ, D)), arr((SEQ, D)), arr((SEQ, 2 * KV)), arr((SEQ, D)), arr((SEQ, D), F32),
            arr((4, 48, SHARD)), arr((EXPERTS, SEQ), F32), arr((EXPERTS, SEQ), F32),
            arr((EXPERTS, 8, 128), F32),
            arr((SHARD, FF)), arr((SHARD, FF)),
        ],
        in_specs=[vm] * 8 + [hb] * 7,
        out_specs=[hb] * 12 + [vm] * 6,
        scratch_shapes=[
            VMEM(slots, BF16),
            VMEM(slots, BF16),
            VMEM(slots, BF16),
            VMEM((N, D), BF16),
            VMEM((D, D), BF16),
            VMEM((D, 2 * KV), BF16),
            VMEM((D, D), BF16),
            VMEM((D, 2 * FF), BF16),
            VMEM((D, FF), BF16),
            VMEM((N, FF), BF16),
            VMEM((D, FF), BF16),
            VMEM((D, FF), BF16),
            VMEM((D, FF), BF16),
            VMEM((6, HALF, FF), BF16),
            VMEM((6, HALF, FF), BF16),
            VMEM((48, SHARD), BF16),
            VMEM((SEQ, D), BF16),
            VMEM((SEQ, D), BF16),
            VMEM((SEQ, 2 * KV), BF16),
            VMEM((SEQ, D), BF16),
            VMEM((SEQ, D), F32),
            VMEM((SEQ, D), BF16),
            VMEM((SEQ, D), F32),
            VMEM((SEQ, 2 * KV), F32),
            VMEM((EXPERTS, 8, 128), F32),
            sem((4, 8)), sem((4, 8)), sem((3,)), sem((3,)), sem((31,)), sem((31,)),
            sem((3, 4)), sem((3, 4)), sem((31,)), sem((31,)), sem((31,)), sem((31,)),
            sem((31,)), sem((31,)), sem((2, 6)), sem((2, 6)), sem((21,)),
        ],
        compiler_params=pltpu.CompilerParams(
            collective_id=0, has_side_effects=True, vmem_limit_bytes=LIMIT
        ),
        name="forth",
    )(
        tokens, cotangent, routes, router, one, two, jnp.asarray(cosine), jnp.asarray(sine),
        wq, wk, wv, wo, wgate, wup, wdown,
    )


WIDE = 8 * HEAD_SIZE

class PairSum:
    def __init__(self, place, partial, landing, send, recv):
        p = place
        self.order = [p.x2, p.xr, p.xl, p.x]
        self.partial, self.landing = partial, landing
        self.half = p.core * HALF
        self.moves = [
            remote(
                partial.at[rows(x * SHARD + HALF - self.half, HALF, 32)],
                landing.at[i],
                send.at[i],
                recv.at[i],
                p.sibling,
            )
            for i, x in enumerate(self.order)
        ]

    def add(self, i):
        self.moves[i].wait_recv()
        where = rows(self.order[i] * SHARD + self.half, HALF, 32)
        self.partial[where, :] = (
            self.partial[where, :].astype(F32) + self.landing[i].astype(F32)
        ).astype(BF16)

    def finish(self):
        for c in self.moves:
            c.wait_send()


class PlaneSum:
    def __init__(self, place, current, piece, out, land_a, land_b, width, z_first, send, recv):
        p = self.p = place
        self.current, self.piece, self.out = current, piece, out
        self.land_a, self.land_b = land_a, land_b
        w = self.w = width // 4
        t = HALF // 4
        a, b = (p.z, p.y) if z_first else (p.y, p.z)
        self.a, self.b = a, b

        def along_a(d):
            return (p.x, p.peer((d, 0, 0) if z_first else (0, d, 0)))

        def along_b(d):
            return (p.x, p.peer((0, d, 0) if z_first else (d, 0, 0)))

        def cut(i):
            return pl.ds(pl.multiple_of(i * w, 128), w)

        self.cut_a = cut(a)
        self.rows_b = rows(b * t, t)
        base = p.core * HALF
        self.mine = (rows(base + b * t, t), cut(a))
        spot = out.at[rows(base + b * t, t), cut(a)]
        strip = out.at[rows(base, HALF, 32), cut(a)]
        whole = out.at[rows(base, HALF, 32)]
        steps = (1, 2, 3)
        self.step_a = [
            remote(
                current.at[:, cut(lax.rem(a + d, 4))],
                land_a.at[d - 1],
                send.at[d - 1],
                recv.at[d - 1],
                along_a(d),
            )
            for d in steps
        ]
        self.step_b = [
            remote(
                piece.at[rows(lax.rem(b + d, 4) * t, t)],
                land_b.at[d - 1],
                send.at[2 + d],
                recv.at[2 + d],
                along_b(d),
            )
            for d in steps
        ]
        self.back_b = [remote(spot, spot, send.at[5 + d], recv.at[5 + d], along_b(d)) for d in steps]
        self.back_a = [
            remote(strip, strip, send.at[8 + d], recv.at[8 + d], along_a(d)) for d in steps
        ]
        self.pass_on = [remote(whole, whole, send.at[12], recv.at[12], p.sibling)]

    def start_a(self, scatter):
        part = HALF // 2
        scatter.arrived()
        for k in range(2):
            self.current[k * part : (k + 1) * part, :] = scatter.result(k).astype(BF16)
        for c in self.step_a:
            c.start()

    def start_b(self):
        for c in self.step_a:
            c.wait_recv()
        total = self.current[:, self.cut_a].astype(F32)
        for k in range(3):
            total += self.land_a[k].astype(F32)
        self.piece[...] = total.astype(BF16)
        for c in self.step_b:
            c.start()

    def start_back_b(self):
        for c in self.step_b:
            c.wait_recv()
        total = self.piece[self.rows_b, :].astype(F32)
        for k in range(3):
            total += self.land_b[k].astype(F32)
        self.out[self.mine] = total.astype(BF16)
        for c in self.back_b:
            c.start()

    def start_back_a(self):
        for c in self.back_b:
            c.wait_recv()
        for c in self.back_a:
            c.start()

    def start_pass(self):
        for c in self.back_a:
            c.wait_recv()
        for c in self.pass_on:
            c.start()

    def finish(self):
        for c in self.pass_on:
            c.wait()
        for c in self.step_a + self.step_b + self.back_b + self.back_a:
            c.wait_send()


def gain_row(small_all, row):
    return jnp.concatenate(
        [small_all[s, row : row + 1, :].astype(F32) for s in range(4)], axis=1
    )


def back_kernel(
    posm, share, dots_in, small_all, cosine, sine,
    tokens_in, cotangent_in, n1_in, q_in, kv_in, o_in, r_in, dr_rows, y_rows, wq, wkv, wo, gate_rows,
    mixed_out, tokens_out, out_o, out_q, out_r, out_small, g_gate,
    mixed, g_tokens, tokens, cotangent, n1, q, kv, o, r,
    drv, y_in, wqv, wkvv, wov, acc, da, do, dqp, drp, dgate, land_gate,
    part_o, part_q, part_r, pair_o, pair_q, pair_r, land_o, land_q, land_r,
    cur_o, cur_q, cur_r, pc_o, pc_q, pc_r, la_o, la_q, la_r, lb_o, lb_q, lb_r,
    sm_part, sm_x, sm_z, sm_y, sm_c,
    ys, yr, ps, pr, ss, sr, es, er, ts, tr, ms, mr, ls,
):
    p = Place()
    peers = p.peers()
    sources = [p.peer(tuple((-v) % m for v, m in zip(o_, (4, 4, 2)))) for o_ in OFFSETS]
    barrier = greet([p.left, p.right, p.across] + [(p.x, t) for t in peers])
    loads = [
        pltpu.make_async_copy(s, d, ls.at[12 + k])
        for k, (s, d) in enumerate(
            [
                (wo, wov), (wq, wqv), (wkv, wkvv), (r_in, r), (cotangent_in, cotangent), (o_in, o),
                (q_in, q), (kv_in, kv), (n1_in, n1), (tokens_in, tokens),
            ]
        )
    ]
    groups = [
        pltpu.make_async_copy(
            dr_rows.at[pl.ds(i * GROUP, GROUP)], drv.at[i % 2], ls.at[6 + i]
        )
        for i in range(4)
    ]
    for c in groups[:2] + loads[3:6] + loads[:1] + loads[6:] + loads[1:3]:
        c.start()
    pl.semaphore_wait(barrier, len(peers) + 3)
    sends = [
        remote(y_rows.at[k], y_in.at[k], ys.at[k], yr.at[k], (p.x, sources[k]))
        for k in range(31)
    ]
    own_y = pltpu.make_async_copy(y_rows.at[31], y_in.at[31], ls.at[5])
    own_y.start()
    places = peers + [p.e]

    def send_y(first, end):
        for c in sends[first:end]:
            c.start()

    send_y(0, 18)

    for i in range(4):
        groups[i].wait()
        hot = jnp.concatenate(slot_rows(posm, i * GROUP, GROUP), axis=0).astype(BF16)
        term = mm(hot, flatten(drv[i % 2]), 0, 0)
        if i < 2:
            groups[i + 2].start()
        if i == 0:
            acc[...] = term
        else:
            acc[...] += term
    for c in loads[3:5]:
        c.wait()
    back, g_two = norm_back(r[...], gain_row(small_all, 33), acc[...])
    dr = cotangent[...].astype(F32) + back
    g_tokens[...] = dr
    da[...] = dr.astype(BF16)

    names = ((part_o, pair_o, land_o), (part_q, pair_q, land_q), (part_r, pair_r, land_r))
    pairs = [PairSum(p, a, b, ps.at[k], pr.at[k]) for k, (a, b, _) in enumerate(names)]
    scatters = [
        Scatter(p, a, c, ss.at[k], sr.at[k], p.core * HALF, HALF)
        for k, (a, _, c) in enumerate(names)
    ]

    def blocks(k, left, right):
        for i, x in enumerate(pairs[k].order):
            where = rows(x * SHARD, SHARD, 128)
            names[k][0][where, :] = mm(left[:, where], right[...], 0, 0).astype(BF16)
            pairs[k].moves[i].start()

    def sum_pairs(k):
        pairs[k].add(0)
        for c in scatters[k].far:
            c.start()
        pairs[k].add(1)
        scatters[k].near[0].start()
        pairs[k].add(2)
        scatters[k].near[1].start()
        pairs[k].add(3)

    loads[5].wait()
    blocks(0, o, da)
    sum_pairs(0)
    loads[0].wait()
    do[...] = mm(da[...], wov[...], 1, 1).astype(BF16)
    part_gate = wov
    load_gate = pltpu.make_async_copy(gate_rows, part_gate.at[:, pl.ds(0, FF)], ls.at[4])
    load_gate.start()

    loads[6].wait()
    loads[7].wait()
    cos = cosine[...]
    sin = sine[...]
    causal = causal_mask()
    group = QUERY_HEADS // KEY_VALUE_HEADS
    for c in range(KEY_VALUE_HEADS):
        k_cut = slice(c * HEAD_SIZE, (c + 1) * HEAD_SIZE)
        v_cut = slice(KV + c * HEAD_SIZE, KV + (c + 1) * HEAD_SIZE)
        dk = dv = None
        for h in range(c * group, (c + 1) * group):
            cut = slice(h * HEAD_SIZE, (h + 1) * HEAD_SIZE)
            soft = softmax_parts(q[:, cut], kv[:, k_cut], causal)
            dp = mm(do[:, cut], kv[:, v_cut], 1, 1)
            ds = (soft * (dp - jnp.sum(soft * dp, axis=-1, keepdims=True))).astype(BF16)
            dq = turn_back(mm(ds, kv[:, k_cut]) * SCALE, cos, sin).astype(BF16)
            if h < 8:
                dqp[:, cut] = dq
            else:
                drp[:, 2 * KV + (h - 8) * HEAD_SIZE : 2 * KV + (h - 7) * HEAD_SIZE] = dq
            k_term = mm(ds, q[:, cut], 0, 0)
            v_term = mm(soft.astype(BF16), do[:, cut], 0, 0)
            dk = k_term if dk is None else dk + k_term
            dv = v_term if dv is None else dv + v_term
        drp[:, k_cut] = turn_back(dk * SCALE, cos, sin).astype(BF16)
        drp[:, v_cut] = dv.astype(BF16)
    scatters[0].relay()

    loads[8].wait()
    blocks(1, n1, dqp)
    blocks(2, n1, drp)
    sum_pairs(1)
    sum_pairs(2)

    loads[1].wait()
    loads[2].wait()
    loads[9].wait()
    dn1 = (
        mm(dqp[...], wqv[:, :WIDE], 1, 1)
        + mm(drp[:, 2 * KV :], wqv[:, WIDE:], 1, 1)
        + mm(drp[:, : 2 * KV], wkvv[...], 1, 1)
    )
    back, g_one = norm_back(tokens[...].astype(F32), gain_row(small_all, 32), dn1)
    g_tokens[...] += back

    work = (
        (cur_o, pc_o, out_o, la_o, lb_o, MODEL_WIDTH, True),
        (cur_q, pc_q, out_q, la_q, lb_q, WIDE, False),
        (cur_r, pc_r, out_r, la_r, lb_r, WIDE, True),
    )
    planes = [PlaneSum(p, *w, ts.at[k], tr.at[k]) for k, w in enumerate(work)]
    sgate = Scatter(p, part_gate, land_gate, es, er, width=FF)

    def relay_q():
        scatters[1].relay()

    def relay_r():
        scatters[2].relay()
        load_gate.wait()
        for c in sgate.far + sgate.near:
            c.start()


    def combine(i):
        group = sends[i * GROUP : (i + 1) * GROUP]
        for c in group:
            c.wait_recv()
        if i == 3:
            own_y.wait()
        weighted = jnp.concatenate(
            [
                slot_rows(posm, t, 1)[0] * share[pl.ds(t, 1), :]
                for t in places[i * GROUP : (i + 1) * GROUP]
            ],
            axis=0,
        )
        high = weighted.astype(BF16)
        low = (weighted - high.astype(F32)).astype(BF16)
        y_now = flatten(y_in[i * GROUP : (i + 1) * GROUP])
        term = mm(high, y_now, 0, 0) + mm(low, y_now, 0, 0)
        if i == 0:
            acc[...] = r[...] + term
        else:
            acc[...] += term

    diagonal = lax.broadcasted_iota(jnp.int32, (CAP, 128), 0) == lax.broadcasted_iota(
        jnp.int32, (CAP, 128), 1
    )
    for k, t in enumerate(places):
        line = jnp.where(diagonal, dots_in[k, 0:1, :], 0.0)
        column = jnp.sum(line, axis=-1, keepdims=True)
        dgate[pl.ds(t, 1), :] = jnp.sum(slot_rows(posm, t, 1)[0] * column, axis=0, keepdims=True)
    dlogits = dgate[...] - share[...] * jnp.sum(dgate[...], axis=0, keepdims=True)
    dlogits = jnp.where(posm[...] >= 0.0, dlogits, 0.0).astype(BF16)
    g_router = mm(dlogits, tokens[...])
    for s in range(4):
        cut = slice(s * SHARD, (s + 1) * SHARD)
        g_tokens[:, cut] += mm(dlogits, small_all[s, 0:32, :], 0, 0)
        sm_part[s] = jnp.concatenate(
            [g_router[:, cut], g_one[:, cut], g_two[:, cut], jnp.zeros((14, SHARD), F32)], axis=0
        ).astype(BF16)
    save_tokens = pltpu.make_async_copy(g_tokens, tokens_out, ls.at[10])
    save_tokens.start()

    small_x = [
        remote(sm_part.at[x], sm_x.at[k], ms.at[k], mr.at[k], (x, p.e))
        for k, x in enumerate([p.xr, p.xl, p.x2])
    ]
    small_z = [
        remote(sm_z.at[p.z], sm_z.at[p.z], ms.at[2 + d], mr.at[2 + d], (p.x, p.peer((d, 0, 0))))
        for d in (1, 2, 3)
    ]
    small_y = [
        remote(sm_y.at[p.y], sm_y.at[p.y], ms.at[5 + d], mr.at[5 + d], (p.x, p.peer((0, d, 0))))
        for d in (1, 2, 3)
    ]
    small_c = [remote(sm_c.at[p.core], sm_c.at[p.core], ms.at[9], mr.at[9], p.sibling)]

    def total(ref, count):
        value = ref[0].astype(F32)
        for k in range(1, count):
            value += ref[k].astype(F32)
        return value

    for c in small_x:
        c.start()
    planes[0].start_a(scatters[0])
    send_y(18, 21)
    relay_q()
    combine(0)
    planes[0].start_b()
    send_y(21, 25)
    relay_r()
    combine(1)
    planes[0].start_back_b()
    send_y(25, 28)
    for c in small_x:
        c.wait_recv()
    sm_z[p.z] = (sm_part[p.x].astype(F32) + total(sm_x, 3)).astype(BF16)
    for c in small_z:
        c.start()
    planes[0].start_back_a()
    send_y(28, 29)
    planes[1].start_a(scatters[1])
    combine(2)
    planes[2].start_a(scatters[2])
    send_y(29, 31)
    for c in small_z:
        c.wait_recv()
    sm_y[p.y] = total(sm_z, 4).astype(BF16)
    for c in small_y:
        c.start()
    planes[1].start_b()
    planes[2].start_b()
    sgate.relay()
    for c in small_y:
        c.wait_recv()
    sm_c[p.core] = total(sm_y, 4).astype(BF16)
    for c in small_c:
        c.start()
    planes[1].start_back_b()
    planes[2].start_back_b()
    combine(3)
    mixed[...] = acc[...].astype(BF16)
    save_mixed = pltpu.make_async_copy(mixed, mixed_out, ls.at[11])
    save_mixed.start()
    planes[1].start_back_a()
    planes[2].start_back_a()
    planes[0].start_pass()
    for c in small_c:
        c.wait_recv()
    out_small[...] = total(sm_c, 2)
    sgate.arrived()
    for half in range(2):
        g_gate[half * HALF : (half + 1) * HALF, :] = sgate.result(half).astype(BF16)
    planes[1].start_pass()
    planes[2].start_pass()
    save_tokens.wait()
    save_mixed.wait()

    for c in sends + small_x + small_z + small_y + small_c:
        c.wait_send()
    for g in pairs + scatters + planes + [sgate]:
        g.finish()


def back(
    tokens, cotangent, posm, share, dots, small_all, n1, q, kv, o, r, dr_rows, y_rows, wq, wkv, wo, gate
):
    D = MODEL_WIDTH
    cosine, sine = rope_tables()

    def arr(shape, dtype=BF16):
        return jax.ShapeDtypeStruct(shape, dtype)

    vm = pl.BlockSpec(memory_space=VMEM)
    hb = pl.BlockSpec(memory_space=ANY)
    sem = pltpu.SemaphoreType.DMA
    widths = (D, WIDE, WIDE)
    return pl.pallas_call(
        back_kernel,
        out_shape=[
            arr((SEQ, D)), arr((SEQ, D), F32), arr((SHARD, D)), arr((SHARD, WIDE)), arr((SHARD, WIDE)),
            arr((48, SHARD), F32), arr((SHARD, FF)),
        ],
        in_specs=[vm] * 6 + [hb] * 13,
        out_specs=[hb] * 2 + [vm] * 5,
        scratch_shapes=[
            VMEM((SEQ, D), BF16),
            VMEM((SEQ, D), F32),
            VMEM((SEQ, D), BF16),
            VMEM((SEQ, D), BF16),
            VMEM((SEQ, D), BF16),
            VMEM((SEQ, D), BF16),
            VMEM((SEQ, 2 * KV), BF16),
            VMEM((SEQ, D), BF16),
            VMEM((SEQ, D), F32),
            VMEM((2, GROUP, CAP, D), BF16),
            VMEM((EXPERTS, CAP, D), BF16),
            VMEM((D, D), BF16),
            VMEM((D, 2 * KV), BF16),
            VMEM((D, D), BF16),
            VMEM((SEQ, D), F32),
            VMEM((SEQ, D), BF16),
            VMEM((SEQ, D), BF16),
            VMEM((SEQ, WIDE), BF16),
            VMEM((SEQ, WIDE), BF16),
            VMEM((EXPERTS, SEQ), F32),
            VMEM((6, HALF, FF), BF16),
            *[VMEM((D, w), BF16) for w in widths],
            *[VMEM((4, HALF, w), BF16) for w in widths],
            *[VMEM((6, HALF // 2, w), BF16) for w in widths],
            *[VMEM((HALF, w), BF16) for w in widths],
            *[VMEM((HALF, w // 4), BF16) for w in widths],
            *[VMEM((3, HALF, w // 4), BF16) for w in widths],
            *[VMEM((3, HALF // 4, w // 4), BF16) for w in widths],
            VMEM((4, 48, SHARD), BF16),
            VMEM((3, 48, SHARD), BF16),
            VMEM((4, 48, SHARD), BF16),
            VMEM((4, 48, SHARD), BF16),
            VMEM((2, 48, SHARD), BF16),
            sem((31,)),
            sem((31,)),
            sem((3, 4)),
            sem((3, 4)),
            sem((3, 6)),
            sem((3, 6)),
            sem((6,)),
            sem((6,)),
            sem((3, 13)),
            sem((3, 13)),
            sem((10,)),
            sem((10,)),
            sem((22,)),
        ],
        compiler_params=pltpu.CompilerParams(
            collective_id=1, has_side_effects=True, vmem_limit_bytes=LIMIT
        ),
        name="back",
    )(
        posm, share, dots, small_all, jnp.asarray(cosine), jnp.asarray(sine),
        tokens, cotangent, n1, q, kv, o, r, dr_rows, y_rows, wq, wkv, wo, gate,
    )


def finish_kernel(mixed, tokens, q, o, r, gate, up, down, small, mixed_, tokens_, q_, k_, v_, o_, gate_, up_, down_, router_, one_, two_):
    mixed_[...] = mixed[...]
    tokens_[...] = tokens[...]
    q_[:, :WIDE] = q[...].astype(F32)
    q_[:, WIDE:] = r[:, 2 * KV :].astype(F32)
    o_[...] = o[...].astype(F32)
    k_[...] = r[:, :KV].astype(F32)
    v_[...] = r[:, KV : 2 * KV].astype(F32)
    gate_[0] = gate[...].astype(F32)
    up_[0] = up[...].astype(F32)
    down_[0] = down[...].astype(F32)
    router_[...] = small[0:32, :]
    one_[...] = small[32, :]
    two_[...] = small[33, :]


def finish(mixed, tokens, q, o, r, gate, up, down, small):
    steps = 4

    def tall(count, width):
        return pl.BlockSpec((count // steps, width), lambda i: (i, 0))

    def owned():
        return pl.BlockSpec((1, SHARD // steps, FF), lambda i: (0, i, 0))

    def arr(*shape, dtype=F32):
        return jax.ShapeDtypeStruct(shape, dtype)

    D = MODEL_WIDTH
    return pl.pallas_call(
        finish_kernel,
        grid=(steps,),
        in_specs=[
            tall(SEQ, D), tall(SEQ, D), tall(SHARD, WIDE), tall(SHARD, D), tall(SHARD, WIDE),
            tall(SHARD, FF), tall(SHARD, FF), tall(SHARD, FF), pl.BlockSpec((48, SHARD), lambda i: (0, 0)),
        ],
        out_specs=[
            tall(SEQ, D), tall(SEQ, D), tall(SHARD, D), tall(SHARD, KV), tall(SHARD, KV), tall(SHARD, D),
            owned(), owned(), owned(), pl.BlockSpec((EXPERTS, SHARD), lambda i: (0, 0)),
            pl.BlockSpec((SHARD,), lambda i: (0,)), pl.BlockSpec((SHARD,), lambda i: (0,)),
        ],
        out_shape=[
            arr(SEQ, D, dtype=BF16), arr(SEQ, D), arr(SHARD, D), arr(SHARD, KV), arr(SHARD, KV), arr(SHARD, D),
            arr(1, SHARD, FF), arr(1, SHARD, FF), arr(1, SHARD, FF), arr(EXPERTS, SHARD),
            arr(SHARD), arr(SHARD),
        ],
        compiler_params=pltpu.CompilerParams(vmem_limit_bytes=LIMIT),
        name="finish",
    )(mixed, tokens, q, o, r, gate, up, down, small)


def shards(
    tokens, routes, w_query, key_matrix, value_matrix, w_output, norm_one, norm_two,
    w_router, w_gate, w_up, w_down, cotangent,
):
    (_, dr_rows, y_rows, fq, fkv, fo, gate, n1, q, kv, o, r, small_all, posm, share, dots, g_up, g_down) = forth(
        tokens, cotangent, routes.T, w_router.T, norm_one, norm_two, w_query, key_matrix, value_matrix, w_output,
        w_gate[0], w_up[0], w_down[0],
    )
    mixed, g_tokens, g_o, g_q, g_r, g_small, g_gate = back(
        tokens, cotangent, posm, share, dots, small_all, n1, q, kv, o, r, dr_rows, y_rows, fq, fkv, fo, gate
    )
    mixed, g_tokens, g_q, g_k, g_v, g_o, g_gate, g_up, g_down, g_router, g_one, g_two = finish(
        mixed, g_tokens, g_q, g_o, g_r, g_gate, g_up, g_down, g_small
    )
    return (
        mixed, g_tokens, g_q, g_k, g_v, g_o, g_one, g_two, g_router.T, g_gate, g_up, g_down
    )


def solution(mesh):
    rows_split = P(("dp", "expert"), None)
    flat = P("dp", None)
    vector = P("dp")
    owned = P("expert", "dp", None)
    return jax.shard_map(
        shards,
        mesh=mesh,
        in_specs=(
            rows_split, rows_split, flat, flat, flat, flat, vector, vector, flat, owned, owned, owned,
            rows_split,
        ),
        out_specs=(
            rows_split, rows_split, flat, flat, flat, flat, vector, vector, flat, owned, owned, owned,
        ),
        check_vma=False,
    )
```
